256 devices in a mesh: grp: 8 (over x, y_lo), dp: 32 (over y_hi, z, core).
Axes of the slice: x: 4, y: 4 (y_hi: 2, y_lo: 2; y = y_hi * 2 + y_lo), z: 8, core: 2. Of those that a mesh axis runs over, the one named last changes fastest.
Arguments:
- latents: bfloat16 [256, 16, 128, 320], P(('grp', 'dp')), may hold values from -6 to 6
- cotangent: bfloat16 [256, 16, 128, 320], P(('grp', 'dp')), may hold values from -6 to 6
- weight: bfloat16 [3, 3, 320, 320], replicated, may hold values from -0.109375 to 0.109375
- gain: float32 [320], replicated, may hold values from 0.25 to 1.75
- shift: float32 [320], replicated, may hold values from -3 to 3
- master: float32 [950272], P(('grp', 'dp')), may hold values from -0.109375 to 0.109375
- first_moment: float32 [950272], P(('grp', 'dp')), may hold values from -0.0014648438 to 0.0014648438
- second_moment: float32 [950272], P(('grp', 'dp')), may hold values from 1e-08 to 1e-06
Outputs:
- grad_input: bfloat16 [256, 16, 128, 320], P(('grp', 'dp'))
- new_weight: bfloat16 [3, 3, 320, 320], replicated
- new_bias: bfloat16 [320], replicated
- new_gain: bfloat16 [320], replicated
- new_shift: bfloat16 [320], replicated
- new_master: float32 [950272], P(('grp', 'dp'))
- new_first: float32 [950272], P(('grp', 'dp'))
- new_second: float32 [950272], P(('grp', 'dp'))
The draws below stay inside these ranges and needn't reach their ends.
All inputs are finite; a program needn't handle non-finite values.
Results may differ from the reference program's by a relative error of at most 0.0033.
Values may be sent and summed in bfloat16 or wider, within the bound.
A program may use at most 64 MiB of HBM per device.

```python
import math
import jax
import jax.numpy as jnp
from jax import lax

C = 320
GROUPS = 32
H_ROWS = 16
WIDTH = 128
PARAMS = 922560
FLAT = 950272
BATCH = 256


def shard_levels(own_key, extent, cuts, least, high):
    level = 1.0
    for position, blocks in cuts:
        steps = jax.random.uniform(jax.random.fold_in(jax.random.fold_in(own_key, 6), position), (blocks,), jnp.float32, least / len(cuts), high / len(cuts))
        level = level * jnp.repeat(jnp.exp(steps), extent[position] // blocks).reshape((-1,) + (1,) * (len(extent) - 1 - position))
    return level


def scatter_about(key, shape, scale, reach, shards=(), dtype=jnp.bfloat16):
    factor_of = shard_levels(key, shape, shards, -0.22, 0.18) if shards else 1.0
    drawn = jax.random.normal(key, shape, jnp.float32) * scale * factor_of
    return jnp.minimum(jnp.maximum(drawn, -reach), reach).astype(dtype)


def setup_inputs(seed: int = 0) -> dict:
    key_of = jax.random.split(jax.random.key(seed), 9)
    latents = scatter_about(key_of[0], (BATCH, H_ROWS, WIDTH, C), 1.0, 6.0, ((0, 256),))
    cotangent = scatter_about(key_of[1], (BATCH, H_ROWS, WIDTH, C), 1.0, 6.0, ((0, 256),))
    weight = scatter_about(key_of[2], (3, 3, C, C), (9 * C) ** -0.5, 0.109375)
    gain = jnp.clip(1.0 + 0.15 * jax.random.normal(key_of[3], (C,), jnp.float32), 0.25, 1.75)
    shift = scatter_about(key_of[4], (C,), 0.5, 3.0, (), jnp.float32)
    master = scatter_about(key_of[5], (FLAT,), (9 * C) ** -0.5, 0.109375, ((0, 256),), jnp.float32)
    first_moment = scatter_about(key_of[6], (FLAT,), 0.0001, 0.0014648438, ((0, 256),), jnp.float32)
    second_moment = jnp.clip(jnp.exp(math.log(9.999999974752427e-07) - 4.6051702 * jax.random.uniform(key_of[7], (FLAT,), jnp.float32) ** shard_levels(key_of[7], (FLAT,), ((0, 256),), -0.2, 0.2)), 9.99999993922529e-09, 9.999999974752427e-07)
    return dict(latents=latents, cotangent=cotangent, weight=weight, gain=gain, shift=shift, master=master, first_moment=first_moment, second_moment=second_moment)


norm_epsilon = 1e-05
beta_first = 0.9
beta_second = 0.999
adam_epsilon = 1e-08
learn_rate = 0.001
weight_decay = 0.01
clip_limit = 1.0
correct_first = 1.0
correct_second = 0.6323045752290363

def norm_act(entries, gain, shift):
    height, breadth, channels = entries.shape
    grouped = entries.reshape(height * breadth, GROUPS, channels // GROUPS)
    centre = lax.optimization_barrier(jnp.mean(grouped, axis=(0, 2), keepdims=True))
    centred = grouped - centre
    spread = lax.optimization_barrier(jnp.mean(centred * centred, axis=(0, 2), keepdims=True))
    normed = (centred * lax.rsqrt(spread + norm_epsilon)).reshape(height, breadth, channels)
    return jax.nn.silu(normed * gain + shift)

def local_grads(sample, cot_sample, weight, gain, shift):
    height, breadth, channels = sample.shape
    activation, pullback = jax.vjp(norm_act, sample.astype(jnp.float32), gain, shift)
    stored = activation.astype(jnp.bfloat16)
    padded = jnp.pad(stored, ((1, 1), (1, 1), (0, 0)))
    cot_rows = cot_sample.reshape(height * breadth, channels)
    padded_grad = jnp.zeros((height + 2, breadth + 2, channels), jnp.float32)
    kernels = []
    for tap_row in range(3):
        for tap_col in range(3):
            window = padded[tap_row:tap_row + height, tap_col:tap_col + breadth].reshape(height * breadth, channels)
            kernels.append(lax.dot_general(window, cot_rows, (((0,), (0,)), ((), ())), preferred_element_type=jnp.float32))
            back = lax.dot_general(cot_rows, weight[tap_row, tap_col], (((1,), (1,)), ((), ())), preferred_element_type=jnp.float32)
            padded_grad = padded_grad.at[tap_row:tap_row + height, tap_col:tap_col + breadth].add(back.reshape(height, breadth, channels))
    grad_act = padded_grad[1:-1, 1:-1]
    grad_in, grad_gain, grad_shift = pullback(grad_act)
    grad_bias = lax.optimization_barrier(jnp.sum(cot_rows.astype(jnp.float32), axis=0))
    kernel_grad = jnp.stack(kernels).reshape(-1)
    flat_grad = jnp.concatenate([kernel_grad, grad_bias, grad_gain, grad_shift])
    return (grad_in.astype(jnp.bfloat16), flat_grad)

def adam_update(summed, norm_total, master, first_moment, second_moment):
    clip = jnp.minimum(1.0, clip_limit / (jnp.sqrt(norm_total) + 1e-06))
    clipped = clip * summed
    new_first = beta_first * first_moment + (1.0 - beta_first) * clipped
    new_second = beta_second * second_moment + (1.0 - beta_second) * clipped * clipped
    step_dir = new_first / correct_first / (jnp.sqrt(new_second / correct_second) + adam_epsilon)
    new_master = master - learn_rate * (step_dir + weight_decay * master)
    return (new_master, new_first, new_second)

def reference(latents, cotangent, weight, gain, shift, master, first_moment, second_moment):

    def per_sample(running, sample_pair):
        grad_in, flat_grad = local_grads(sample_pair[0], sample_pair[1], weight, gain, shift)
        return (running + flat_grad, grad_in)
    start_sum = jnp.zeros((PARAMS,), jnp.float32)
    summed, grad_input = lax.scan(per_sample, start_sum, (latents, cotangent))
    summed = jnp.concatenate([summed, jnp.zeros((FLAT - PARAMS,), jnp.float32)])
    norm_total = jnp.sum(summed * summed)
    new_master, new_first, new_second = adam_update(summed, norm_total, master, first_moment, second_moment)
    rounded = new_master.astype(jnp.bfloat16)
    kernel_size = 9 * C * C
    new_weight = rounded[:kernel_size].reshape(3, 3, C, C)
    new_bias = rounded[kernel_size:kernel_size + C]
    new_gain = rounded[kernel_size + C:kernel_size + 2 * C]
    new_shift = rounded[kernel_size + 2 * C:kernel_size + 3 * C]
    return (grad_input, new_weight, new_bias, new_gain, new_shift, new_master, new_first, new_second)
```

```python
import functools

import jax
import jax.numpy as jnp
from jax import lax
from jax.experimental import pallas as pl
from jax.experimental.pallas import tpu as pltpu
from jax.sharding import PartitionSpec as P

GROUPS = 32
LANES = 128
PAD_ROWS = 32

norm_epsilon = 1e-05
beta_first = 0.9
beta_second = 0.999
adam_epsilon = 1e-08
learn_rate = 0.001
weight_decay = 0.01
clip_limit = 1.0
correct_first = 1.0
correct_second = 0.6323045752290363

MESH = pl.DeviceIdType.MESH
VMEM_LIMIT = 60 * 1024 * 1024


def swap_halves(block):
    return pltpu.roll(block, LANES // 2, axis=1)


def lower_half(shape):
    return lax.broadcasted_iota(jnp.int32, shape, 1) < LANES // 2


def grads_kernel(
    shard_rows,
    x_ref,
    cot_ref,
    w_ref,
    gain_ref,
    shift_ref,
    gin_ref,
    own_ref,
    other_ref,
    act3,
    cot3,
    wcat,
    kgrad,
    flat,
    normed_s,
    dact_s,
    gact,
):
    height, channels, width = x_ref.shape
    count = height * width * (channels // GROUPS)
    core = lax.axis_index("dp") % 2
    f32, bf16 = jnp.float32, jnp.bfloat16

    row_id = lax.broadcasted_iota(jnp.int32, (channels, channels), 0)
    col_id = lax.broadcasted_iota(jnp.int32, (channels, channels), 1)
    eye = (row_id == col_id).astype(f32)
    per = 1.0 / (channels // GROUPS)
    row_group = jnp.floor((row_id.astype(f32) + 0.5) * per)
    col_group = jnp.floor((col_id.astype(f32) + 0.5) * per)
    same_group = (row_group == col_group).astype(f32)

    def group_mean(block):
        mixed = jnp.dot(
            same_group, block, precision=lax.Precision.HIGHEST, preferred_element_type=f32
        )
        return jnp.sum(mixed, axis=1, keepdims=True) * (1.0 / count)

    def as_column(row):
        return jnp.sum(eye * row, axis=1, keepdims=True)

    def as_row(column):
        return jnp.sum(eye * column, axis=0, keepdims=True)

    gain = as_column(gain_ref[...])
    shift = as_column(shift_ref[...])

    zero_block = jnp.zeros((channels, width), f32)
    total = lax.fori_loop(
        0, height, lambda r, s: s + x_ref[r].astype(f32), zero_block
    )
    centre = group_mean(total)

    def spread_step(r, s):
        centred = x_ref[r].astype(f32) - centre
        return s + centred * centred

    spread = group_mean(lax.fori_loop(0, height, spread_step, zero_block))
    rstd = lax.rsqrt(spread + norm_epsilon)

    lane = lax.broadcasted_iota(jnp.int32, (channels, width), 1)
    zero_bf = jnp.zeros((channels, width), bf16)
    act3[0:channels, 0:width] = zero_bf
    act3[2 * channels : 3 * channels, (height - 1) * width : height * width] = zero_bf
    cot3[3 * channels :, :] = jnp.zeros((cot3.shape[0] - 3 * channels, cot3.shape[1]), bf16)

    bias_total = zero_block
    for r in range(height):
        normed = (x_ref[r].astype(f32) - centre) * rstd
        pre = normed * gain + shift
        sig = 1.0 / (1.0 + jnp.exp(-pre))
        act = (pre * sig).astype(bf16)
        normed_s[r] = normed
        dact_s[r] = sig * (1.0 + pre * (1.0 - sig))
        for i in range(3):
            dest = r - i + 1
            if 0 <= dest < height:
                act3[i * channels : (i + 1) * channels, dest * width : (dest + 1) * width] = act
        cot = cot_ref[r].astype(f32)
        bias_total = bias_total + cot
        place = slice(r * width, (r + 1) * width)
        ahead = jnp.where(lane < width - 1, pltpu.roll(cot, width - 1, axis=1), 0.0)
        behind = jnp.where(lane > 0, pltpu.roll(cot, 1, axis=1), 0.0)
        cot3[0:channels, place] = ahead.astype(bf16)
        cot3[channels : 2 * channels, place] = cot_ref[r]
        cot3[2 * channels : 3 * channels, place] = behind.astype(bf16)

    def kernel_step(n, carry):
        start = pl.multiple_of(n * 256, 256)
        block = lax.dot_general(
            act3[...],
            cot3[pl.ds(start, 256), :],
            (((1,), (1,)), ((), ())),
            preferred_element_type=f32,
        )
        kgrad[2 * n] = block[:, :LANES]
        kgrad[2 * n + 1] = block[:, LANES:]
        return carry

    lax.fori_loop(0, cot3.shape[0] // 256, kernel_step, 0)

    wcat[...] = jnp.zeros_like(wcat)
    for i in range(3):
        for j in range(3):
            wcat[i * channels : (i + 1) * channels, j * channels : (j + 1) * channels] = w_ref[
                3 * i + j
            ]
    gact[...] = jnp.zeros_like(gact)

    def back_step(n, carry):
        start = pl.multiple_of(n * 256, 256)
        block = jnp.dot(wcat[...], cot3[:, pl.ds(start, 256)], preferred_element_type=f32)
        for i in range(3):
            for h in range(2):
                gact[2 * n + h + i] += block[
                    i * channels : (i + 1) * channels, h * width : (h + 1) * width
                ]
        return carry

    lax.fori_loop(0, height // 2, back_step, 0)

    def sums_step(r, carry):
        shift_sum, gain_sum = carry
        dpre = gact[r + 1] * dact_s[r]
        gact[r + 1] = dpre
        return shift_sum + dpre, gain_sum + dpre * normed_s[r]

    shift_sum, gain_sum = lax.fori_loop(0, height, sums_step, (zero_block, zero_block))
    mean_grad = group_mean(shift_sum * gain)
    mean_cross = group_mean(gain_sum * gain)

    def input_step(r, carry):
        slope = gact[r + 1] * gain
        gin_ref[r] = (rstd * (slope - mean_grad - normed_s[r] * mean_cross)).astype(bf16)
        return carry

    lax.fori_loop(0, height, input_step, 0)

    half = channels // 2
    low = lower_half((half, LANES))
    flat_rows = flat.shape[0]
    for i in range(3):
        for j in range(3):
            first = (j * channels) // LANES
            even = [kgrad[first + b, pl.ds(i * channels, half, stride=2), :] for b in range(3)]
            odd = [kgrad[first + b, pl.ds(i * channels + 1, half, stride=2), :] for b in range(3)]
            if j == 1:
                even_r = [swap_halves(e) for e in even]
                pieces = [
                    jnp.where(low, even_r[0], even_r[1]),
                    jnp.where(low, even_r[1], even_r[2]),
                    jnp.where(low, even_r[2], odd[0]),
                    odd[1],
                    odd[2],
                ]
            else:
                odd_r = [swap_halves(o) for o in odd]
                pieces = [
                    even[0],
                    even[1],
                    jnp.where(low, even[2], odd_r[0]),
                    jnp.where(low, odd_r[0], odd_r[1]),
                    jnp.where(low, odd_r[1], odd_r[2]),
                ]
            base = (3 * i + j) * (channels * channels // LANES)
            for b in range(5):
                flat[pl.ds(base + b, half, stride=5), :] = pieces[b]

    used = 9 * channels * channels // LANES
    bias_row = as_row(jnp.sum(bias_total, axis=1, keepdims=True))
    gain_row = as_row(jnp.sum(gain_sum, axis=1, keepdims=True))
    shift_row = as_row(jnp.sum(shift_sum, axis=1, keepdims=True))
    flat[used:flat_rows, :] = jnp.zeros((flat_rows - used, LANES), f32)
    flat[used : used + 1, :] = bias_row[:, 0:128]
    flat[used + 1 : used + 2, :] = bias_row[:, 128:256]
    flat[used + 2 : used + 3, 0:64] = bias_row[:, 256:320]
    flat[used + 2 : used + 3, 64:128] = gain_row[:, 0:64]
    flat[used + 3 : used + 4, :] = gain_row[:, 64:192]
    flat[used + 4 : used + 5, :] = gain_row[:, 192:320]
    flat[used + 5 : used + 6, :] = shift_row[:, 0:128]
    flat[used + 6 : used + 7, :] = shift_row[:, 128:256]
    flat[used + 7 : used + 8, 0:64] = shift_row[:, 256:320]

    def shard_step(q, carry):
        own_ref[q] = flat[pl.ds((2 * q + core) * shard_rows, PAD_ROWS), :]
        other_ref[q] = flat[pl.ds((2 * q + 1 - core) * shard_rows, PAD_ROWS), :].astype(bf16)
        return carry

    lax.fori_loop(0, own_ref.shape[0], shard_step, 0)


def sample_grads(x, cot, weight, gain, shift, shards, shard_rows):
    height, channels, width = x.shape
    f32, bf16 = jnp.float32, jnp.bfloat16
    wide = -(-3 * channels // 256) * 256
    flat_rows = shards * shard_rows + PAD_ROWS
    return pl.pallas_call(
        functools.partial(grads_kernel, shard_rows),
        out_shape=(
            jax.ShapeDtypeStruct(x.shape, bf16),
            jax.ShapeDtypeStruct((shards // 2, PAD_ROWS, LANES), f32),
            jax.ShapeDtypeStruct((shards // 2, PAD_ROWS, LANES), bf16),
        ),
        scratch_shapes=[
            pltpu.VMEM((3 * channels, height * width), bf16),
            pltpu.VMEM((wide, height * width), bf16),
            pltpu.VMEM((3 * channels, wide), bf16),
            pltpu.VMEM((wide // LANES, 3 * channels, LANES), f32),
            pltpu.VMEM((flat_rows, LANES), f32),
            pltpu.VMEM((height, channels, width), f32),
            pltpu.VMEM((height, channels, width), f32),
            pltpu.VMEM((height + 2, channels, width), f32),
        ],
        compiler_params=pltpu.CompilerParams(vmem_limit_bytes=VMEM_LIMIT),
    )(x, cot, weight.reshape(9, channels, channels), gain[None], shift[None])


def update_kernel(
    split_rows,
    own_ref,
    other_ref,
    master_ref,
    first_ref,
    second_ref,
    gath,
    new_master_ref,
    new_first_ref,
    new_second_ref,
    recv1,
    send2,
    recv2,
    acc,
    recv3,
    norm_line,
    norm_plane,
    s1,
    r1,
    s2,
    r2,
    s3,
    r3,
    sl,
    rl,
    sp,
    rp,
    sa,
    ra,
    sb,
    rb,
    sc,
    rc,
):
    f32, bf16 = jnp.float32, jnp.bfloat16
    plane, depth = own_ref.shape[0], own_ref.shape[1]
    line = 2 * depth
    grp, dp = lax.axis_index("grp"), lax.axis_index("dp")
    p = grp * split_rows + dp // line
    spot = dp % line
    z, core = spot // 2, spot % 2
    shard_rows = master_ref.shape[0]

    def device(p_, spot_):
        return (p_ // split_rows, (p_ % split_rows) * line + spot_)

    def in_plane(t):
        return device((p + t) % plane, spot)

    def in_line(t):
        return device(p, (spot + t) % line)

    def in_depth(t):
        return device(p, ((z + t) % depth) * 2 + core)

    partner = device(p, z * 2 + 1 - core)

    def copy(src, dst, send, recv, target):
        return pltpu.make_async_remote_copy(
            src_ref=src,
            dst_ref=dst,
            send_sem=send,
            recv_sem=recv,
            device_id=target,
            device_id_type=MESH,
        )

    def loop(lo, hi, body):
        def step(t, carry):
            body(t)
            return carry

        lax.fori_loop(lo, hi, step, 0)

    barrier = pltpu.get_barrier_semaphore()
    loop(1, plane, lambda t: pl.semaphore_signal(barrier, inc=1, device_id=in_plane(t), device_id_type=MESH))
    loop(1, line, lambda t: pl.semaphore_signal(barrier, inc=1, device_id=in_line(t), device_id_type=MESH))
    pl.semaphore_wait(barrier, plane + line - 2)

    def pair(t):
        q = (p + t) % plane
        return copy(other_ref.at[q], recv1.at[q], s1.at[t], r1.at[t], partner)

    loop(1, plane, lambda t: pair(t).start())
    pair(0).start()

    def across(t):
        return copy(send2.at[t], recv2.at[t], s2.at[t], r2.at[t], in_plane(t))

    def across_start(t):
        pair(t).wait_recv()
        q = (p + t) % plane
        send2[t] = (own_ref[q] + recv1[q].astype(f32)).astype(bf16)
        across(t).start()

    loop(1, plane, across_start)
    pair(0).wait_recv()
    acc[...] = own_ref[p] + recv1[p].astype(f32)

    def across_take(t):
        across(t).wait_recv()
        acc[...] += recv2[t].astype(f32)

    loop(1, plane, across_take)

    def along(t):
        return copy(acc.at[(z + t) % depth], recv3.at[t], s3.at[t], r3.at[t], in_depth(t))

    loop(1, depth, lambda t: along(t).start())
    recv3[0] = acc[z]
    loop(1, depth, lambda t: along(t).wait_recv())
    summed = recv3[0]
    for t in range(1, depth):
        summed = summed + recv3[t]
    live = lax.broadcasted_iota(jnp.int32, summed.shape, 0) < shard_rows
    summed = jnp.where(live, summed, 0.0)

    squares = summed * summed
    norm_line[0] = squares[0:8] + squares[8:16] + squares[16:24] + squares[24:32]

    def line_copy(t):
        return copy(norm_line.at[0], norm_line.at[t], sl.at[t], rl.at[t], in_line(t))

    loop(1, line, lambda t: line_copy(t).start())
    loop(1, line, lambda t: line_copy(t).wait_recv())
    part = norm_line[0]
    for t in range(1, line):
        part = part + norm_line[t]
    norm_plane[0] = part

    def plane_copy(t):
        return copy(norm_plane.at[0], norm_plane.at[t], sp.at[t], rp.at[t], in_plane(t))

    loop(1, plane, lambda t: plane_copy(t).start())
    loop(1, plane, lambda t: plane_copy(t).wait_recv())
    part = norm_plane[0]
    for t in range(1, plane):
        part = part + norm_plane[t]
    norm_total = jnp.sum(jnp.sum(part, axis=1, keepdims=True), axis=0, keepdims=True)

    clip = jnp.minimum(1.0, clip_limit / (jnp.sqrt(norm_total) + 1e-06))
    clipped = (clip * summed)[0:shard_rows]
    new_first = beta_first * first_ref[...] + (1.0 - beta_first) * clipped
    new_second = beta_second * second_ref[...] + (1.0 - beta_second) * clipped * clipped
    step_dir = new_first / correct_first / (jnp.sqrt(new_second / correct_second) + adam_epsilon)
    master = master_ref[...]
    new_master = master - learn_rate * (step_dir + weight_decay * master)
    new_master_ref[...] = new_master
    new_first_ref[...] = new_first
    new_second_ref[...] = new_second
    recv3[0, 0:shard_rows] = new_master
    gath[core, p, z] = recv3[0].astype(bf16)

    def gather_depth(t):
        mine = gath.at[core, p, z]
        return copy(mine, mine, sa.at[t], ra.at[t], in_depth(t))

    def gather_plane(t):
        mine = gath.at[core, p]
        return copy(mine, mine, sb.at[t], rb.at[t], in_plane(t))

    def gather_core(t):
        block = gath.at[core, (p + plane - t) % plane]
        return copy(block, block, sc.at[t], rc.at[t], partner)

    loop(1, depth, lambda t: gather_depth(t).start())
    loop(1, depth, lambda t: gather_depth(t).wait_recv())
    loop(1, plane, lambda t: gather_plane(t).start())
    gather_core(0).start()

    def pass_on(t):
        gather_plane(t).wait_recv()
        gather_core(t).start()

    loop(1, plane, pass_on)
    loop(0, plane, lambda t: gather_core(t).wait_recv())

    loop(0, plane, lambda t: pair(t).wait_send())
    loop(1, plane, lambda t: across(t).wait_send())
    loop(1, depth, lambda t: along(t).wait_send())
    loop(1, line, lambda t: line_copy(t).wait_send())
    loop(1, plane, lambda t: plane_copy(t).wait_send())
    loop(1, depth, lambda t: gather_depth(t).wait_send())
    loop(1, plane, lambda t: gather_plane(t).wait_send())
    loop(0, plane, lambda t: gather_core(t).wait_send())


def reduce_and_update(own, other, master, first, second, plane, depth, split_rows):
    f32, bf16 = jnp.float32, jnp.bfloat16
    line = 2 * depth
    own = own.reshape(plane, depth, PAD_ROWS, LANES)
    other = other.reshape(plane, depth, PAD_ROWS, LANES)
    shard = jax.ShapeDtypeStruct(master.shape, f32)
    dma = lambda n: pltpu.SemaphoreType.DMA((n,))
    return pl.pallas_call(
        functools.partial(update_kernel, split_rows),
        out_shape=(
            jax.ShapeDtypeStruct((2, plane, depth, PAD_ROWS, LANES), bf16),
            shard,
            shard,
            shard,
        ),
        in_specs=[pl.BlockSpec(memory_space=pltpu.VMEM)] * 5,
        out_specs=[pl.BlockSpec(memory_space=pltpu.VMEM)] * 4,
        scratch_shapes=[
            pltpu.VMEM((plane, depth, PAD_ROWS, LANES), bf16),
            pltpu.VMEM((plane, depth, PAD_ROWS, LANES), bf16),
            pltpu.VMEM((plane, depth, PAD_ROWS, LANES), bf16),
            pltpu.VMEM((depth, PAD_ROWS, LANES), f32),
            pltpu.VMEM((depth, PAD_ROWS, LANES), f32),
            pltpu.VMEM((line, 8, LANES), f32),
            pltpu.VMEM((plane, 8, LANES), f32),
        ]
        + [dma(n) for n in (plane, plane, plane, plane, depth, depth, line, line)]
        + [dma(n) for n in (plane, plane, depth, depth, plane, plane, plane, plane)],
        compiler_params=pltpu.CompilerParams(
            collective_id=0, has_side_effects=True, vmem_limit_bytes=VMEM_LIMIT
        ),
    )(own, other, master, first, second)


def unpack_kernel(shard_rows, gath, weight_ref, bias_ref, gain_ref, shift_ref, flat, rows):
    f32, bf16 = jnp.float32, jnp.bfloat16
    plane, depth = gath.shape[1], gath.shape[2]
    total, channels = weight_ref.shape

    def shard_step(q, carry):
        for core in range(2):
            block = gath[core, q // depth, q % depth].astype(f32)
            flat[pl.ds((2 * q + core) * shard_rows, PAD_ROWS), :] = block
        return carry

    lax.fori_loop(0, plane * depth, shard_step, 0)

    half = channels // 2
    low = lower_half((half, LANES))
    five = channels * channels // LANES

    def rows_step(n, carry):
        piece = [flat[pl.ds(n * five + b, half, stride=5), :] for b in range(5)]
        turned = [swap_halves(piece[b]) for b in range(2, 5)]
        even = [piece[0], piece[1], piece[2]]
        odd = [
            jnp.where(low, turned[0], turned[1]),
            jnp.where(low, turned[1], turned[2]),
            turned[2],
        ]
        for b in range(3):
            rows[b, pl.ds(0, half, stride=2), :] = even[b]
            rows[b, pl.ds(1, half, stride=2), :] = odd[b]
        place = pl.ds(pl.multiple_of(n * channels, channels), channels)
        weight_ref[place, 0:128] = rows[0].astype(bf16)
        weight_ref[place, 128:256] = rows[1].astype(bf16)
        weight_ref[place, 256:channels] = rows[2, :, 0 : channels - 256].astype(bf16)
        return carry

    lax.fori_loop(0, total // channels, rows_step, 0)

    used = total * channels // LANES
    tail = [flat[used + b : used + b + 1, :].astype(bf16) for b in range(8)]
    bias_ref[:, 0:128] = tail[0]
    bias_ref[:, 128:256] = tail[1]
    bias_ref[:, 256:320] = tail[2][:, 0:64]
    gain_ref[:, 0:64] = tail[2][:, 64:128]
    gain_ref[:, 64:192] = tail[3]
    gain_ref[:, 192:320] = tail[4]
    shift_ref[:, 0:128] = tail[5]
    shift_ref[:, 128:256] = tail[6]
    shift_ref[:, 256:320] = tail[7][:, 0:64]


def unpack(gath, channels, shard_rows):
    bf16, f32 = jnp.bfloat16, jnp.float32
    shards = 2 * gath.shape[1] * gath.shape[2]
    row = jax.ShapeDtypeStruct((1, channels), bf16)
    return pl.pallas_call(
        functools.partial(unpack_kernel, shard_rows),
        out_shape=(jax.ShapeDtypeStruct((9 * channels, channels), bf16), row, row, row),
        scratch_shapes=[
            pltpu.VMEM((shards * shard_rows + PAD_ROWS, LANES), f32),
            pltpu.VMEM((3, channels, LANES), f32),
        ],
        compiler_params=pltpu.CompilerParams(vmem_limit_bytes=VMEM_LIMIT),
    )(gath)


def on_device(latents, cotangent, weight, gain, shift, master, first_moment, second_moment):
    groups, owners = lax.axis_size("grp"), lax.axis_size("dp")
    channels = weight.shape[2]
    split_rows = 2
    depth = owners // (2 * split_rows)
    plane = groups * split_rows
    shard_rows = master.shape[0] // LANES
    x = jnp.transpose(latents[0], (0, 2, 1))
    cot = jnp.transpose(cotangent[0], (0, 2, 1))
    grad_in, own, other = sample_grads(x, cot, weight, gain, shift, groups * owners, shard_rows)
    shaped = [a.reshape(shard_rows, LANES) for a in (master, first_moment, second_moment)]
    gath, new_master, new_first, new_second = reduce_and_update(
        own, other, *shaped, plane, depth, split_rows
    )
    new_weight, new_bias, new_gain, new_shift = unpack(gath, channels, shard_rows)
    return (
        jnp.transpose(grad_in, (0, 2, 1))[None],
        new_weight.reshape(weight.shape),
        new_bias.reshape(channels),
        new_gain.reshape(channels),
        new_shift.reshape(channels),
        new_master.reshape(-1),
        new_first.reshape(-1),
        new_second.reshape(-1),
    )


def solution(mesh):
    split = ("grp", "dp")
    whole = P(split, None, None, None)
    in_specs = (whole, whole, P(), P(), P(), P(split), P(split), P(split))
    out_specs = (whole, P(), P(), P(), P(), P(split), P(split), P(split))
    return jax.shard_map(
        on_device, mesh=mesh, in_specs=in_specs, out_specs=out_specs, check_vma=False
    )
```

```python
import functools

import jax
import jax.numpy as jnp
from jax import lax
from jax.experimental import pallas as pl
from jax.experimental.pallas import tpu as pltpu
from jax.sharding import PartitionSpec as P

GROUPS = 32
LANES = 128
PAD_ROWS = 32

norm_epsilon = 1e-05
beta_first = 0.9
beta_second = 0.999
adam_epsilon = 1e-08
learn_rate = 0.001
weight_decay = 0.01
clip_limit = 1.0
correct_first = 1.0
correct_second = 0.6323045752290363

MESH = pl.DeviceIdType.MESH
VMEM_LIMIT = 60 * 1024 * 1024


def swap_halves(block):
    return pltpu.roll(block, LANES // 2, axis=1)


def lower_half(shape):
    return lax.broadcasted_iota(jnp.int32, shape, 1) < LANES // 2


def layer_kernel(
    split_rows,
    plane,
    depth,
    x_ref,
    cot_ref,
    w_hbm,
    gain_ref,
    shift_ref,
    master_ref,
    first_ref,
    second_ref,
    gin_hbm,
    gath_hbm,
    new_master_ref,
    new_first_ref,
    new_second_ref,
    w_ref,
    gin_ref,
    gath,
    act3,
    cot3,
    wcat,
    kgrad,
    flat,
    normed_s,
    dact_s,
    gact,
    send1,
    recv1,
    send2,
    recv2,
    acc,
    recv3,
    norm_line,
    norm_plane,
    w_sem,
    gin_sem,
    s1,
    r1,
    s2,
    r2,
    s3,
    r3,
    sl,
    rl,
    sp,
    rp,
    sa,
    ra,
    sb,
    rb,
    sc,
    rc,
    out_sem,
):
    f32, bf16 = jnp.float32, jnp.bfloat16
    line = 2 * depth
    grp, dp = lax.axis_index("grp"), lax.axis_index("dp")
    p = grp * split_rows + dp // line
    spot = dp % line
    z, core = spot // 2, spot % 2
    shard_rows = master_ref.shape[0]

    def device(p_, spot_):
        return (p_ // split_rows, (p_ % split_rows) * line + spot_)

    def in_plane(t):
        return device((p + t) % plane, spot)

    def in_line(t):
        return device(p, (spot + t) % line)

    def in_depth(t):
        return device(p, ((z + t) % depth) * 2 + core)

    partner = device(p, z * 2 + 1 - core)

    def copy(src, dst, send, recv, target):
        return pltpu.make_async_remote_copy(
            src_ref=src,
            dst_ref=dst,
            send_sem=send,
            recv_sem=recv,
            device_id=target,
            device_id_type=MESH,
        )

    def loop(lo, hi, body):
        def step(t, carry):
            body(t)
            return carry

        lax.fori_loop(lo, hi, step, 0)

    barrier = pltpu.get_barrier_semaphore()

    def greet(target):
        pl.semaphore_signal(barrier, inc=1, device_id=target, device_id_type=MESH)

    loop(1, plane, lambda t: greet(in_plane(t)))
    loop(1, line, lambda t: greet(in_line(t)))
    w_copy = pltpu.make_async_copy(w_hbm, w_ref, w_sem)
    w_copy.start()

    height, channels, width = x_ref.shape
    count = height * width * (channels // GROUPS)

    row_id = lax.broadcasted_iota(jnp.int32, (channels, channels), 0)
    col_id = lax.broadcasted_iota(jnp.int32, (channels, channels), 1)
    eye = (row_id == col_id).astype(f32)
    per = 1.0 / (channels // GROUPS)
    row_group = jnp.floor((row_id.astype(f32) + 0.5) * per)
    col_group = jnp.floor((col_id.astype(f32) + 0.5) * per)
    same_group = (row_group == col_group).astype(f32)

    def group_mean(block):
        mixed = jnp.dot(
            same_group, block, precision=lax.Precision.HIGHEST, preferred_element_type=f32
        )
        return jnp.sum(mixed, axis=1, keepdims=True) * (1.0 / count)

    def as_column(row):
        return jnp.sum(eye * row, axis=1, keepdims=True)

    def as_row(column):
        return jnp.sum(eye * column, axis=0, keepdims=True)

    gain = as_column(gain_ref[...].reshape(1, channels))
    shift = as_column(shift_ref[...].reshape(1, channels))

    zero_block = jnp.zeros((channels, width), f32)
    total = lax.fori_loop(
        0, height, lambda r, s: s + x_ref[r].astype(f32), zero_block
    )
    centre = group_mean(total)

    def spread_step(r, s):
        centred = x_ref[r].astype(f32) - centre
        return s + centred * centred

    spread = group_mean(lax.fori_loop(0, height, spread_step, zero_block))
    rstd = lax.rsqrt(spread + norm_epsilon)

    lane = lax.broadcasted_iota(jnp.int32, (channels, width), 1)
    zero_bf = jnp.zeros((channels, width), bf16)
    act3[0:channels, 0:width] = zero_bf
    act3[2 * channels : 3 * channels, (height - 1) * width : height * width] = zero_bf
    cot3[3 * channels :, :] = jnp.zeros((cot3.shape[0] - 3 * channels, cot3.shape[1]), bf16)

    bias_total = zero_block
    for r in range(height):
        normed = (x_ref[r].astype(f32) - centre) * rstd
        pre = normed * gain + shift
        sig = 1.0 / (1.0 + jnp.exp(-pre))
        act = (pre * sig).astype(bf16)
        normed_s[r] = normed
        dact_s[r] = sig * (1.0 + pre * (1.0 - sig))
        for i in range(3):
            dest = r - i + 1
            if 0 <= dest < height:
                act3[i * channels : (i + 1) * channels, dest * width : (dest + 1) * width] = act
        cot = cot_ref[r].astype(f32)
        bias_total = bias_total + cot
        place = slice(r * width, (r + 1) * width)
        ahead = jnp.where(lane < width - 1, pltpu.roll(cot, width - 1, axis=1), 0.0)
        behind = jnp.where(lane > 0, pltpu.roll(cot, 1, axis=1), 0.0)
        cot3[0:channels, place] = ahead.astype(bf16)
        cot3[channels : 2 * channels, place] = cot_ref[r]
        cot3[2 * channels : 3 * channels, place] = behind.astype(bf16)

    def kernel_step(n, carry):
        start = pl.multiple_of(n * 256, 256)
        block = lax.dot_general(
            act3[...],
            cot3[pl.ds(start, 256), :],
            (((1,), (1,)), ((), ())),
            preferred_element_type=f32,
        )
        kgrad[2 * n] = block[:, :LANES]
        kgrad[2 * n + 1] = block[:, LANES:]
        return carry

    lax.fori_loop(0, cot3.shape[0] // 256, kernel_step, 0)

    half = channels // 2
    low = lower_half((half, LANES))
    flat_rows = flat.shape[0]
    for i in range(3):
        for j in range(3):
            first = (j * channels) // LANES
            even = [kgrad[first + b, pl.ds(i * channels, half, stride=2), :] for b in range(3)]
            odd = [kgrad[first + b, pl.ds(i * channels + 1, half, stride=2), :] for b in range(3)]
            if j == 1:
                even_r = [swap_halves(e) for e in even]
                pieces = [
                    jnp.where(low, even_r[0], even_r[1]),
                    jnp.where(low, even_r[1], even_r[2]),
                    jnp.where(low, even_r[2], odd[0]),
                    odd[1],
                    odd[2],
                ]
            else:
                odd_r = [swap_halves(o) for o in odd]
                pieces = [
                    even[0],
                    even[1],
                    jnp.where(low, even[2], odd_r[0]),
                    jnp.where(low, odd_r[0], odd_r[1]),
                    jnp.where(low, odd_r[1], odd_r[2]),
                ]
            base = (3 * i + j) * (channels * channels // LANES)
            for b in range(5):
                flat[pl.ds(base + b, half, stride=5), :] = pieces[b]

    used = 9 * channels * channels // LANES
    flat[used:flat_rows, :] = jnp.zeros((flat_rows - used, LANES), f32)
    last = used // (shard_rows * line)

    def chunk(t):
        return (p + t) % plane

    def pair(t):
        q = chunk(t)
        return copy(send1.at[q], recv1.at[q], s1.at[t], r1.at[t], partner)

    def pair_start(t):
        q = chunk(t)
        for k in range(depth):
            row = ((q * depth + k) * 2 + 1 - core) * shard_rows
            send1[q, k] = flat[pl.ds(row, PAD_ROWS), :].astype(bf16)
        pair(t).start()

    def early(body):
        def step(t):
            @pl.when(chunk(t) != last)
            def _():
                body(t)

        return step

    pl.semaphore_wait(barrier, plane + line - 2)
    loop(1, plane, early(pair_start))
    early(pair_start)(0)

    w_copy.wait()
    wcat[...] = jnp.zeros_like(wcat)
    for i in range(3):
        for j in range(3):
            wcat[i * channels : (i + 1) * channels, j * channels : (j + 1) * channels] = w_ref[
                3 * i + j
            ]
    gact[...] = jnp.zeros_like(gact)

    def back_step(n, carry):
        start = pl.multiple_of(n * 256, 256)
        block = jnp.dot(wcat[...], cot3[:, pl.ds(start, 256)], preferred_element_type=f32)
        for i in range(3):
            for h in range(2):
                gact[2 * n + h + i] += block[
                    i * channels : (i + 1) * channels, h * width : (h + 1) * width
                ]
        return carry

    w_first = height // 4
    lax.fori_loop(0, w_first, back_step, 0)

    def across(t):
        return copy(send2.at[t], recv2.at[t], s2.at[t], r2.at[t], in_plane(t))

    def pair_sum(q, k):
        row = ((q * depth + k) * 2 + core) * shard_rows
        return flat[pl.ds(row, PAD_ROWS), :] + recv1[q, k].astype(f32)

    def across_start(t):
        pair(t).wait_recv()
        q = chunk(t)
        for k in range(depth):
            send2[t, k] = pair_sum(q, k).astype(bf16)
        across(t).start()

    loop(1, plane, early(across_start))

    lax.fori_loop(w_first, height // 2, back_step, 0)

    def sums_step(r, carry):
        shift_sum, gain_sum = carry
        dpre = gact[r + 1] * dact_s[r]
        gact[r + 1] = dpre
        return shift_sum + dpre, gain_sum + dpre * normed_s[r]

    shift_sum, gain_sum = lax.fori_loop(0, height, sums_step, (zero_block, zero_block))
    mean_grad = group_mean(shift_sum * gain)
    mean_cross = group_mean(gain_sum * gain)

    bias_row = as_row(jnp.sum(bias_total, axis=1, keepdims=True))
    gain_row = as_row(jnp.sum(gain_sum, axis=1, keepdims=True))
    shift_row = as_row(jnp.sum(shift_sum, axis=1, keepdims=True))
    flat[used : used + 1, :] = bias_row[:, 0:128]
    flat[used + 1 : used + 2, :] = bias_row[:, 128:256]
    flat[used + 2 : used + 3, 0:64] = bias_row[:, 256:320]
    flat[used + 2 : used + 3, 64:128] = gain_row[:, 0:64]
    flat[used + 3 : used + 4, :] = gain_row[:, 64:192]
    flat[used + 4 : used + 5, :] = gain_row[:, 192:320]
    flat[used + 5 : used + 6, :] = shift_row[:, 0:128]
    flat[used + 6 : used + 7, :] = shift_row[:, 128:256]
    flat[used + 7 : used + 8, 0:64] = shift_row[:, 256:320]

    last_t = (last + plane - p) % plane
    pair_start(last_t)

    def input_step(r, carry):
        slope = gact[r + 1] * gain
        gin_ref[r] = (rstd * (slope - mean_grad - normed_s[r] * mean_cross)).astype(bf16)
        return carry

    lax.fori_loop(0, height, input_step, 0)

    gin_copy = pltpu.make_async_copy(gin_ref, gin_hbm, gin_sem)
    gin_copy.start()

    @pl.when(p != last)
    def _():
        across_start(last_t)

    pair(0).wait_recv()
    for k in range(depth):
        acc[k] = pair_sum(p, k)

    def across_take(t):
        across(t).wait_recv()
        acc[...] += recv2[t].astype(f32)

    loop(1, plane, across_take)

    def along(t):
        return copy(acc.at[(z + t) % depth], recv3.at[t], s3.at[t], r3.at[t], in_depth(t))

    loop(1, depth, lambda t: along(t).start())
    recv3[0] = acc[z]
    loop(1, depth, lambda t: along(t).wait_recv())
    summed = recv3[0]
    for t in range(1, depth):
        summed = summed + recv3[t]
    live = lax.broadcasted_iota(jnp.int32, summed.shape, 0) < shard_rows
    summed = jnp.where(live, summed, 0.0)

    squares = summed * summed
    norm_line[0] = squares[0:8] + squares[8:16] + squares[16:24] + squares[24:32]

    def line_copy(t):
        return copy(norm_line.at[0], norm_line.at[t], sl.at[t], rl.at[t], in_line(t))

    loop(1, line, lambda t: line_copy(t).start())
    loop(1, line, lambda t: line_copy(t).wait_recv())
    part = norm_line[0]
    for t in range(1, line):
        part = part + norm_line[t]
    norm_plane[0] = part

    def plane_copy(t):
        return copy(norm_plane.at[0], norm_plane.at[t], sp.at[t], rp.at[t], in_plane(t))

    loop(1, plane, lambda t: plane_copy(t).start())
    loop(1, plane, lambda t: plane_copy(t).wait_recv())
    part = norm_plane[0]
    for t in range(1, plane):
        part = part + norm_plane[t]
    norm_total = jnp.sum(jnp.sum(part, axis=1, keepdims=True), axis=0, keepdims=True)

    clip = jnp.minimum(1.0, clip_limit / (jnp.sqrt(norm_total) + 1e-06))
    clipped = (clip * summed)[0:shard_rows]
    new_first = beta_first * first_ref[...] + (1.0 - beta_first) * clipped
    new_second = beta_second * second_ref[...] + (1.0 - beta_second) * clipped * clipped
    step_dir = new_first / correct_first / (jnp.sqrt(new_second / correct_second) + adam_epsilon)
    master = master_ref[...]
    new_master = master - learn_rate * (step_dir + weight_decay * master)
    new_master_ref[...] = new_master
    new_first_ref[...] = new_first
    new_second_ref[...] = new_second
    recv3[0, 0:shard_rows] = new_master
    gath[core, p, z] = recv3[0].astype(bf16)

    def gather_depth(t):
        mine = gath.at[core, p, z]
        return copy(mine, mine, sa.at[t], ra.at[t], in_depth(t))

    def gather_plane(t):
        mine = gath.at[core, p]
        return copy(mine, mine, sb.at[t], rb.at[t], in_plane(t))

    def gather_core(t):
        block = gath.at[core, (p + plane - t) % plane]
        return copy(block, block, sc.at[t], rc.at[t], partner)

    loop(1, depth, lambda t: gather_depth(t).start())
    loop(1, depth, lambda t: gather_depth(t).wait_recv())
    loop(1, plane, lambda t: gather_plane(t).start())
    gather_core(0).start()

    def keep(c, t):
        q = (p + plane - t) % plane
        return pltpu.make_async_copy(gath.at[c, q], gath_hbm.at[c, q], out_sem.at[c, t])

    keep(core, 0).start()

    def pass_on(t):
        gather_plane(t).wait_recv()
        gather_core(t).start()
        keep(core, t).start()

    loop(1, plane, pass_on)

    def take(t):
        gather_core(t).wait_recv()
        keep(1 - core, t).start()

    loop(0, plane, take)

    loop(0, plane, lambda t: pair(t).wait_send())
    loop(1, plane, lambda t: across(t).wait_send())
    loop(1, depth, lambda t: along(t).wait_send())
    loop(1, line, lambda t: line_copy(t).wait_send())
    loop(1, plane, lambda t: plane_copy(t).wait_send())
    loop(1, depth, lambda t: gather_depth(t).wait_send())
    loop(1, plane, lambda t: gather_plane(t).wait_send())
    loop(0, plane, lambda t: gather_core(t).wait_send())
    gin_copy.wait()
    loop(0, plane, lambda t: keep(core, t).wait())
    loop(0, plane, lambda t: keep(1 - core, t).wait())


def run_layer(x, cot, weight, gain, shift, master, first, second, plane, depth, split_rows):
    f32, bf16 = jnp.float32, jnp.bfloat16
    height, channels, width = x.shape
    line = 2 * depth
    wide = -(-3 * channels // 256) * 256
    flat_rows = plane * line * master.shape[0] + PAD_ROWS
    shard = jax.ShapeDtypeStruct(master.shape, f32)
    weight = weight.reshape(9, channels, channels)
    gathered = (2, plane, depth, PAD_ROWS, LANES)
    part = (plane, depth, PAD_ROWS, LANES)
    dma = lambda *n: pltpu.SemaphoreType.DMA(n)
    vmem, anywhere = pl.BlockSpec(memory_space=pltpu.VMEM), pl.BlockSpec(memory_space=pl.ANY)
    return pl.pallas_call(
        functools.partial(layer_kernel, split_rows, plane, depth),
        out_shape=(
            jax.ShapeDtypeStruct(x.shape, bf16),
            jax.ShapeDtypeStruct(gathered, bf16),
            shard,
            shard,
            shard,
        ),
        in_specs=[vmem, vmem, anywhere, vmem, vmem, vmem, vmem, vmem],
        out_specs=[anywhere, anywhere, vmem, vmem, vmem],
        scratch_shapes=[
            pltpu.VMEM(weight.shape, bf16),
            pltpu.VMEM(x.shape, bf16),
            pltpu.VMEM(gathered, bf16),
            pltpu.VMEM((3 * channels, height * width), bf16),
            pltpu.VMEM((wide, height * width), bf16),
            pltpu.VMEM((3 * channels, wide), bf16),
            pltpu.VMEM((wide // LANES, 3 * channels, LANES), f32),
            pltpu.VMEM((flat_rows, LANES), f32),
            pltpu.VMEM((height, channels, width), f32),
            pltpu.VMEM((height, channels, width), f32),
            pltpu.VMEM((height + 2, channels, width), f32),
            pltpu.VMEM(part, bf16),
            pltpu.VMEM(part, bf16),
            pltpu.VMEM(part, bf16),
            pltpu.VMEM(part, bf16),
            pltpu.VMEM((depth, PAD_ROWS, LANES), f32),
            pltpu.VMEM((depth, PAD_ROWS, LANES), f32),
            pltpu.VMEM((line, 8, LANES), f32),
            pltpu.VMEM((plane, 8, LANES), f32),
            pltpu.SemaphoreType.DMA,
            pltpu.SemaphoreType.DMA,
        ]
        + [dma(n) for n in (plane, plane, plane, plane, depth, depth, line, line)]
        + [dma(n) for n in (plane, plane, depth, depth, plane, plane, plane, plane)]
        + [dma(2, plane)],
        compiler_params=pltpu.CompilerParams(
            collective_id=0, has_side_effects=True, vmem_limit_bytes=VMEM_LIMIT
        ),
    )(x, cot, weight, gain, shift, master, first, second)


def unpack_kernel(shard_rows, gath, weight_ref, bias_ref, gain_ref, shift_ref, flat, rows):
    f32, bf16 = jnp.float32, jnp.bfloat16
    plane, depth = gath.shape[1], gath.shape[2]
    total, channels = weight_ref.shape

    def shard_step(q, carry):
        for core in range(2):
            block = gath[core, q // depth, q % depth].astype(f32)
            flat[pl.ds((2 * q + core) * shard_rows, PAD_ROWS), :] = block
        return carry

    lax.fori_loop(0, plane * depth, shard_step, 0)

    half = channels // 2
    low = lower_half((half, LANES))
    five = channels * channels // LANES

    def rows_step(n, carry):
        piece = [flat[pl.ds(n * five + b, half, stride=5), :] for b in range(5)]
        turned = [swap_halves(piece[b]) for b in range(2, 5)]
        even = [piece[0], piece[1], piece[2]]
        odd = [
            jnp.where(low, turned[0], turned[1]),
            jnp.where(low, turned[1], turned[2]),
            turned[2],
        ]
        for b in range(3):
            rows[b, pl.ds(0, half, stride=2), :] = even[b]
            rows[b, pl.ds(1, half, stride=2), :] = odd[b]
        place = pl.ds(pl.multiple_of(n * channels, channels), channels)
        weight_ref[place, 0:128] = rows[0].astype(bf16)
        weight_ref[place, 128:256] = rows[1].astype(bf16)
        weight_ref[place, 256:channels] = rows[2, :, 0 : channels - 256].astype(bf16)
        return carry

    lax.fori_loop(0, total // channels, rows_step, 0)

    used = total * channels // LANES
    tail = [flat[used + b : used + b + 1, :].astype(bf16) for b in range(8)]
    bias_ref[:, 0:128] = tail[0]
    bias_ref[:, 128:256] = tail[1]
    bias_ref[:, 256:320] = tail[2][:, 0:64]
    gain_ref[:, 0:64] = tail[2][:, 64:128]
    gain_ref[:, 64:192] = tail[3]
    gain_ref[:, 192:320] = tail[4]
    shift_ref[:, 0:128] = tail[5]
    shift_ref[:, 128:256] = tail[6]
    shift_ref[:, 256:320] = tail[7][:, 0:64]


def unpack(gath, channels, shard_rows):
    bf16, f32 = jnp.bfloat16, jnp.float32
    shards = 2 * gath.shape[1] * gath.shape[2]
    row = jax.ShapeDtypeStruct((1, channels), bf16)
    return pl.pallas_call(
        functools.partial(unpack_kernel, shard_rows),
        out_shape=(jax.ShapeDtypeStruct((9 * channels, channels), bf16), row, row, row),
        scratch_shapes=[
            pltpu.VMEM((shards * shard_rows + PAD_ROWS, LANES), f32),
            pltpu.VMEM((3, channels, LANES), f32),
        ],
        compiler_params=pltpu.CompilerParams(vmem_limit_bytes=VMEM_LIMIT),
    )(gath)


def on_device(latents, cotangent, weight, gain, shift, master, first_moment, second_moment):
    groups, owners = lax.axis_size("grp"), lax.axis_size("dp")
    channels = weight.shape[2]
    split_rows = 2
    depth = owners // (2 * split_rows)
    plane = groups * split_rows
    shard_rows = master.shape[0] // LANES
    x = jnp.transpose(latents[0], (0, 2, 1))
    cot = jnp.transpose(cotangent[0], (0, 2, 1))
    shaped = [a.reshape(shard_rows, LANES) for a in (master, first_moment, second_moment)]
    grad_in, gath, new_master, new_first, new_second = run_layer(
        x, cot, weight, gain, shift, *shaped, plane, depth, split_rows
    )
    new_weight, new_bias, new_gain, new_shift = unpack(gath, channels, shard_rows)
    return (
        jnp.transpose(grad_in, (0, 2, 1))[None],
        new_weight.reshape(weight.shape),
        new_bias.reshape(channels),
        new_gain.reshape(channels),
        new_shift.reshape(channels),
        new_master.reshape(-1),
        new_first.reshape(-1),
        new_second.reshape(-1),
    )


def solution(mesh):
    split = ("grp", "dp")
    whole = P(split, None, None, None)
    in_specs = (whole, whole, P(), P(), P(), P(split), P(split), P(split))
    out_specs = (whole, P(), P(), P(), P(), P(split), P(split), P(split))
    return jax.shard_map(
        on_device, mesh=mesh, in_specs=in_specs, out_specs=out_specs, check_vma=False
    )
```

```python
import functools

import jax
import jax.numpy as jnp
from jax import lax
from jax.experimental import pallas as pl
from jax.experimental.pallas import tpu as pltpu
from jax.sharding import PartitionSpec as P

GROUPS = 32
LANES = 128
PAD_ROWS = 32

norm_epsilon = 1e-05
beta_first = 0.9
beta_second = 0.999
adam_epsilon = 1e-08
learn_rate = 0.001
weight_decay = 0.01
clip_limit = 1.0
correct_first = 1.0
correct_second = 0.6323045752290363

MESH = pl.DeviceIdType.MESH
VMEM_LIMIT = 60 * 1024 * 1024


def swap_halves(block):
    return pltpu.roll(block, LANES // 2, axis=1)


def lower_half(shape):
    return lax.broadcasted_iota(jnp.int32, shape, 1) < LANES // 2


def layer_kernel(
    split_rows,
    plane,
    depth,
    x_ref,
    cot_ref,
    w_hbm,
    gain_ref,
    shift_ref,
    master_ref,
    first_ref,
    second_ref,
    gin_hbm,
    wout_hbm,
    tail_ref,
    new_master_ref,
    new_first_ref,
    new_second_ref,
    w_ref,
    gin_ref,
    gath,
    wout,
    rows,
    act3,
    cot3,
    wcat,
    kgrad,
    flat,
    normed_s,
    dact_s,
    gact,
    send1,
    recv1,
    send2,
    recv2,
    acc,
    recv3,
    norm_line,
    norm_plane,
    w_sem,
    gin_sem,
    s1,
    r1,
    s2,
    r2,
    s3,
    r3,
    sl,
    rl,
    sp,
    rp,
    sa,
    ra,
    sb,
    rb,
    sc,
    rc,
    out_sem,
):
    f32, bf16 = jnp.float32, jnp.bfloat16
    line = 2 * depth
    grp, dp = lax.axis_index("grp"), lax.axis_index("dp")
    p = grp * split_rows + dp // line
    spot = dp % line
    z, core = spot // 2, spot % 2
    shard_rows = master_ref.shape[0]

    def device(p_, spot_):
        return (p_ // split_rows, (p_ % split_rows) * line + spot_)

    def in_plane(t):
        return device((p + t) % plane, spot)

    def in_line(t):
        return device(p, (spot + t) % line)

    def in_depth(t):
        return device(p, ((z + t) % depth) * 2 + core)

    partner = device(p, z * 2 + 1 - core)

    def copy(src, dst, send, recv, target):
        return pltpu.make_async_remote_copy(
            src_ref=src,
            dst_ref=dst,
            send_sem=send,
            recv_sem=recv,
            device_id=target,
            device_id_type=MESH,
        )

    def loop(lo, hi, body):
        def step(t, carry):
            body(t)
            return carry

        lax.fori_loop(lo, hi, step, 0)

    barrier = pltpu.get_barrier_semaphore()

    def greet(target):
        pl.semaphore_signal(barrier, inc=1, device_id=target, device_id_type=MESH)

    loop(1, plane, lambda t: greet(in_plane(t)))
    loop(1, line, lambda t: greet(in_line(t)))
    w_copy = pltpu.make_async_copy(w_hbm, w_ref, w_sem)
    w_copy.start()

    height, channels, width = x_ref.shape
    count = height * width * (channels // GROUPS)

    row_id = lax.broadcasted_iota(jnp.int32, (channels, channels), 0)
    col_id = lax.broadcasted_iota(jnp.int32, (channels, channels), 1)
    eye = (row_id == col_id).astype(f32)
    per = 1.0 / (channels // GROUPS)
    row_group = jnp.floor((row_id.astype(f32) + 0.5) * per)
    col_group = jnp.floor((col_id.astype(f32) + 0.5) * per)
    same_group = (row_group == col_group).astype(f32)

    def group_mean(block):
        mixed = jnp.dot(
            same_group, block, precision=lax.Precision.HIGHEST, preferred_element_type=f32
        )
        return jnp.sum(mixed, axis=1, keepdims=True) * (1.0 / count)

    def as_column(row):
        return jnp.sum(eye * row, axis=1, keepdims=True)

    def as_row(column):
        return jnp.sum(eye * column, axis=0, keepdims=True)

    gain = as_column(gain_ref[...].reshape(1, channels))
    shift = as_column(shift_ref[...].reshape(1, channels))

    zero_block = jnp.zeros((channels, width), f32)
    total = lax.fori_loop(
        0, height, lambda r, s: s + x_ref[r].astype(f32), zero_block
    )
    centre = group_mean(total)

    def spread_step(r, s):
        centred = x_ref[r].astype(f32) - centre
        return s + centred * centred

    spread = group_mean(lax.fori_loop(0, height, spread_step, zero_block))
    rstd = lax.rsqrt(spread + norm_epsilon)

    lane = lax.broadcasted_iota(jnp.int32, (channels, width), 1)
    zero_bf = jnp.zeros((channels, width), bf16)
    act3[0:channels, 0:width] = zero_bf
    act3[2 * channels : 3 * channels, (height - 1) * width : height * width] = zero_bf
    cot3[3 * channels :, :] = jnp.zeros((cot3.shape[0] - 3 * channels, cot3.shape[1]), bf16)

    bias_total = zero_block
    for r in range(height):
        normed = (x_ref[r].astype(f32) - centre) * rstd
        pre = normed * gain + shift
        sig = 1.0 / (1.0 + jnp.exp(-pre))
        act = (pre * sig).astype(bf16)
        normed_s[r] = normed
        dact_s[r] = sig * (1.0 + pre * (1.0 - sig))
        for i in range(3):
            dest = r - i + 1
            if 0 <= dest < height:
                act3[i * channels : (i + 1) * channels, dest * width : (dest + 1) * width] = act
        cot = cot_ref[r].astype(f32)
        bias_total = bias_total + cot
        place = slice(r * width, (r + 1) * width)
        ahead = jnp.where(lane < width - 1, pltpu.roll(cot, width - 1, axis=1), 0.0)
        behind = jnp.where(lane > 0, pltpu.roll(cot, 1, axis=1), 0.0)
        cot3[0:channels, place] = ahead.astype(bf16)
        cot3[channels : 2 * channels, place] = cot_ref[r]
        cot3[2 * channels : 3 * channels, place] = behind.astype(bf16)

    def kernel_step(n, carry):
        start = pl.multiple_of(n * 256, 256)
        block = lax.dot_general(
            act3[...],
            cot3[pl.ds(start, 256), :],
            (((1,), (1,)), ((), ())),
            preferred_element_type=f32,
        )
        kgrad[2 * n] = block[:, :LANES]
        kgrad[2 * n + 1] = block[:, LANES:]
        return carry

    lax.fori_loop(0, cot3.shape[0] // 256, kernel_step, 0)

    half = channels // 2
    low = lower_half((half, LANES))
    flat_rows = flat.shape[0]
    for i in range(3):
        for j in range(3):
            first = (j * channels) // LANES
            even = [kgrad[first + b, pl.ds(i * channels, half, stride=2), :] for b in range(3)]
            odd = [kgrad[first + b, pl.ds(i * channels + 1, half, stride=2), :] for b in range(3)]
            if j == 1:
                even_r = [swap_halves(e) for e in even]
                pieces = [
                    jnp.where(low, even_r[0], even_r[1]),
                    jnp.where(low, even_r[1], even_r[2]),
                    jnp.where(low, even_r[2], odd[0]),
                    odd[1],
                    odd[2],
                ]
            else:
                odd_r = [swap_halves(o) for o in odd]
                pieces = [
                    even[0],
                    even[1],
                    jnp.where(low, even[2], odd_r[0]),
                    jnp.where(low, odd_r[0], odd_r[1]),
                    jnp.where(low, odd_r[1], odd_r[2]),
                ]
            base = (3 * i + j) * (channels * channels // LANES)
            for b in range(5):
                flat[pl.ds(base + b, half, stride=5), :] = pieces[b]

    used = 9 * channels * channels // LANES
    flat[used:flat_rows, :] = jnp.zeros((flat_rows - used, LANES), f32)
    last = used // (shard_rows * line)

    def chunk(t):
        return (p + t) % plane

    def pair(t):
        q = chunk(t)
        return copy(send1.at[q], recv1.at[q], s1.at[t], r1.at[t], partner)

    def pair_start(t):
        q = chunk(t)
        for k in range(depth):
            row = ((q * depth + k) * 2 + 1 - core) * shard_rows
            send1[q, k] = flat[pl.ds(row, PAD_ROWS), :].astype(bf16)
        pair(t).start()

    def early(body):
        def step(t):
            @pl.when(chunk(t) != last)
            def _():
                body(t)

        return step

    pl.semaphore_wait(barrier, plane + line - 2)
    loop(1, plane, early(pair_start))
    early(pair_start)(0)

    w_copy.wait()
    wcat[...] = jnp.zeros_like(wcat)
    for i in range(3):
        for j in range(3):
            wcat[i * channels : (i + 1) * channels, j * channels : (j + 1) * channels] = w_ref[
                3 * i + j
            ]
    gact[...] = jnp.zeros_like(gact)

    def back_step(n, carry):
        start = pl.multiple_of(n * 256, 256)
        block = jnp.dot(wcat[...], cot3[:, pl.ds(start, 256)], preferred_element_type=f32)
        for i in range(3):
            for h in range(2):
                gact[2 * n + h + i] += block[
                    i * channels : (i + 1) * channels, h * width : (h + 1) * width
                ]
        return carry

    w_first = height // 4
    lax.fori_loop(0, w_first, back_step, 0)

    def across(t):
        return copy(send2.at[t], recv2.at[t], s2.at[t], r2.at[t], in_plane(t))

    def pair_sum(q, k):
        row = ((q * depth + k) * 2 + core) * shard_rows
        return flat[pl.ds(row, PAD_ROWS), :] + recv1[q, k].astype(f32)

    def across_start(t):
        pair(t).wait_recv()
        q = chunk(t)
        for k in range(depth):
            send2[t, k] = pair_sum(q, k).astype(bf16)
        across(t).start()

    loop(1, plane, early(across_start))

    lax.fori_loop(w_first, height // 2, back_step, 0)

    def sums_step(r, carry):
        shift_sum, gain_sum = carry
        dpre = gact[r + 1] * dact_s[r]
        gact[r + 1] = dpre
        return shift_sum + dpre, gain_sum + dpre * normed_s[r]

    shift_sum, gain_sum = lax.fori_loop(0, height, sums_step, (zero_block, zero_block))
    mean_grad = group_mean(shift_sum * gain)
    mean_cross = group_mean(gain_sum * gain)

    bias_row = as_row(jnp.sum(bias_total, axis=1, keepdims=True))
    gain_row = as_row(jnp.sum(gain_sum, axis=1, keepdims=True))
    shift_row = as_row(jnp.sum(shift_sum, axis=1, keepdims=True))
    flat[used : used + 1, :] = bias_row[:, 0:128]
    flat[used + 1 : used + 2, :] = bias_row[:, 128:256]
    flat[used + 2 : used + 3, 0:64] = bias_row[:, 256:320]
    flat[used + 2 : used + 3, 64:128] = gain_row[:, 0:64]
    flat[used + 3 : used + 4, :] = gain_row[:, 64:192]
    flat[used + 4 : used + 5, :] = gain_row[:, 192:320]
    flat[used + 5 : used + 6, :] = shift_row[:, 0:128]
    flat[used + 6 : used + 7, :] = shift_row[:, 128:256]
    flat[used + 7 : used + 8, 0:64] = shift_row[:, 256:320]

    last_t = (last + plane - p) % plane
    pair_start(last_t)

    def input_step(r, carry):
        slope = gact[r + 1] * gain
        gin_ref[r] = (rstd * (slope - mean_grad - normed_s[r] * mean_cross)).astype(bf16)
        return carry

    lax.fori_loop(0, height, input_step, 0)

    gin_copy = pltpu.make_async_copy(gin_ref, gin_hbm, gin_sem)
    gin_copy.start()

    @pl.when(p != last)
    def _():
        across_start(last_t)

    pair(0).wait_recv()
    for k in range(depth):
        acc[k] = pair_sum(p, k)

    def across_take(t):
        across(t).wait_recv()
        acc[...] += recv2[t].astype(f32)

    loop(1, plane, across_take)

    def along(t):
        return copy(acc.at[(z + t) % depth], recv3.at[t], s3.at[t], r3.at[t], in_depth(t))

    loop(1, depth, lambda t: along(t).start())
    recv3[0] = acc[z]
    loop(1, depth, lambda t: along(t).wait_recv())
    summed = recv3[0]
    for t in range(1, depth):
        summed = summed + recv3[t]
    live = lax.broadcasted_iota(jnp.int32, summed.shape, 0) < shard_rows
    summed = jnp.where(live, summed, 0.0)

    squares = summed * summed
    norm_line[0] = squares[0:8] + squares[8:16] + squares[16:24] + squares[24:32]

    def line_copy(t):
        return copy(norm_line.at[0], norm_line.at[t], sl.at[t], rl.at[t], in_line(t))

    loop(1, line, lambda t: line_copy(t).start())
    loop(1, line, lambda t: line_copy(t).wait_recv())
    sumsq = norm_line[0]
    for t in range(1, line):
        sumsq = sumsq + norm_line[t]
    norm_plane[0] = sumsq

    def plane_copy(t):
        return copy(norm_plane.at[0], norm_plane.at[t], sp.at[t], rp.at[t], in_plane(t))

    loop(1, plane, lambda t: plane_copy(t).start())
    loop(1, plane, lambda t: plane_copy(t).wait_recv())
    sumsq = norm_plane[0]
    for t in range(1, plane):
        sumsq = sumsq + norm_plane[t]
    norm_total = jnp.sum(jnp.sum(sumsq, axis=1, keepdims=True), axis=0, keepdims=True)

    clip = jnp.minimum(1.0, clip_limit / (jnp.sqrt(norm_total) + 1e-06))
    clipped = (clip * summed)[0:shard_rows]
    new_first = beta_first * first_ref[...] + (1.0 - beta_first) * clipped
    new_second = beta_second * second_ref[...] + (1.0 - beta_second) * clipped * clipped
    step_dir = new_first / correct_first / (jnp.sqrt(new_second / correct_second) + adam_epsilon)
    master = master_ref[...]
    new_master = master - learn_rate * (step_dir + weight_decay * master)
    new_master_ref[...] = new_master
    new_first_ref[...] = new_first
    new_second_ref[...] = new_second
    recv3[0, 0:shard_rows] = new_master
    gath[core, p // gath.shape[2], p % gath.shape[2], z] = recv3[0].astype(bf16)

    x_size, w_size = gath.shape[1], gath.shape[2]
    half_depth = depth // 2
    xi, wi = p // w_size, p % w_size

    def gather_depth(t):
        mine = gath.at[core, xi, wi, z]
        return copy(mine, mine, sa.at[t], ra.at[t], in_depth(t))

    def back_x(t):
        return (xi + x_size - t) % x_size

    def back_w(t):
        return (wi + w_size - t) % w_size

    def part(c, h, tx, tw):
        return gath.at[c, back_x(tx), back_w(tw), pl.ds(h * half_depth, half_depth)]

    def slots_x(h, t, tw):
        spots = (h, t, 0) if h == 0 else (h, tw, t)
        return sb.at[spots], rb.at[spots]

    def slots_w(h, t, tx):
        spots = (h, t, 0) if h == 1 else (h, tx, t)
        return sb.at[spots], rb.at[spots]

    def along_x(h, t, tw):
        block = part(core, h, 0, tw)
        target = device(((xi + t) % x_size) * w_size + wi, spot)
        return copy(block, block, *slots_x(h, t, tw), target)

    def along_w(h, t, tx):
        block = part(core, h, tx, 0)
        target = device(xi * w_size + (wi + t) % w_size, spot)
        return copy(block, block, *slots_w(h, t, tx), target)

    def got_x(h, t, tw):
        block = part(core, h, t, tw)
        target = device(((xi + t) % x_size) * w_size + wi, spot)
        return copy(block, block, *slots_x(h, t, tw), target)

    def got_w(h, t, tx):
        block = part(core, h, tx, t)
        target = device(xi * w_size + (wi + t) % w_size, spot)
        return copy(block, block, *slots_w(h, t, tx), target)

    def gather_core(h, tx, tw):
        block = part(core, h, tx, tw)
        return copy(block, block, sc.at[h, tx, tw], rc.at[h, tx, tw], partner)

    def got_core(h, tx, tw):
        block = part(1 - core, h, tx, tw)
        return copy(block, block, sc.at[h, tx, tw], rc.at[h, tx, tw], partner)

    def to_flat(c, h, tx, tw):
        sx, sw = back_x(tx), back_w(tw)
        for k in range(half_depth):
            spot_k = (h * half_depth + k) * 2 + c
            row = ((sx * w_size + sw) * line + spot_k) * shard_rows
            block = gath[c, sx, sw, h * half_depth + k].astype(f32)
            flat[pl.ds(row, shard_rows), :] = block[0:shard_rows]

    loop(1, depth, lambda t: gather_depth(t).start())
    loop(1, depth, lambda t: gather_depth(t).wait_recv())
    loop(1, x_size, lambda t: along_x(0, t, 0).start())
    loop(1, w_size, lambda t: along_w(1, t, 0).start())
    loop(1, w_size, lambda t: along_w(0, t, 0).start())
    loop(1, x_size, lambda t: along_x(1, t, 0).start())
    gather_core(0, 0, 0).start()
    gather_core(1, 0, 0).start()
    to_flat(core, 0, 0, 0)
    to_flat(core, 1, 0, 0)

    def first_x(t):
        got_x(0, t, 0).wait_recv()
        loop(1, w_size, lambda s: along_w(0, s, t).start())
        gather_core(0, t, 0).start()

    def first_w(t):
        got_w(1, t, 0).wait_recv()
        loop(1, x_size, lambda s: along_x(1, s, t).start())
        gather_core(1, 0, t).start()

    def first(t):
        first_x(t)
        first_w(t)

    loop(1, x_size, first)

    def first_flat(t):
        to_flat(core, 0, t, 0)
        to_flat(core, 1, 0, t)

    loop(1, x_size, first_flat)

    def second(n):
        a, b = n // (w_size - 1), n % (w_size - 1) + 1
        got_w(0, b, a).wait_recv()
        gather_core(0, a, b).start()
        got_x(1, b, a).wait_recv()
        gather_core(1, b, a).start()
        to_flat(core, 0, a, b)
        to_flat(core, 1, b, a)

    loop(0, x_size * (w_size - 1), second)

    def third(n):
        a, b = n // w_size, n % w_size
        got_core(0, a, b).wait_recv()
        to_flat(1 - core, 0, a, b)
        got_core(1, b, a).wait_recv()
        to_flat(1 - core, 1, b, a)

    loop(0, x_size * w_size, third)

    five = channels * channels // LANES

    def wout_copy(n):
        place = pl.ds(pl.multiple_of(n * channels, channels), channels)
        return pltpu.make_async_copy(wout.at[place], wout_hbm.at[place], out_sem.at[n])

    def rows_step(n):
        piece = [flat[pl.ds(n * five + b, half, stride=5), :] for b in range(5)]
        turned = [swap_halves(piece[b]) for b in range(2, 5)]
        even = [piece[0], piece[1], piece[2]]
        odd = [
            jnp.where(low, turned[0], turned[1]),
            jnp.where(low, turned[1], turned[2]),
            turned[2],
        ]
        for b in range(3):
            rows[b, pl.ds(0, half, stride=2), :] = even[b]
            rows[b, pl.ds(1, half, stride=2), :] = odd[b]
        place = pl.ds(pl.multiple_of(n * channels, channels), channels)
        wout[place, 0:128] = rows[0].astype(bf16)
        wout[place, 128:256] = rows[1].astype(bf16)
        wout[place, 256:channels] = rows[2, :, 0 : channels - 256].astype(bf16)
        wout_copy(n).start()

    loop(0, 9, rows_step)
    tail_ref[...] = flat[used : used + 8, :]

    loop(0, plane, lambda t: pair(t).wait_send())
    loop(1, plane, lambda t: across(t).wait_send())
    loop(1, depth, lambda t: along(t).wait_send())
    loop(1, line, lambda t: line_copy(t).wait_send())
    loop(1, plane, lambda t: plane_copy(t).wait_send())
    loop(1, depth, lambda t: gather_depth(t).wait_send())

    def all_sent(n):
        a, b = n // w_size, n % w_size
        gather_core(0, a, b).wait_send()
        gather_core(1, a, b).wait_send()

        @pl.when(b > 0)
        def _():
            along_w(0, b, a).wait_send()
            along_x(1, b, a).wait_send()

    loop(0, x_size * w_size, all_sent)
    loop(1, x_size, lambda t: along_x(0, t, 0).wait_send())
    loop(1, w_size, lambda t: along_w(1, t, 0).wait_send())
    gin_copy.wait()
    loop(0, 9, lambda n: wout_copy(n).wait())


def run_layer(x, cot, weight, gain, shift, master, first, second, plane, depth, split_rows):
    f32, bf16 = jnp.float32, jnp.bfloat16
    height, channels, width = x.shape
    line = 2 * depth
    wide = -(-3 * channels // 256) * 256
    flat_rows = plane * line * master.shape[0] + PAD_ROWS
    shard = jax.ShapeDtypeStruct(master.shape, f32)
    weight = weight.reshape(9, channels, channels)
    ring_w = 2 * split_rows
    ring_x = plane // ring_w
    gathered = (2, ring_x, ring_w, depth, PAD_ROWS, LANES)
    part = (plane, depth, PAD_ROWS, LANES)
    dma = lambda *n: pltpu.SemaphoreType.DMA(n)
    vmem, anywhere = pl.BlockSpec(memory_space=pltpu.VMEM), pl.BlockSpec(memory_space=pl.ANY)
    return pl.pallas_call(
        functools.partial(layer_kernel, split_rows, plane, depth),
        out_shape=(
            jax.ShapeDtypeStruct(x.shape, bf16),
            jax.ShapeDtypeStruct((9 * channels, channels), bf16),
            jax.ShapeDtypeStruct((8, LANES), f32),
            shard,
            shard,
            shard,
        ),
        in_specs=[vmem, vmem, anywhere, vmem, vmem, vmem, vmem, vmem],
        out_specs=[anywhere, anywhere, vmem, vmem, vmem, vmem],
        scratch_shapes=[
            pltpu.VMEM(weight.shape, bf16),
            pltpu.VMEM(x.shape, bf16),
            pltpu.VMEM(gathered, bf16),
            pltpu.VMEM((9 * channels, channels), bf16),
            pltpu.VMEM((3, channels, LANES), f32),
            pltpu.VMEM((3 * channels, height * width), bf16),
            pltpu.VMEM((wide, height * width), bf16),
            pltpu.VMEM((3 * channels, wide), bf16),
            pltpu.VMEM((wide // LANES, 3 * channels, LANES), f32),
            pltpu.VMEM((flat_rows, LANES), f32),
            pltpu.VMEM((height, channels, width), f32),
            pltpu.VMEM((height, channels, width), f32),
            pltpu.VMEM((height + 2, channels, width), f32),
            pltpu.VMEM(part, bf16),
            pltpu.VMEM(part, bf16),
            pltpu.VMEM(part, bf16),
            pltpu.VMEM(part, bf16),
            pltpu.VMEM((depth, PAD_ROWS, LANES), f32),
            pltpu.VMEM((depth, PAD_ROWS, LANES), f32),
            pltpu.VMEM((line, 8, LANES), f32),
            pltpu.VMEM((plane, 8, LANES), f32),
            pltpu.SemaphoreType.DMA,
            pltpu.SemaphoreType.DMA,
        ]
        + [dma(n) for n in (plane, plane, plane, plane, depth, depth, line, line)]
        + [dma(n) for n in (plane, plane, depth, depth)]
        + [dma(2, ring_x, ring_w)] * 4
        + [dma(9)],
        compiler_params=pltpu.CompilerParams(
            collective_id=0, has_side_effects=True, vmem_limit_bytes=VMEM_LIMIT
        ),
    )(x, cot, weight, gain, shift, master, first, second)


def finish_kernel(tail_ref, *refs):
    bf16 = jnp.bfloat16
    count = 5
    sources, targets = refs[:count], refs[count : 2 * count]
    bias_ref, gain_ref, shift_ref = refs[2 * count : 2 * count + 3]
    stages, in_sem, out_sem = refs[2 * count + 3 : 3 * count + 3], refs[-2], refs[-1]
    ins, outs = [], []
    for n in range(count):
        rows = sources[n].shape[0]
        cuts = 4 if n < 2 else 1
        for c in range(cuts):
            place = pl.ds(c * (rows // cuts), rows // cuts)
            k = len(ins)
            ins.append(
                pltpu.make_async_copy(sources[n].at[place], stages[n].at[place], in_sem.at[k])
            )
            outs.append(
                pltpu.make_async_copy(stages[n].at[place], targets[n].at[place], out_sem.at[k])
            )
    for each in ins:
        each.start()
    tail = [tail_ref[b : b + 1, :] for b in range(8)]
    rows = (
        [tail[0], tail[1], tail[2][:, 0:64]],
        [tail[2][:, 64:128], tail[3], tail[4]],
        [tail[5], tail[6], tail[7][:, 0:64]],
    )
    for ref, row in zip((bias_ref, gain_ref, shift_ref), rows):
        ref[...] = jnp.concatenate(row, axis=1).astype(bf16).reshape(ref.shape)
    for arrived, leaving in zip(ins, outs):
        arrived.wait()
        leaving.start()
    for each in outs:
        each.wait()


def finish(tail, results, channels):
    row = jax.ShapeDtypeStruct((channels,), jnp.bfloat16)
    vmem, anywhere = pl.BlockSpec(memory_space=pltpu.VMEM), pl.BlockSpec(memory_space=pl.ANY)
    return pl.pallas_call(
        finish_kernel,
        out_shape=tuple(jax.ShapeDtypeStruct(r.shape, r.dtype) for r in results) + (row,) * 3,
        in_specs=[vmem] + [anywhere] * 5,
        out_specs=[anywhere] * 5 + [vmem] * 3,
        scratch_shapes=[pltpu.VMEM(r.shape, r.dtype) for r in results]
        + [pltpu.SemaphoreType.DMA((11,))] * 2,
    )(tail, *results)


def on_device(latents, cotangent, weight, gain, shift, master, first_moment, second_moment):
    groups, owners = lax.axis_size("grp"), lax.axis_size("dp")
    channels = weight.shape[2]
    split_rows = 2
    depth = owners // (2 * split_rows)
    plane = groups * split_rows
    shard_rows = master.shape[0] // LANES
    x = jnp.transpose(latents[0], (0, 2, 1))
    cot = jnp.transpose(cotangent[0], (0, 2, 1))
    shaped = [a.reshape(shard_rows, LANES) for a in (master, first_moment, second_moment)]
    grad_in, new_weight, tail, *state = run_layer(
        x, cot, weight, gain, shift, *shaped, plane, depth, split_rows
    )
    results = finish(tail, (grad_in, new_weight, *state), channels)
    grad_in, new_weight, new_master, new_first, new_second = results[:5]
    new_bias, new_gain, new_shift = results[5:]
    return (
        jnp.transpose(grad_in, (0, 2, 1))[None],
        new_weight.reshape(weight.shape),
        new_bias,
        new_gain,
        new_shift,
        new_master.reshape(-1),
        new_first.reshape(-1),
        new_second.reshape(-1),
    )


def solution(mesh):
    split = ("grp", "dp")
    whole = P(split, None, None, None)
    in_specs = (whole, whole, P(), P(), P(), P(split), P(split), P(split))
    out_specs = (whole, P(), P(), P(), P(), P(split), P(split), P(split))
    return jax.shard_map(
        on_device, mesh=mesh, in_specs=in_specs, out_specs=out_specs, check_vma=False
    )
```

```python
import functools

import jax
import jax.numpy as jnp
from jax import lax
from jax.experimental import pallas as pl
from jax.experimental.pallas import tpu as pltpu
from jax.sharding import PartitionSpec as P

GROUPS = 32
LANES = 128
PAD_ROWS = 32

norm_epsilon = 1e-05
beta_first = 0.9
beta_second = 0.999
adam_epsilon = 1e-08
learn_rate = 0.001
weight_decay = 0.01
clip_limit = 1.0
correct_first = 1.0
correct_second = 0.6323045752290363

MESH = pl.DeviceIdType.MESH
VMEM_LIMIT = 48 * 1024 * 1024


def swap_halves(block):
    return pltpu.roll(block, LANES // 2, axis=1)


def lower_half(shape):
    return lax.broadcasted_iota(jnp.int32, shape, 1) < LANES // 2


def layer_kernel(
    split_rows,
    plane,
    depth,
    x_hbm,
    cot_hbm,
    w_hbm,
    gain_hbm,
    shift_hbm,
    master_hbm,
    first_hbm,
    second_hbm,
    gin_ref,
    wout,
    tail_ref,
    new_master_ref,
    new_first_ref,
    new_second_ref,
    x_ref,
    cot_ref,
    w_ref,
    gain_ref,
    shift_ref,
    gath,
    rows,
    act3,
    cot3,
    wcat,
    kgrad,
    flat,
    normed_s,
    dact_s,
    gact,
    send1,
    recv1,
    send2,
    recv2,
    acc,
    recv3,
    state,
    gsum,
    norm_line,
    norm_plane,
    tails,
    in_sem,
    s1,
    r1,
    s2,
    r2,
    s3,
    r3,
    sl,
    rl,
    sp,
    rp,
    ss,
    rs,
    sg,
    rg,
    sb,
    rb,
    sc,
    rc,
    st,
    rt,
):
    f32, bf16 = jnp.float32, jnp.bfloat16
    line = 2 * depth
    grp, dp = lax.axis_index("grp"), lax.axis_index("dp")
    p = grp * split_rows + dp // line
    spot = dp % line
    z, core = spot // 2, spot % 2
    shard_rows = master_hbm.shape[0]

    def device(p_, spot_):
        return (p_ // split_rows, (p_ % split_rows) * line + spot_)

    def in_plane(t):
        return device((p + t) % plane, spot)

    def in_line(t):
        return device(p, (spot + t) % line)

    def in_depth(t):
        return device(p, ((z + t) % depth) * 2 + core)

    partner = device(p, z * 2 + 1 - core)

    def copy(src, dst, send, recv, target):
        return pltpu.make_async_remote_copy(
            src_ref=src,
            dst_ref=dst,
            send_sem=send,
            recv_sem=recv,
            device_id=target,
            device_id_type=MESH,
        )

    def loop(lo, hi, body):
        def step(t, carry):
            body(t)
            return carry

        lax.fori_loop(lo, hi, step, 0)

    state[z] = jnp.zeros(state.shape[1:], f32)
    pairs = [(x_hbm, x_ref), (gain_hbm, gain_ref), (shift_hbm, shift_ref)]
    pairs += [(cot_hbm, cot_ref), (w_hbm, w_ref)]
    for n, ref in enumerate((master_hbm, first_hbm, second_hbm)):
        pairs.append((ref, state.at[z, n, pl.ds(0, shard_rows)]))
    loads = [
        pltpu.make_async_copy(source, target, in_sem.at[n])
        for n, (source, target) in enumerate(pairs)
    ]
    for load in loads:
        load.start()

    barrier = pltpu.get_barrier_semaphore()

    def greet(target):
        pl.semaphore_signal(barrier, inc=1, device_id=target, device_id_type=MESH)

    loop(1, plane, lambda t: greet(in_plane(t)))
    loop(1, line, lambda t: greet(in_line(t)))

    height, channels, width = x_ref.shape
    count = height * width * (channels // GROUPS)

    row_id = lax.broadcasted_iota(jnp.int32, (channels, channels), 0)
    col_id = lax.broadcasted_iota(jnp.int32, (channels, channels), 1)
    eye = (row_id == col_id).astype(f32)
    per = 1.0 / (channels // GROUPS)
    row_group = jnp.floor((row_id.astype(f32) + 0.5) * per)
    col_group = jnp.floor((col_id.astype(f32) + 0.5) * per)
    same_group = (row_group == col_group).astype(f32)

    def group_mean(block):
        mixed = jnp.dot(
            same_group, block, precision=lax.Precision.HIGHEST, preferred_element_type=f32
        )
        return jnp.sum(mixed, axis=1, keepdims=True) * (1.0 / count)

    def as_column(row):
        return jnp.sum(eye * row, axis=1, keepdims=True)

    def as_row(column):
        return jnp.sum(eye * column, axis=0, keepdims=True)

    for load in loads[:3]:
        load.wait()
    gain = as_column(gain_ref[...].reshape(1, channels))
    shift = as_column(shift_ref[...].reshape(1, channels))

    zero_block = jnp.zeros((channels, width), f32)
    total = lax.fori_loop(
        0, height, lambda r, s: s + x_ref[r].astype(f32), zero_block
    )
    centre = group_mean(total)

    def spread_step(r, s):
        centred = x_ref[r].astype(f32) - centre
        return s + centred * centred

    spread = group_mean(lax.fori_loop(0, height, spread_step, zero_block))
    rstd = lax.rsqrt(spread + norm_epsilon)

    lane = lax.broadcasted_iota(jnp.int32, (channels, width), 1)
    zero_bf = jnp.zeros((channels, width), bf16)
    act3[0:channels, 0:width] = zero_bf
    act3[2 * channels : 3 * channels, (height - 1) * width : height * width] = zero_bf
    cot3[3 * channels :, :] = jnp.zeros((cot3.shape[0] - 3 * channels, cot3.shape[1]), bf16)

    loads[3].wait()
    bias_total = zero_block
    for r in range(height):
        normed = (x_ref[r].astype(f32) - centre) * rstd
        pre = normed * gain + shift
        sig = 1.0 / (1.0 + jnp.exp(-pre))
        act = (pre * sig).astype(bf16)
        normed_s[r] = normed
        dact_s[r] = sig * (1.0 + pre * (1.0 - sig))
        for i in range(3):
            dest = r - i + 1
            if 0 <= dest < height:
                act3[i * channels : (i + 1) * channels, dest * width : (dest + 1) * width] = act
        cot = cot_ref[r].astype(f32)
        bias_total = bias_total + cot
        place = slice(r * width, (r + 1) * width)
        ahead = jnp.where(lane < width - 1, pltpu.roll(cot, width - 1, axis=1), 0.0)
        behind = jnp.where(lane > 0, pltpu.roll(cot, 1, axis=1), 0.0)
        cot3[0:channels, place] = ahead.astype(bf16)
        cot3[channels : 2 * channels, place] = cot_ref[r]
        cot3[2 * channels : 3 * channels, place] = behind.astype(bf16)

    def kernel_step(n, carry):
        start = pl.multiple_of(n * 256, 256)
        block = lax.dot_general(
            act3[...],
            cot3[pl.ds(start, 256), :],
            (((1,), (1,)), ((), ())),
            preferred_element_type=f32,
        )
        kgrad[2 * n] = block[:, :LANES]
        kgrad[2 * n + 1] = block[:, LANES:]
        return carry

    lax.fori_loop(0, cot3.shape[0] // 256, kernel_step, 0)

    half = channels // 2
    low = lower_half((half, LANES))
    flat_rows = flat.shape[0]
    for i in range(3):
        for j in range(3):
            first = (j * channels) // LANES
            even = [kgrad[first + b, pl.ds(i * channels, half, stride=2), :] for b in range(3)]
            odd = [kgrad[first + b, pl.ds(i * channels + 1, half, stride=2), :] for b in range(3)]
            if j == 1:
                even_r = [swap_halves(e) for e in even]
                pieces = [
                    jnp.where(low, even_r[0], even_r[1]),
                    jnp.where(low, even_r[1], even_r[2]),
                    jnp.where(low, even_r[2], odd[0]),
                    odd[1],
                    odd[2],
                ]
            else:
                odd_r = [swap_halves(o) for o in odd]
                pieces = [
                    even[0],
                    even[1],
                    jnp.where(low, even[2], odd_r[0]),
                    jnp.where(low, odd_r[0], odd_r[1]),
                    jnp.where(low, odd_r[1], odd_r[2]),
                ]
            base = (3 * i + j) * (channels * channels // LANES)
            for b in range(5):
                flat[pl.ds(base + b, half, stride=5), :] = pieces[b]

    used = 9 * channels * channels // LANES
    flat[used:flat_rows, :] = jnp.zeros((flat_rows - used, LANES), f32)

    pl.semaphore_wait(barrier, plane + line - 2)

    for load in loads[5:]:
        load.wait()

    def spread_state(t):
        return copy(state.at[z], state.at[z], ss.at[t], rs.at[t], in_depth(t))

    loop(1, depth, lambda t: spread_state(t).start())

    def chunk(t):
        return (p + t) % plane

    def pair(t):
        q = chunk(t)
        return copy(send1.at[q], recv1.at[q], s1.at[t], r1.at[t], partner)

    def pair_start(t):
        q = chunk(t)
        for k in range(depth):
            row = ((q * depth + k) * 2 + 1 - core) * shard_rows
            send1[q, k] = flat[pl.ds(row, PAD_ROWS), :].astype(bf16)
        pair(t).start()

    loop(1, plane, pair_start)
    pair_start(0)

    loads[4].wait()
    wcat[...] = jnp.zeros_like(wcat)
    for i in range(3):
        for j in range(3):
            wcat[i * channels : (i + 1) * channels, j * channels : (j + 1) * channels] = w_ref[
                3 * i + j
            ]
    gact[...] = jnp.zeros_like(gact)

    def across(t):
        return copy(send2.at[t], recv2.at[t], s2.at[t], r2.at[t], in_plane(t))

    def pair_sum(q, k):
        row = ((q * depth + k) * 2 + core) * shard_rows
        return flat[pl.ds(row, PAD_ROWS), :] + recv1[q, k].astype(f32)

    def across_start(t):
        pair(t).wait_recv()
        q = chunk(t)
        for k in range(depth):
            send2[t, k] = pair_sum(q, k).astype(bf16)
        across(t).start()

    loop(1, plane, across_start)

    def back_step(n, carry):
        start = pl.multiple_of(n * 256, 256)
        block = jnp.dot(wcat[...], cot3[:, pl.ds(start, 256)], preferred_element_type=f32)
        for i in range(3):
            for h in range(2):
                gact[2 * n + h + i] += block[
                    i * channels : (i + 1) * channels, h * width : (h + 1) * width
                ]
        return carry

    lax.fori_loop(0, height // 2, back_step, 0)

    def sums_step(r, carry):
        shift_sum, gain_sum = carry
        dpre = gact[r + 1] * dact_s[r]
        gact[r + 1] = dpre
        return shift_sum + dpre, gain_sum + dpre * normed_s[r]

    shift_sum, gain_sum = lax.fori_loop(0, height, sums_step, (zero_block, zero_block))
    mean_grad = group_mean(shift_sum * gain)
    mean_cross = group_mean(gain_sum * gain)

    bias_row = as_row(jnp.sum(bias_total, axis=1, keepdims=True))
    gain_row = as_row(jnp.sum(gain_sum, axis=1, keepdims=True))
    shift_row = as_row(jnp.sum(shift_sum, axis=1, keepdims=True))
    tail_shard = used // shard_rows
    tail_place, tail_spot = tail_shard // line, tail_shard % line
    tail_z, tail_core = tail_spot // 2, tail_spot % 2
    tail_row = used - tail_shard * shard_rows
    owns_tail = core == tail_core
    tails[0] = jnp.zeros(tails.shape[1:], f32)
    tails[0, 0:1, :] = bias_row[:, 0:128]
    tails[0, 1:2, :] = bias_row[:, 128:256]
    tails[0, 2:3, 0:64] = bias_row[:, 256:320]
    tails[0, 2:3, 64:128] = gain_row[:, 0:64]
    tails[0, 3:4, :] = gain_row[:, 64:192]
    tails[0, 4:5, :] = gain_row[:, 192:320]
    tails[0, 5:6, :] = shift_row[:, 0:128]
    tails[0, 6:7, :] = shift_row[:, 128:256]
    tails[0, 7:8, 0:64] = shift_row[:, 256:320]

    tail_pair = copy(tails.at[0], tails.at[plane + 1], st.at[0], rt.at[0], partner)

    @pl.when(core != tail_core)
    def _():
        tail_pair.start()

    def tail_across(t):
        return copy(
            tails.at[plane], tails.at[t], st.at[1], rt.at[t], device(tail_place, spot)
        )

    tail_t = (tail_place + plane - p) % plane

    @pl.when(owns_tail)
    def _():
        tail_pair.wait_recv()
        tails[plane] = tails[0] + tails[plane + 1]

        @pl.when(p != tail_place)
        def _():
            tail_across(tail_t).start()

    def input_step(r, carry):
        slope = gact[r + 1] * gain
        gin_ref[r] = (rstd * (slope - mean_grad - normed_s[r] * mean_cross)).astype(bf16)
        return carry

    lax.fori_loop(0, height, input_step, 0)

    pair(0).wait_recv()
    for k in range(depth):
        acc[k] = pair_sum(p, k)

    def across_take(t):
        across(t).wait_recv()
        acc[...] += recv2[t].astype(f32)

    loop(1, plane, across_take)

    @pl.when(jnp.logical_and(owns_tail, p == tail_place))
    def _():
        entries = pl.ds(tail_row, 8)
        acc[tail_z, entries] += tails[plane]

        def tail_take(t):
            tail_across(t).wait_recv()
            acc[tail_z, entries] += tails[t]

        loop(1, plane, tail_take)

    def along(t):
        return copy(acc.at[(z + t) % depth], recv3.at[t], s3.at[t], r3.at[t], in_depth(t))

    loop(1, depth, lambda t: along(t).start())
    recv3[0] = acc[z]
    loop(1, depth, lambda t: along(t).wait_recv())
    summed = recv3[0]
    for t in range(1, depth):
        summed = summed + recv3[t]
    live = lax.broadcasted_iota(jnp.int32, summed.shape, 0) < shard_rows
    summed = jnp.where(live, summed, 0.0)

    squares = summed * summed
    norm_line[spot] = squares[0:8] + squares[8:16] + squares[16:24] + squares[24:32]
    gsum[z] = summed

    def line_copy(t):
        mine = norm_line.at[spot]
        return copy(mine, mine, sl.at[t], rl.at[t], in_line(t))

    def line_got(t):
        theirs = norm_line.at[(spot + line - t) % line]
        return copy(theirs, theirs, sl.at[t], rl.at[t], in_line(t))

    def spread_sum(t):
        return copy(gsum.at[z], gsum.at[z], sg.at[t], rg.at[t], in_depth(t))

    def sum_got(t):
        theirs = gsum.at[(z + depth - t) % depth]
        return copy(theirs, theirs, sg.at[t], rg.at[t], in_depth(t))

    def state_got(t):
        theirs = state.at[(z + depth - t) % depth]
        return copy(theirs, theirs, ss.at[t], rs.at[t], in_depth(t))

    loop(1, line, lambda t: line_copy(t).start())
    loop(1, depth, lambda t: spread_sum(t).start())
    loop(1, line, lambda t: line_got(t).wait_recv())
    sumsq = norm_line[0]
    for n in range(1, line):
        sumsq = sumsq + norm_line[n]
    norm_plane[p] = sumsq

    def plane_copy(t):
        mine = norm_plane.at[p]
        return copy(mine, mine, sp.at[t], rp.at[t], in_plane(t))

    def plane_got(t):
        theirs = norm_plane.at[(p + plane - t) % plane]
        return copy(theirs, theirs, sp.at[t], rp.at[t], in_plane(t))

    loop(1, plane, lambda t: plane_copy(t).start())
    loop(1, depth, lambda t: state_got(t).wait_recv())
    loop(1, depth, lambda t: sum_got(t).wait_recv())
    loop(1, plane, lambda t: plane_got(t).wait_recv())
    sumsq = norm_plane[0]
    for n in range(1, plane):
        sumsq = sumsq + norm_plane[n]
    norm_total = jnp.sum(jnp.sum(sumsq, axis=1, keepdims=True), axis=0, keepdims=True)
    clip = jnp.minimum(1.0, clip_limit / (jnp.sqrt(norm_total) + 1e-06))

    def adam(total, master, first, second):
        clipped = clip * total
        new_first = beta_first * first + (1.0 - beta_first) * clipped
        new_second = beta_second * second + (1.0 - beta_second) * clipped * clipped
        step_dir = new_first / correct_first / (
            jnp.sqrt(new_second / correct_second) + adam_epsilon
        )
        return master - learn_rate * (step_dir + weight_decay * master), new_first, new_second

    x_size, w_size = gath.shape[1], gath.shape[2]
    xi, wi = p // w_size, p % w_size
    for k in range(depth):
        updated, _, _ = adam(gsum[k], state[k, 0], state[k, 1], state[k, 2])
        gath[core, xi, wi, k] = updated.astype(bf16)

    half_depth = depth // 2

    def back_x(t):
        return (xi + x_size - t) % x_size

    def back_w(t):
        return (wi + w_size - t) % w_size

    def part(c, h, tx, tw):
        return gath.at[c, back_x(tx), back_w(tw), pl.ds(h * half_depth, half_depth)]

    def slots_x(h, t, tw):
        spots = (h, t, 0) if h == 0 else (h, tw, t)
        return sb.at[spots], rb.at[spots]

    def slots_w(h, t, tx):
        spots = (h, t, 0) if h == 1 else (h, tx, t)
        return sb.at[spots], rb.at[spots]

    def along_x(h, t, tw):
        block = part(core, h, 0, tw)
        target = device(((xi + t) % x_size) * w_size + wi, spot)
        return copy(block, block, *slots_x(h, t, tw), target)

    def along_w(h, t, tx):
        block = part(core, h, tx, 0)
        target = device(xi * w_size + (wi + t) % w_size, spot)
        return copy(block, block, *slots_w(h, t, tx), target)

    def got_x(h, t, tw):
        block = part(core, h, t, tw)
        target = device(((xi + t) % x_size) * w_size + wi, spot)
        return copy(block, block, *slots_x(h, t, tw), target)

    def got_w(h, t, tx):
        block = part(core, h, tx, t)
        target = device(xi * w_size + (wi + t) % w_size, spot)
        return copy(block, block, *slots_w(h, t, tx), target)

    def gather_core(h, tx, tw):
        block = part(core, h, tx, tw)
        return copy(block, block, sc.at[h, tx, tw], rc.at[h, tx, tw], partner)

    def got_core(h, tx, tw):
        block = part(1 - core, h, tx, tw)
        return copy(block, block, sc.at[h, tx, tw], rc.at[h, tx, tw], partner)

    def to_flat(c, h, tx, tw):
        sx, sw = back_x(tx), back_w(tw)
        for k in range(half_depth):
            spot_k = (h * half_depth + k) * 2 + c
            row = ((sx * w_size + sw) * line + spot_k) * shard_rows
            block = gath[c, sx, sw, h * half_depth + k].astype(f32)
            flat[pl.ds(row, shard_rows), :] = block[0:shard_rows]

    loop(1, x_size, lambda t: along_x(0, t, 0).start())
    loop(1, w_size, lambda t: along_w(1, t, 0).start())
    loop(1, w_size, lambda t: along_w(0, t, 0).start())
    loop(1, x_size, lambda t: along_x(1, t, 0).start())
    gather_core(0, 0, 0).start()
    gather_core(1, 0, 0).start()
    to_flat(core, 0, 0, 0)
    to_flat(core, 1, 0, 0)
    results = adam(gsum[z], state[z, 0], state[z, 1], state[z, 2])
    for ref, value in zip((new_master_ref, new_first_ref, new_second_ref), results):
        ref[...] = value[0:shard_rows]

    def first_x(t):
        got_x(0, t, 0).wait_recv()
        loop(1, w_size, lambda s: along_w(0, s, t).start())
        gather_core(0, t, 0).start()

    def first_w(t):
        got_w(1, t, 0).wait_recv()
        loop(1, x_size, lambda s: along_x(1, s, t).start())
        gather_core(1, 0, t).start()

    def first(t):
        first_x(t)
        first_w(t)

    loop(1, x_size, first)

    def first_flat(t):
        to_flat(core, 0, t, 0)
        to_flat(core, 1, 0, t)

    loop(1, x_size, first_flat)

    def second(n):
        a, b = n // (w_size - 1), n % (w_size - 1) + 1
        got_w(0, b, a).wait_recv()
        gather_core(0, a, b).start()
        got_x(1, b, a).wait_recv()
        gather_core(1, b, a).start()
        to_flat(core, 0, a, b)
        to_flat(core, 1, b, a)

    loop(0, x_size * (w_size - 1), second)

    def third(n):
        a, b = n // w_size, n % w_size
        got_core(0, a, b).wait_recv()
        to_flat(1 - core, 0, a, b)
        got_core(1, b, a).wait_recv()
        to_flat(1 - core, 1, b, a)

    loop(0, x_size * w_size, third)

    five = channels * channels // LANES

    def rows_step(n):
        piece = [flat[pl.ds(n * five + b, half, stride=5), :] for b in range(5)]
        turned = [swap_halves(piece[b]) for b in range(2, 5)]
        even = [piece[0], piece[1], piece[2]]
        odd = [
            jnp.where(low, turned[0], turned[1]),
            jnp.where(low, turned[1], turned[2]),
            turned[2],
        ]
        for b in range(3):
            rows[b, pl.ds(0, half, stride=2), :] = even[b]
            rows[b, pl.ds(1, half, stride=2), :] = odd[b]
        place = pl.ds(pl.multiple_of(n * channels, channels), channels)
        wout[place, 0:128] = rows[0].astype(bf16)
        wout[place, 128:256] = rows[1].astype(bf16)
        wout[place, 256:channels] = rows[2, :, 0 : channels - 256].astype(bf16)

    loop(0, 9, rows_step)
    tail_ref[...] = flat[used : used + 8, :]

    loop(0, plane, lambda t: pair(t).wait_send())
    loop(1, plane, lambda t: across(t).wait_send())
    loop(1, depth, lambda t: along(t).wait_send())
    loop(1, line, lambda t: line_copy(t).wait_send())
    loop(1, plane, lambda t: plane_copy(t).wait_send())
    loop(1, depth, lambda t: spread_state(t).wait_send())
    loop(1, depth, lambda t: spread_sum(t).wait_send())

    @pl.when(core != tail_core)
    def _():
        tail_pair.wait_send()

    @pl.when(jnp.logical_and(owns_tail, p != tail_place))
    def _():
        tail_across(tail_t).wait_send()

    def all_sent(n):
        a, b = n // w_size, n % w_size
        gather_core(0, a, b).wait_send()
        gather_core(1, a, b).wait_send()

        @pl.when(b > 0)
        def _():
            along_w(0, b, a).wait_send()
            along_x(1, b, a).wait_send()

    loop(0, x_size * w_size, all_sent)
    loop(1, x_size, lambda t: along_x(0, t, 0).wait_send())
    loop(1, w_size, lambda t: along_w(1, t, 0).wait_send())


def run_layer(x, cot, weight, gain, shift, master, first, second, plane, depth, split_rows):
    f32, bf16 = jnp.float32, jnp.bfloat16
    height, channels, width = x.shape
    line = 2 * depth
    wide = -(-3 * channels // 256) * 256
    flat_rows = plane * line * master.shape[0] + PAD_ROWS
    shard = pltpu.VMEM(master.shape, f32)
    weight = weight.reshape(9, channels, channels)
    ring_w = 2 * split_rows
    ring_x = plane // ring_w
    gathered = (2, ring_x, ring_w, depth, PAD_ROWS, LANES)
    part = (plane, depth, PAD_ROWS, LANES)
    dma = lambda *n: pltpu.SemaphoreType.DMA(n)
    vmem, hbm = pl.BlockSpec(memory_space=pltpu.VMEM), pl.BlockSpec(memory_space=pltpu.HBM)
    operands = (x, cot, weight, gain, shift, master, first, second)
    operands = [pltpu.with_memory_space_constraint(a, pltpu.HBM) for a in operands]
    return pl.pallas_call(
        functools.partial(layer_kernel, split_rows, plane, depth),
        out_shape=(
            pltpu.VMEM(x.shape, bf16),
            pltpu.VMEM((9 * channels, channels), bf16),
            pltpu.VMEM((8, LANES), f32),
            shard,
            shard,
            shard,
        ),
        in_specs=[hbm] * 8,
        out_specs=[vmem] * 6,
        scratch_shapes=[
            pltpu.VMEM(x.shape, bf16),
            pltpu.VMEM(x.shape, bf16),
            pltpu.VMEM(weight.shape, bf16),
            pltpu.VMEM(gain.shape, f32),
            pltpu.VMEM(shift.shape, f32),
            pltpu.VMEM(gathered, bf16),
            pltpu.VMEM((3, channels, LANES), f32),
            pltpu.VMEM((3 * channels, height * width), bf16),
            pltpu.VMEM((wide, height * width), bf16),
            pltpu.VMEM((3 * channels, wide), bf16),
            pltpu.VMEM((wide // LANES, 3 * channels, LANES), f32),
            pltpu.VMEM((flat_rows, LANES), f32),
            pltpu.VMEM((height, channels, width), f32),
            pltpu.VMEM((height, channels, width), f32),
            pltpu.VMEM((height + 2, channels, width), f32),
            pltpu.VMEM(part, bf16),
            pltpu.VMEM(part, bf16),
            pltpu.VMEM(part, bf16),
            pltpu.VMEM(part, bf16),
            pltpu.VMEM((depth, PAD_ROWS, LANES), f32),
            pltpu.VMEM((depth, PAD_ROWS, LANES), f32),
            pltpu.VMEM((depth, 3, PAD_ROWS, LANES), f32),
            pltpu.VMEM((depth, PAD_ROWS, LANES), f32),
            pltpu.VMEM((line, 8, LANES), f32),
            pltpu.VMEM((plane, 8, LANES), f32),
            pltpu.VMEM((plane + 2, 8, LANES), f32),
            dma(8),
        ]
        + [dma(n) for n in (plane, plane, plane, plane, depth, depth, line, line)]
        + [dma(n) for n in (plane, plane, depth, depth, depth, depth)]
        + [dma(2, ring_x, ring_w)] * 4
        + [dma(2), dma(plane)],
        compiler_params=pltpu.CompilerParams(
            collective_id=0, has_side_effects=True, vmem_limit_bytes=VMEM_LIMIT
        ),
    )(*operands)


def finish_kernel(tail_ref, *refs):
    count = 5
    sources, targets = refs[:count], refs[count : 2 * count]
    rows_out, sems = refs[2 * count : 2 * count + 3], refs[-1]
    copies = [
        pltpu.make_async_copy(sources[n], targets[n], sems.at[n]) for n in range(count)
    ]
    for each in copies:
        each.start()
    tail = [tail_ref[b : b + 1, :] for b in range(8)]
    rows = (
        [tail[0], tail[1], tail[2][:, 0:64]],
        [tail[2][:, 64:128], tail[3], tail[4]],
        [tail[5], tail[6], tail[7][:, 0:64]],
    )
    for ref, row in zip(rows_out, rows):
        ref[...] = jnp.concatenate(row, axis=1).astype(ref.dtype).reshape(ref.shape)
    for each in copies:
        each.wait()


def finish(tail, results, channels):
    row = jax.ShapeDtypeStruct((channels,), jnp.bfloat16)
    vmem, anywhere = pl.BlockSpec(memory_space=pltpu.VMEM), pl.BlockSpec(memory_space=pl.ANY)
    pinned = [pltpu.with_memory_space_constraint(r, pltpu.VMEM) for r in (tail, *results)]
    return pl.pallas_call(
        finish_kernel,
        out_shape=tuple(jax.ShapeDtypeStruct(r.shape, r.dtype) for r in results) + (row,) * 3,
        in_specs=[vmem] * 6,
        out_specs=[anywhere] * 5 + [vmem] * 3,
        scratch_shapes=[pltpu.SemaphoreType.DMA((5,))],
        compiler_params=pltpu.CompilerParams(vmem_limit_bytes=4 * 1024 * 1024),
    )(*pinned)


def on_device(latents, cotangent, weight, gain, shift, master, first_moment, second_moment):
    groups, owners = lax.axis_size("grp"), lax.axis_size("dp")
    channels = weight.shape[2]
    split_rows = 2
    depth = owners // (2 * split_rows)
    plane = groups * split_rows
    shard_rows = master.shape[0] // LANES
    x = jnp.transpose(latents[0], (0, 2, 1))
    cot = jnp.transpose(cotangent[0], (0, 2, 1))
    shaped = [a.reshape(shard_rows, LANES) for a in (master, first_moment, second_moment)]
    grad_in, new_weight, tail, *state = run_layer(
        x, cot, weight, gain, shift, *shaped, plane, depth, split_rows
    )
    results = finish(tail, (grad_in, new_weight, *state), channels)
    grad_in, new_weight, new_master, new_first, new_second = results[:5]
    new_bias, new_gain, new_shift = results[5:]
    return (
        jnp.transpose(grad_in, (0, 2, 1))[None],
        new_weight.reshape(weight.shape),
        new_bias,
        new_gain,
        new_shift,
        new_master.reshape(-1),
        new_first.reshape(-1),
        new_second.reshape(-1),
    )


def solution(mesh):
    split = ("grp", "dp")
    whole = P(split, None, None, None)
    in_specs = (whole, whole, P(), P(), P(), P(split), P(split), P(split))
    out_specs = (whole, P(), P(), P(), P(), P(split), P(split), P(split))
    return jax.shard_map(
        on_device, mesh=mesh, in_specs=in_specs, out_specs=out_specs, check_vma=False
    )
```

```python
import functools

import jax
import jax.numpy as jnp
from jax import lax
from jax.experimental import pallas as pl
from jax.experimental.pallas import tpu as pltpu
from jax.sharding import PartitionSpec as P

GROUPS = 32
LANES = 128
PAD_ROWS = 32

norm_epsilon = 1e-05
beta_first = 0.9
beta_second = 0.999
adam_epsilon = 1e-08
learn_rate = 0.001
weight_decay = 0.01
clip_limit = 1.0
correct_first = 1.0
correct_second = 0.6323045752290363

MESH = pl.DeviceIdType.MESH
VMEM_LIMIT = 48 * 1024 * 1024


def swap_halves(block):
    return pltpu.roll(block, LANES // 2, axis=1)


def lower_half(shape):
    return lax.broadcasted_iota(jnp.int32, shape, 1) < LANES // 2


def layer_kernel(
    split_rows,
    plane,
    depth,
    x_hbm,
    cot_hbm,
    w_hbm,
    gain_hbm,
    shift_hbm,
    master_hbm,
    first_hbm,
    second_hbm,
    gin_ref,
    wout,
    tail_ref,
    new_master_ref,
    new_first_ref,
    new_second_ref,
    x_ref,
    cot_ref,
    w_ref,
    gain_ref,
    shift_ref,
    gath,
    rows,
    act3,
    cot3,
    wcat,
    kgrad,
    flat,
    normed_s,
    dact_s,
    gact,
    send1,
    recv1,
    send2,
    recv2,
    acc,
    recv3,
    state,
    gsum,
    norm_line,
    norm_plane,
    tails,
    tail_line,
    in_sem,
    s1,
    r1,
    s2,
    r2,
    s3,
    r3,
    sl,
    rl,
    sp,
    rp,
    ss,
    rs,
    sg,
    rg,
    sb,
    rb,
    sc,
    rc,
    st,
    rt,
):
    f32, bf16 = jnp.float32, jnp.bfloat16
    line = 2 * depth
    grp, dp = lax.axis_index("grp"), lax.axis_index("dp")
    p = grp * split_rows + dp // line
    spot = dp % line
    z, core = spot // 2, spot % 2
    shard_rows = master_hbm.shape[0]

    def device(p_, spot_):
        return (p_ // split_rows, (p_ % split_rows) * line + spot_)

    def in_plane(t):
        return device((p + t) % plane, spot)

    def in_line(t):
        return device(p, (spot + t) % line)

    def in_depth(t):
        return device(p, ((z + t) % depth) * 2 + core)

    partner = device(p, z * 2 + 1 - core)

    def copy(src, dst, send, recv, target):
        return pltpu.make_async_remote_copy(
            src_ref=src,
            dst_ref=dst,
            send_sem=send,
            recv_sem=recv,
            device_id=target,
            device_id_type=MESH,
        )

    def loop(lo, hi, body):
        def step(t, carry):
            body(t)
            return carry

        lax.fori_loop(lo, hi, step, 0)

    state[z] = jnp.zeros(state.shape[1:], f32)
    pairs = [(x_hbm, x_ref), (gain_hbm, gain_ref), (shift_hbm, shift_ref)]
    pairs += [(cot_hbm, cot_ref), (w_hbm, w_ref)]
    for n, ref in enumerate((master_hbm, first_hbm, second_hbm)):
        pairs.append((ref, state.at[z, n, pl.ds(0, shard_rows)]))
    loads = [
        pltpu.make_async_copy(source, target, in_sem.at[n])
        for n, (source, target) in enumerate(pairs)
    ]
    for load in loads:
        load.start()

    barrier = pltpu.get_barrier_semaphore()

    def greet(target):
        pl.semaphore_signal(barrier, inc=1, device_id=target, device_id_type=MESH)

    loop(1, plane, lambda t: greet(in_plane(t)))
    loop(1, line, lambda t: greet(in_line(t)))

    height, channels, width = x_ref.shape
    count = height * width * (channels // GROUPS)

    row_id = lax.broadcasted_iota(jnp.int32, (channels, channels), 0)
    col_id = lax.broadcasted_iota(jnp.int32, (channels, channels), 1)
    eye = (row_id == col_id).astype(f32)
    per = 1.0 / (channels // GROUPS)
    row_group = jnp.floor((row_id.astype(f32) + 0.5) * per)
    col_group = jnp.floor((col_id.astype(f32) + 0.5) * per)
    same_group = (row_group == col_group).astype(f32)

    def group_mean(block):
        mixed = jnp.dot(
            same_group, block, precision=lax.Precision.HIGHEST, preferred_element_type=f32
        )
        return jnp.sum(mixed, axis=1, keepdims=True) * (1.0 / count)

    def as_column(row):
        return jnp.sum(eye * row, axis=1, keepdims=True)

    def as_row(column):
        return jnp.sum(eye * column, axis=0, keepdims=True)

    for load in loads[:3]:
        load.wait()
    gain = as_column(gain_ref[...].reshape(1, channels))
    shift = as_column(shift_ref[...].reshape(1, channels))

    zero_block = jnp.zeros((channels, width), f32)
    total = lax.fori_loop(
        0, height, lambda r, s: s + x_ref[r].astype(f32), zero_block
    )
    centre = group_mean(total)

    def spread_step(r, s):
        centred = x_ref[r].astype(f32) - centre
        return s + centred * centred

    spread = group_mean(lax.fori_loop(0, height, spread_step, zero_block))
    rstd = lax.rsqrt(spread + norm_epsilon)

    lane = lax.broadcasted_iota(jnp.int32, (channels, width), 1)
    zero_bf = jnp.zeros((channels, width), bf16)
    act3[0:channels, 0:width] = zero_bf
    act3[2 * channels : 3 * channels, (height - 1) * width : height * width] = zero_bf
    cot3[3 * channels :, :] = jnp.zeros((cot3.shape[0] - 3 * channels, cot3.shape[1]), bf16)

    loads[3].wait()
    bias_total = zero_block
    for r in range(height):
        normed = (x_ref[r].astype(f32) - centre) * rstd
        pre = normed * gain + shift
        sig = 1.0 / (1.0 + jnp.exp(-pre))
        act = (pre * sig).astype(bf16)
        normed_s[r] = normed
        dact_s[r] = sig * (1.0 + pre * (1.0 - sig))
        for i in range(3):
            dest = r - i + 1
            if 0 <= dest < height:
                act3[i * channels : (i + 1) * channels, dest * width : (dest + 1) * width] = act
        cot = cot_ref[r].astype(f32)
        bias_total = bias_total + cot
        place = slice(r * width, (r + 1) * width)
        ahead = jnp.where(lane < width - 1, pltpu.roll(cot, width - 1, axis=1), 0.0)
        behind = jnp.where(lane > 0, pltpu.roll(cot, 1, axis=1), 0.0)
        cot3[0:channels, place] = ahead.astype(bf16)
        cot3[channels : 2 * channels, place] = cot_ref[r]
        cot3[2 * channels : 3 * channels, place] = behind.astype(bf16)

    for n in range(cot3.shape[0] // 256):
        block = lax.dot_general(
            act3[...],
            cot3[n * 256 : (n + 1) * 256, :],
            (((1,), (1,)), ((), ())),
            preferred_element_type=f32,
        )
        kgrad[2 * n] = block[:, :LANES]
        kgrad[2 * n + 1] = block[:, LANES:]

    half = channels // 2
    low = lower_half((half, LANES))
    flat_rows = flat.shape[0]
    for i in range(3):
        for j in range(3):
            first = (j * channels) // LANES
            even = [kgrad[first + b, pl.ds(i * channels, half, stride=2), :] for b in range(3)]
            odd = [kgrad[first + b, pl.ds(i * channels + 1, half, stride=2), :] for b in range(3)]
            if j == 1:
                even_r = [swap_halves(e) for e in even]
                pieces = [
                    jnp.where(low, even_r[0], even_r[1]),
                    jnp.where(low, even_r[1], even_r[2]),
                    jnp.where(low, even_r[2], odd[0]),
                    odd[1],
                    odd[2],
                ]
            else:
                odd_r = [swap_halves(o) for o in odd]
                pieces = [
                    even[0],
                    even[1],
                    jnp.where(low, even[2], odd_r[0]),
                    jnp.where(low, odd_r[0], odd_r[1]),
                    jnp.where(low, odd_r[1], odd_r[2]),
                ]
            base = (3 * i + j) * (channels * channels // LANES)
            for b in range(5):
                flat[pl.ds(base + b, half, stride=5), :] = pieces[b]

    used = 9 * channels * channels // LANES
    flat[used:flat_rows, :] = jnp.zeros((flat_rows - used, LANES), f32)

    pl.semaphore_wait(barrier, plane + line - 2)

    def far_first(n):
        return jnp.where(n == 0, 2, jnp.where(n == 1, 1, jnp.where(n == 2, 3, 0)))

    x_size, w_size = gath.shape[1], gath.shape[2]
    xi, wi = p // w_size, p % w_size
    yi = (wi % 2) * 2 + wi // 2
    own_t = plane - 1

    def chunk(t):
        x_to = (xi + far_first(t // 4)) % x_size
        y_to = (yi + far_first(t % 4)) % w_size
        return x_to * w_size + (y_to % 2) * 2 + y_to // 2

    def pair(t):
        q = chunk(t)
        return copy(send1.at[q], recv1.at[q], s1.at[t], r1.at[t], partner)

    def pair_start(t):
        q = chunk(t)
        for k in range(depth):
            row = ((q * depth + k) * 2 + 1 - core) * shard_rows
            send1[q, k] = flat[pl.ds(row, PAD_ROWS), :].astype(bf16)
        pair(t).start()

    def across(t):
        return copy(send2.at[t], recv2.at[t], s2.at[t], r2.at[t], device(chunk(t), spot))

    def pair_sum(q, k):
        row = ((q * depth + k) * 2 + core) * shard_rows
        return flat[pl.ds(row, PAD_ROWS), :] + recv1[q, k].astype(f32)

    def across_start(t):
        pair(t).wait_recv()
        q = chunk(t)
        for k in range(depth):
            send2[t, k] = pair_sum(q, k).astype(bf16)
        across(t).start()

    lead = 3
    loop(0, lead, pair_start)

    def both(t):
        pair_start(t + lead)
        across_start(t)

    loop(0, plane - lead, both)
    loop(plane - lead, own_t, across_start)

    for load in loads[5:]:
        load.wait()

    def spread_state(t):
        return copy(state.at[z], state.at[z], ss.at[t], rs.at[t], in_depth(t))

    loop(1, depth, lambda t: spread_state(t).start())

    loads[4].wait()
    wcat[...] = jnp.zeros_like(wcat)
    for i in range(3):
        for j in range(3):
            wcat[i * channels : (i + 1) * channels, j * channels : (j + 1) * channels] = w_ref[
                3 * i + j
            ]
    gact[...] = jnp.zeros_like(gact)

    def back_step(n, carry):
        start = pl.multiple_of(n * 512, 512)
        block = jnp.dot(wcat[...], cot3[:, pl.ds(start, 512)], preferred_element_type=f32)
        for i in range(3):
            for h in range(4):
                gact[4 * n + h + i] += block[
                    i * channels : (i + 1) * channels, h * width : (h + 1) * width
                ]
        return carry

    lax.fori_loop(0, height // 4, back_step, 0)

    def sums_step(r, carry):
        shift_sum, gain_sum = carry
        dpre = gact[r + 1] * dact_s[r]
        gact[r + 1] = dpre
        return shift_sum + dpre, gain_sum + dpre * normed_s[r]

    shift_sum, gain_sum = lax.fori_loop(0, height, sums_step, (zero_block, zero_block))
    mean_grad = group_mean(shift_sum * gain)
    mean_cross = group_mean(gain_sum * gain)

    bias_row = as_row(jnp.sum(bias_total, axis=1, keepdims=True))
    gain_row = as_row(jnp.sum(gain_sum, axis=1, keepdims=True))
    shift_row = as_row(jnp.sum(shift_sum, axis=1, keepdims=True))
    tail_shard = used // shard_rows
    tail_place, tail_spot = tail_shard // line, tail_shard % line
    tail_z, tail_core = tail_spot // 2, tail_spot % 2
    tail_row = used - tail_shard * shard_rows
    owns_tail = core == tail_core
    tails[0] = jnp.zeros(tails.shape[1:], f32)
    tails[0, 0:1, :] = bias_row[:, 0:128]
    tails[0, 1:2, :] = bias_row[:, 128:256]
    tails[0, 2:3, 0:64] = bias_row[:, 256:320]
    tails[0, 2:3, 64:128] = gain_row[:, 0:64]
    tails[0, 3:4, :] = gain_row[:, 64:192]
    tails[0, 4:5, :] = gain_row[:, 192:320]
    tails[0, 5:6, :] = shift_row[:, 0:128]
    tails[0, 6:7, :] = shift_row[:, 128:256]
    tails[0, 7:8, 0:64] = shift_row[:, 256:320]

    tail_pair = copy(tails.at[0], tails.at[plane + 1], st.at[0], rt.at[0], partner)

    @pl.when(core != tail_core)
    def _():
        tail_pair.start()

    def tail_across(t):
        return copy(
            tails.at[plane], tails.at[t], st.at[1], rt.at[t], device(tail_place, spot)
        )

    tail_t = (tail_place + plane - p) % plane

    @pl.when(owns_tail)
    def _():
        tail_pair.wait_recv()
        tails[plane] = tails[0] + tails[plane + 1]

        @pl.when(p != tail_place)
        def _():
            tail_across(tail_t).start()

    def input_step(r, carry):
        slope = gact[r + 1] * gain
        gin_ref[r] = (rstd * (slope - mean_grad - normed_s[r] * mean_cross)).astype(bf16)
        return carry

    lax.fori_loop(0, height, input_step, 0)

    pair(own_t).wait_recv()
    for k in range(depth):
        acc[k] = pair_sum(p, k)

    def across_take(t):
        across(t).wait_recv()
        acc[...] += recv2[t].astype(f32)

    loop(0, own_t, across_take)

    def along(t):
        return copy(acc.at[(z + t) % depth], recv3.at[t], s3.at[t], r3.at[t], in_depth(t))

    loop(1, depth, lambda t: along(t).start())
    recv3[0] = acc[z]
    at_tail = jnp.logical_and(owns_tail, p == tail_place)

    def tail_along(t):
        return copy(tails.at[0], tail_line.at[t], st.at[2], rt.at[plane + t], device(p, tail_spot))

    tail_zt = (tail_z + depth - z) % depth

    @pl.when(at_tail)
    def _():
        def tail_take(t):
            tail_across(t).wait_recv()
            tails[plane] += tails[t]

        loop(1, plane, tail_take)
        tails[0] = tails[plane]

        @pl.when(z != tail_z)
        def _():
            tail_along(tail_zt).start()

    loop(1, depth, lambda t: along(t).wait_recv())

    @pl.when(jnp.logical_and(at_tail, z == tail_z))
    def _():
        entries = pl.ds(tail_row, 8)
        recv3[0, entries] += tails[0]

        def tail_sum(t):
            tail_along(t).wait_recv()
            recv3[0, entries] += tail_line[t]

        loop(1, depth, tail_sum)

    summed = recv3[0]
    for t in range(1, depth):
        summed = summed + recv3[t]
    live = lax.broadcasted_iota(jnp.int32, summed.shape, 0) < shard_rows
    summed = jnp.where(live, summed, 0.0)

    squares = summed * summed
    norm_line[spot] = squares[0:8] + squares[8:16] + squares[16:24] + squares[24:32]
    gsum[z] = summed

    def line_copy(t):
        mine = norm_line.at[spot]
        return copy(mine, mine, sl.at[t], rl.at[t], in_line(t))

    def line_got(t):
        theirs = norm_line.at[(spot + line - t) % line]
        return copy(theirs, theirs, sl.at[t], rl.at[t], in_line(t))

    def spread_sum(t):
        return copy(gsum.at[z], gsum.at[z], sg.at[t], rg.at[t], in_depth(t))

    def sum_got(t):
        theirs = gsum.at[(z + depth - t) % depth]
        return copy(theirs, theirs, sg.at[t], rg.at[t], in_depth(t))

    def state_got(t):
        theirs = state.at[(z + depth - t) % depth]
        return copy(theirs, theirs, ss.at[t], rs.at[t], in_depth(t))

    loop(1, line, lambda t: line_copy(t).start())
    loop(1, depth, lambda t: spread_sum(t).start())
    loop(1, line, lambda t: line_got(t).wait_recv())
    sumsq = norm_line[0]
    for n in range(1, line):
        sumsq = sumsq + norm_line[n]
    norm_plane[p] = sumsq

    def plane_copy(t):
        mine = norm_plane.at[p]
        return copy(mine, mine, sp.at[t], rp.at[t], in_plane(t))

    def plane_got(t):
        theirs = norm_plane.at[(p + plane - t) % plane]
        return copy(theirs, theirs, sp.at[t], rp.at[t], in_plane(t))

    loop(1, plane, lambda t: plane_copy(t).start())
    loop(1, depth, lambda t: state_got(t).wait_recv())
    loop(1, depth, lambda t: sum_got(t).wait_recv())
    loop(1, plane, lambda t: plane_got(t).wait_recv())
    sumsq = norm_plane[0]
    for n in range(1, plane):
        sumsq = sumsq + norm_plane[n]
    norm_total = jnp.sum(jnp.sum(sumsq, axis=1, keepdims=True), axis=0, keepdims=True)
    clip = jnp.minimum(1.0, clip_limit / (jnp.sqrt(norm_total) + 1e-06))

    def adam(total, master, first, second):
        clipped = clip * total
        new_first = beta_first * first + (1.0 - beta_first) * clipped
        new_second = beta_second * second + (1.0 - beta_second) * clipped * clipped
        step_dir = new_first / correct_first / (
            jnp.sqrt(new_second / correct_second) + adam_epsilon
        )
        return master - learn_rate * (step_dir + weight_decay * master), new_first, new_second

    for k in range(depth):
        updated, _, _ = adam(gsum[k], state[k, 0], state[k, 1], state[k, 2])
        gath[core, xi, wi, k] = updated.astype(bf16)

    half_depth = depth // 2

    def back_x(t):
        return (xi + x_size - t) % x_size

    def back_w(t):
        return (wi + w_size - t) % w_size

    def part(c, h, tx, tw):
        return gath.at[c, back_x(tx), back_w(tw), pl.ds(h * half_depth, half_depth)]

    def slots_x(h, t, tw):
        spots = (h, t, 0) if h == 0 else (h, tw, t)
        return sb.at[spots], rb.at[spots]

    def slots_w(h, t, tx):
        spots = (h, t, 0) if h == 1 else (h, tx, t)
        return sb.at[spots], rb.at[spots]

    def along_x(h, t, tw):
        block = part(core, h, 0, tw)
        target = device(((xi + t) % x_size) * w_size + wi, spot)
        return copy(block, block, *slots_x(h, t, tw), target)

    def along_w(h, t, tx):
        block = part(core, h, tx, 0)
        target = device(xi * w_size + (wi + t) % w_size, spot)
        return copy(block, block, *slots_w(h, t, tx), target)

    def got_x(h, t, tw):
        block = part(core, h, t, tw)
        target = device(((xi + t) % x_size) * w_size + wi, spot)
        return copy(block, block, *slots_x(h, t, tw), target)

    def got_w(h, t, tx):
        block = part(core, h, tx, t)
        target = device(xi * w_size + (wi + t) % w_size, spot)
        return copy(block, block, *slots_w(h, t, tx), target)

    def gather_core(h, tx, tw):
        block = part(core, h, tx, tw)
        return copy(block, block, sc.at[h, tx, tw], rc.at[h, tx, tw], partner)

    def got_core(h, tx, tw):
        block = part(1 - core, h, tx, tw)
        return copy(block, block, sc.at[h, tx, tw], rc.at[h, tx, tw], partner)

    def to_flat(c, h, tx, tw):
        sx, sw = back_x(tx), back_w(tw)
        for k in range(half_depth):
            spot_k = (h * half_depth + k) * 2 + c
            row = ((sx * w_size + sw) * line + spot_k) * shard_rows
            block = gath[c, sx, sw, h * half_depth + k].astype(f32)
            flat[pl.ds(row, shard_rows), :] = block[0:shard_rows]

    loop(1, x_size, lambda t: along_x(0, t, 0).start())
    loop(1, w_size, lambda t: along_w(1, t, 0).start())
    loop(1, w_size, lambda t: along_w(0, t, 0).start())
    loop(1, x_size, lambda t: along_x(1, t, 0).start())
    gather_core(0, 0, 0).start()
    gather_core(1, 0, 0).start()
    to_flat(core, 0, 0, 0)
    to_flat(core, 1, 0, 0)
    results = adam(gsum[z], state[z, 0], state[z, 1], state[z, 2])
    for ref, value in zip((new_master_ref, new_first_ref, new_second_ref), results):
        ref[...] = value[0:shard_rows]

    def first_x(t):
        got_x(0, t, 0).wait_recv()
        loop(1, w_size, lambda s: along_w(0, s, t).start())
        gather_core(0, t, 0).start()

    def first_w(t):
        got_w(1, t, 0).wait_recv()
        loop(1, x_size, lambda s: along_x(1, s, t).start())
        gather_core(1, 0, t).start()

    def first(t):
        first_x(t)
        first_w(t)

    loop(1, x_size, first)

    def first_flat(t):
        to_flat(core, 0, t, 0)
        to_flat(core, 1, 0, t)

    loop(1, x_size, first_flat)

    def second(n):
        a, b = n // (w_size - 1), n % (w_size - 1) + 1
        got_w(0, b, a).wait_recv()
        gather_core(0, a, b).start()
        got_x(1, b, a).wait_recv()
        gather_core(1, b, a).start()
        to_flat(core, 0, a, b)
        to_flat(core, 1, b, a)

    loop(0, x_size * (w_size - 1), second)

    def third(n):
        a, b = n // w_size, n % w_size
        got_core(0, a, b).wait_recv()
        to_flat(1 - core, 0, a, b)
        got_core(1, b, a).wait_recv()
        to_flat(1 - core, 1, b, a)

    loop(0, x_size * w_size, third)

    five = channels * channels // LANES

    def rows_step(n):
        piece = [flat[pl.ds(n * five + b, half, stride=5), :] for b in range(5)]
        turned = [swap_halves(piece[b]) for b in range(2, 5)]
        even = [piece[0], piece[1], piece[2]]
        odd = [
            jnp.where(low, turned[0], turned[1]),
            jnp.where(low, turned[1], turned[2]),
            turned[2],
        ]
        for b in range(3):
            rows[b, pl.ds(0, half, stride=2), :] = even[b]
            rows[b, pl.ds(1, half, stride=2), :] = odd[b]
        place = pl.ds(pl.multiple_of(n * channels, channels), channels)
        wout[place, 0:128] = rows[0].astype(bf16)
        wout[place, 128:256] = rows[1].astype(bf16)
        wout[place, 256:channels] = rows[2, :, 0 : channels - 256].astype(bf16)

    loop(0, 9, rows_step)
    tail_ref[...] = flat[used : used + 8, :]

    loop(0, plane, lambda t: pair(t).wait_send())
    loop(0, own_t, lambda t: across(t).wait_send())
    loop(1, depth, lambda t: along(t).wait_send())
    loop(1, line, lambda t: line_copy(t).wait_send())
    loop(1, plane, lambda t: plane_copy(t).wait_send())
    loop(1, depth, lambda t: spread_state(t).wait_send())
    loop(1, depth, lambda t: spread_sum(t).wait_send())

    @pl.when(core != tail_core)
    def _():
        tail_pair.wait_send()

    @pl.when(jnp.logical_and(owns_tail, p != tail_place))
    def _():
        tail_across(tail_t).wait_send()

    @pl.when(jnp.logical_and(at_tail, z != tail_z))
    def _():
        tail_along(tail_zt).wait_send()

    def all_sent(n):
        a, b = n // w_size, n % w_size
        gather_core(0, a, b).wait_send()
        gather_core(1, a, b).wait_send()

        @pl.when(b > 0)
        def _():
            along_w(0, b, a).wait_send()
            along_x(1, b, a).wait_send()

    loop(0, x_size * w_size, all_sent)
    loop(1, x_size, lambda t: along_x(0, t, 0).wait_send())
    loop(1, w_size, lambda t: along_w(1, t, 0).wait_send())


def run_layer(x, cot, weight, gain, shift, master, first, second, plane, depth, split_rows):
    f32, bf16 = jnp.float32, jnp.bfloat16
    height, channels, width = x.shape
    line = 2 * depth
    wide = -(-3 * channels // 256) * 256
    flat_rows = plane * line * master.shape[0] + PAD_ROWS
    shard = pltpu.VMEM(master.shape, f32)
    weight = weight.reshape(9, channels, channels)
    ring_w = 2 * split_rows
    ring_x = plane // ring_w
    gathered = (2, ring_x, ring_w, depth, PAD_ROWS, LANES)
    part = (plane, depth, PAD_ROWS, LANES)
    dma = lambda *n: pltpu.SemaphoreType.DMA(n)
    vmem, hbm = pl.BlockSpec(memory_space=pltpu.VMEM), pl.BlockSpec(memory_space=pltpu.HBM)
    operands = (x, cot, weight, gain, shift, master, first, second)
    operands = [pltpu.with_memory_space_constraint(a, pltpu.HBM) for a in operands]
    return pl.pallas_call(
        functools.partial(layer_kernel, split_rows, plane, depth),
        out_shape=(
            pltpu.VMEM(x.shape, bf16),
            pltpu.VMEM((9 * channels, channels), bf16),
            pltpu.VMEM((8, LANES), f32),
            shard,
            shard,
            shard,
        ),
        in_specs=[hbm] * 8,
        out_specs=[vmem] * 6,
        scratch_shapes=[
            pltpu.VMEM(x.shape, bf16),
            pltpu.VMEM(x.shape, bf16),
            pltpu.VMEM(weight.shape, bf16),
            pltpu.VMEM(gain.shape, f32),
            pltpu.VMEM(shift.shape, f32),
            pltpu.VMEM(gathered, bf16),
            pltpu.VMEM((3, channels, LANES), f32),
            pltpu.VMEM((3 * channels, height * width), bf16),
            pltpu.VMEM((wide, height * width), bf16),
            pltpu.VMEM((3 * channels, wide), bf16),
            pltpu.VMEM((wide // LANES, 3 * channels, LANES), f32),
            pltpu.VMEM((flat_rows, LANES), f32),
            pltpu.VMEM((height, channels, width), f32),
            pltpu.VMEM((height, channels, width), f32),
            pltpu.VMEM((height + 2, channels, width), f32),
            pltpu.VMEM(part, bf16),
            pltpu.VMEM(part, bf16),
            pltpu.VMEM(part, bf16),
            pltpu.VMEM(part, bf16),
            pltpu.VMEM((depth, PAD_ROWS, LANES), f32),
            pltpu.VMEM((depth, PAD_ROWS, LANES), f32),
            pltpu.VMEM((depth, 3, PAD_ROWS, LANES), f32),
            pltpu.VMEM((depth, PAD_ROWS, LANES), f32),
            pltpu.VMEM((line, 8, LANES), f32),
            pltpu.VMEM((plane, 8, LANES), f32),
            pltpu.VMEM((plane + 2, 8, LANES), f32),
            pltpu.VMEM((depth, 8, LANES), f32),
            dma(8),
        ]
        + [dma(n) for n in (plane, plane, plane, plane, depth, depth, line, line)]
        + [dma(n) for n in (plane, plane, depth, depth, depth, depth)]
        + [dma(2, ring_x, ring_w)] * 4
        + [dma(3), dma(plane + depth)],
        compiler_params=pltpu.CompilerParams(
            collective_id=0, has_side_effects=True, vmem_limit_bytes=VMEM_LIMIT
        ),
    )(*operands)


def finish_kernel(tail_ref, *refs):
    count = 5
    sources, targets = refs[:count], refs[count : 2 * count]
    rows_out, sems = refs[2 * count : 2 * count + 3], refs[-1]
    copies = [
        pltpu.make_async_copy(sources[n], targets[n], sems.at[n]) for n in range(count)
    ]
    for each in copies:
        each.start()
    tail = [tail_ref[b : b + 1, :] for b in range(8)]
    rows = (
        [tail[0], tail[1], tail[2][:, 0:64]],
        [tail[2][:, 64:128], tail[3], tail[4]],
        [tail[5], tail[6], tail[7][:, 0:64]],
    )
    for ref, row in zip(rows_out, rows):
        ref[...] = jnp.concatenate(row, axis=1).astype(ref.dtype).reshape(ref.shape)
    for each in copies:
        each.wait()


def finish(tail, results, channels):
    row = jax.ShapeDtypeStruct((channels,), jnp.bfloat16)
    vmem, anywhere = pl.BlockSpec(memory_space=pltpu.VMEM), pl.BlockSpec(memory_space=pl.ANY)
    pinned = [pltpu.with_memory_space_constraint(r, pltpu.VMEM) for r in (tail, *results)]
    return pl.pallas_call(
        finish_kernel,
        out_shape=tuple(jax.ShapeDtypeStruct(r.shape, r.dtype) for r in results) + (row,) * 3,
        in_specs=[vmem] * 6,
        out_specs=[anywhere] * 5 + [vmem] * 3,
        scratch_shapes=[pltpu.SemaphoreType.DMA((5,))],
        compiler_params=pltpu.CompilerParams(vmem_limit_bytes=4 * 1024 * 1024),
    )(*pinned)


def on_device(latents, cotangent, weight, gain, shift, master, first_moment, second_moment):
    groups, owners = lax.axis_size("grp"), lax.axis_size("dp")
    channels = weight.shape[2]
    split_rows = 2
    depth = owners // (2 * split_rows)
    plane = groups * split_rows
    shard_rows = master.shape[0] // LANES
    x = jnp.transpose(latents[0], (0, 2, 1))
    cot = jnp.transpose(cotangent[0], (0, 2, 1))
    shaped = [a.reshape(shard_rows, LANES) for a in (master, first_moment, second_moment)]
    grad_in, new_weight, tail, *state = run_layer(
        x, cot, weight, gain, shift, *shaped, plane, depth, split_rows
    )
    results = finish(tail, (grad_in, new_weight, *state), channels)
    grad_in, new_weight, new_master, new_first, new_second = results[:5]
    new_bias, new_gain, new_shift = results[5:]
    return (
        jnp.transpose(grad_in, (0, 2, 1))[None],
        new_weight.reshape(weight.shape),
        new_bias,
        new_gain,
        new_shift,
        new_master.reshape(-1),
        new_first.reshape(-1),
        new_second.reshape(-1),
    )


def solution(mesh):
    split = ("grp", "dp")
    whole = P(split, None, None, None)
    in_specs = (whole, whole, P(), P(), P(), P(split), P(split), P(split))
    out_specs = (whole, P(), P(), P(), P(), P(split), P(split), P(split))
    return jax.shard_map(
        on_device, mesh=mesh, in_specs=in_specs, out_specs=out_specs, check_vma=False
    )
```

```python
import functools

import jax
import jax.numpy as jnp
from jax import lax
from jax.experimental import pallas as pl
from jax.experimental.pallas import tpu as pltpu
from jax.sharding import PartitionSpec as P

GROUPS = 32
LANES = 128
PAD_ROWS = 32

norm_epsilon = 1e-05
beta_first = 0.9
beta_second = 0.999
adam_epsilon = 1e-08
learn_rate = 0.001
weight_decay = 0.01
clip_limit = 1.0
correct_first = 1.0
correct_second = 0.6323045752290363

MESH = pl.DeviceIdType.MESH
VMEM_LIMIT = 48 * 1024 * 1024


def swap_halves(block):
    return pltpu.roll(block, LANES // 2, axis=1)


def lower_half(shape):
    return lax.broadcasted_iota(jnp.int32, shape, 1) < LANES // 2


def layer_kernel(
    split_rows,
    plane,
    depth,
    x_hbm,
    cot_hbm,
    w_hbm,
    gain_hbm,
    shift_hbm,
    master_hbm,
    first_hbm,
    second_hbm,
    gin_ref,
    wout,
    tail_ref,
    new_master_ref,
    new_first_ref,
    new_second_ref,
    x_ref,
    cot_ref,
    w_ref,
    gain_ref,
    shift_ref,
    gath,
    rows,
    act3,
    cot3,
    wcat,
    kgrad,
    flat,
    normed_s,
    dact_s,
    gact,
    send1,
    recv1,
    send2,
    recv2,
    acc,
    recv3,
    state,
    gsum,
    norm_line,
    norm_plane,
    tails,
    sendz,
    recvz,
    zacc,
    recvf,
    in_sem,
    s1,
    r1,
    s2,
    r2,
    s3,
    r3,
    sl,
    rl,
    sp,
    rp,
    ss,
    rs,
    sg,
    rg,
    sb,
    rb,
    sc,
    rc,
    st,
    rt,
    sz,
    rz,
    sf,
    rf,
):
    f32, bf16 = jnp.float32, jnp.bfloat16
    line = 2 * depth
    grp, dp = lax.axis_index("grp"), lax.axis_index("dp")
    p = grp * split_rows + dp // line
    spot = dp % line
    z, core = spot // 2, spot % 2
    shard_rows = master_hbm.shape[0]

    def device(p_, spot_):
        return (p_ // split_rows, (p_ % split_rows) * line + spot_)

    def in_plane(t):
        return device((p + t) % plane, spot)

    def in_line(t):
        return device(p, (spot + t) % line)

    def in_depth(t):
        return device(p, ((z + t) % depth) * 2 + core)

    partner = device(p, z * 2 + 1 - core)

    def copy(src, dst, send, recv, target):
        return pltpu.make_async_remote_copy(
            src_ref=src,
            dst_ref=dst,
            send_sem=send,
            recv_sem=recv,
            device_id=target,
            device_id_type=MESH,
        )

    def loop(lo, hi, body):
        def step(t, carry):
            body(t)
            return carry

        lax.fori_loop(lo, hi, step, 0)

    state[z] = jnp.zeros(state.shape[1:], f32)
    pairs = [(x_hbm, x_ref), (gain_hbm, gain_ref), (shift_hbm, shift_ref)]
    pairs += [(cot_hbm, cot_ref), (w_hbm, w_ref)]
    for n, ref in enumerate((master_hbm, first_hbm, second_hbm)):
        pairs.append((ref, state.at[z, n, pl.ds(0, shard_rows)]))
    loads = [
        pltpu.make_async_copy(source, target, in_sem.at[n])
        for n, (source, target) in enumerate(pairs)
    ]
    for load in loads:
        load.start()

    barrier = pltpu.get_barrier_semaphore()

    def greet(target):
        pl.semaphore_signal(barrier, inc=1, device_id=target, device_id_type=MESH)

    loop(1, plane, lambda t: greet(in_plane(t)))
    loop(1, line, lambda t: greet(in_line(t)))

    height, channels, width = x_ref.shape
    count = height * width * (channels // GROUPS)

    row_id = lax.broadcasted_iota(jnp.int32, (channels, channels), 0)
    col_id = lax.broadcasted_iota(jnp.int32, (channels, channels), 1)
    eye = (row_id == col_id).astype(f32)
    per = 1.0 / (channels // GROUPS)
    row_group = jnp.floor((row_id.astype(f32) + 0.5) * per)
    col_group = jnp.floor((col_id.astype(f32) + 0.5) * per)
    same_group = (row_group == col_group).astype(f32)

    def group_mean(block):
        mixed = jnp.dot(
            same_group, block, precision=lax.Precision.HIGHEST, preferred_element_type=f32
        )
        return jnp.sum(mixed, axis=1, keepdims=True) * (1.0 / count)

    def as_column(row):
        return jnp.sum(eye * row, axis=1, keepdims=True)

    def as_row(column):
        return jnp.sum(eye * column, axis=0, keepdims=True)

    for load in loads[:3]:
        load.wait()
    gain = as_column(gain_ref[...].reshape(1, channels))
    shift = as_column(shift_ref[...].reshape(1, channels))

    zero_block = jnp.zeros((channels, width), f32)
    total = lax.fori_loop(
        0, height, lambda r, s: s + x_ref[r].astype(f32), zero_block
    )
    centre = group_mean(total)

    def spread_step(r, s):
        centred = x_ref[r].astype(f32) - centre
        return s + centred * centred

    spread = group_mean(lax.fori_loop(0, height, spread_step, zero_block))
    rstd = lax.rsqrt(spread + norm_epsilon)

    pl.semaphore_wait(barrier, plane + line - 2)

    for load in loads[5:]:
        load.wait()

    def spread_state(t):
        return copy(state.at[z], state.at[z], ss.at[t], rs.at[t], in_depth(t))

    loop(1, depth, lambda t: spread_state(t).start())

    lane = lax.broadcasted_iota(jnp.int32, (channels, width), 1)
    zero_bf = jnp.zeros((channels, width), bf16)
    act3[0:channels, 0:width] = zero_bf
    act3[2 * channels : 3 * channels, (height - 1) * width : height * width] = zero_bf
    cot3[:, 0:width] = jnp.zeros((cot3.shape[0], width), bf16)
    cot3[:, (height + 1) * width :] = jnp.zeros((cot3.shape[0], width), bf16)
    cot3[3 * channels :, :] = jnp.zeros((cot3.shape[0] - 3 * channels, cot3.shape[1]), bf16)

    loads[3].wait()
    bias_total = zero_block
    for r in range(height):
        normed = (x_ref[r].astype(f32) - centre) * rstd
        pre = normed * gain + shift
        sig = 1.0 / (1.0 + jnp.exp(-pre))
        act = (pre * sig).astype(bf16)
        normed_s[r] = normed
        dact_s[r] = sig * (1.0 + pre * (1.0 - sig))
        for i in range(3):
            dest = r - i + 1
            if 0 <= dest < height:
                act3[i * channels : (i + 1) * channels, dest * width : (dest + 1) * width] = act
        cot = cot_ref[r].astype(f32)
        bias_total = bias_total + cot
        place = slice((r + 1) * width, (r + 2) * width)
        ahead = jnp.where(lane < width - 1, pltpu.roll(cot, width - 1, axis=1), 0.0)
        behind = jnp.where(lane > 0, pltpu.roll(cot, 1, axis=1), 0.0)
        cot3[0:channels, place] = ahead.astype(bf16)
        cot3[channels : 2 * channels, place] = cot_ref[r]
        cot3[2 * channels : 3 * channels, place] = behind.astype(bf16)

    for n in range(cot3.shape[0] // 256):
        block = lax.dot_general(
            act3[...],
            cot3[n * 256 : (n + 1) * 256, width : (height + 1) * width],
            (((1,), (1,)), ((), ())),
            preferred_element_type=f32,
        )
        kgrad[2 * n] = block[:, :LANES]
        kgrad[2 * n + 1] = block[:, LANES:]

    half = channels // 2
    low = lower_half((half, LANES))
    flat_rows = flat.shape[0]
    for i in range(3):
        for j in range(3):
            first = (j * channels) // LANES
            even = [kgrad[first + b, pl.ds(i * channels, half, stride=2), :] for b in range(3)]
            odd = [kgrad[first + b, pl.ds(i * channels + 1, half, stride=2), :] for b in range(3)]
            if j == 1:
                even_r = [swap_halves(e) for e in even]
                pieces = [
                    jnp.where(low, even_r[0], even_r[1]),
                    jnp.where(low, even_r[1], even_r[2]),
                    jnp.where(low, even_r[2], odd[0]),
                    odd[1],
                    odd[2],
                ]
            else:
                odd_r = [swap_halves(o) for o in odd]
                pieces = [
                    even[0],
                    even[1],
                    jnp.where(low, even[2], odd_r[0]),
                    jnp.where(low, odd_r[0], odd_r[1]),
                    jnp.where(low, odd_r[1], odd_r[2]),
                ]
            base = (3 * i + j) * (channels * channels // LANES)
            for b in range(5):
                flat[pl.ds(base + b, half, stride=5), :] = pieces[b]

    used = 9 * channels * channels // LANES
    flat[used:flat_rows, :] = jnp.zeros((flat_rows - used, LANES), f32)


    def far_first(n):
        return jnp.where(n == 0, 2, jnp.where(n == 1, 1, jnp.where(n == 2, 3, 0)))

    x_size, w_size = gath.shape[1], gath.shape[2]
    xi, wi = p // w_size, p % w_size
    yi = (wi % 2) * 2 + wi // 2
    own_t = plane - 1

    def chunk(t):
        t = jnp.where(t == 3, 4, jnp.where(t == 4, 3, t))
        x_to = (xi + far_first(t // 4)) % x_size
        y_to = (yi + far_first(t % 4)) % w_size
        return x_to * w_size + (y_to % 2) * 2 + y_to // 2

    def pair(t):
        q = chunk(t)
        return copy(send1.at[q], recv1.at[q], s1.at[t], r1.at[t], partner)

    def pair_start(t):
        q = chunk(t)
        for k in range(depth):
            row = ((q * depth + k) * 2 + 1 - core) * shard_rows
            send1[q, k] = flat[pl.ds(row, PAD_ROWS), :].astype(bf16)
        pair(t).start()

    def across(t):
        return copy(send2.at[t], recv2.at[t], s2.at[t], r2.at[t], device(chunk(t), spot))

    def pair_sum(q, k):
        row = ((q * depth + k) * 2 + core) * shard_rows
        return flat[pl.ds(row, PAD_ROWS), :] + recv1[q, k].astype(f32)

    def across_start(t):
        pair(t).wait_recv()
        q = chunk(t)
        for k in range(depth):
            send2[t, k] = pair_sum(q, k).astype(bf16)
        across(t).start()

    far, lead = zacc.shape[0], 4

    def far_step(t):
        pair_start(t + lead)
        pair(t).wait_recv()
        q = chunk(t)
        for k in range(depth):
            sendz[k, t] = pair_sum(q, k).astype(bf16)
        zacc[t] = pair_sum(q, z)

    def far_along(t):
        return copy(
            sendz.at[(z + t) % depth], recvz.at[t], sz.at[t], rz.at[t], in_depth(t)
        )

    def far_across(t):
        return copy(zacc.at[t], recvf.at[t], sf.at[t], rf.at[t], device(chunk(t), spot))

    def both(t):
        pair_start(t + lead)
        across_start(t)

    loop(0, lead, pair_start)
    loop(0, far, far_step)
    loop(1, depth, lambda t: far_along(t).start())
    loop(far, plane - lead, both)
    loop(plane - lead, own_t, across_start)

    loads[4].wait()
    wcat[...] = jnp.zeros_like(wcat)
    for i in range(3):
        for j in range(3):
            wcat[i * channels : (i + 1) * channels, j * channels : (j + 1) * channels] = w_ref[
                3 * i + j
            ]

    def back_step(n, carry):
        shift_sum, gain_sum = carry
        block = None
        for i in range(3):
            start = pl.multiple_of((2 * n + 2 - i) * width, width)
            term = jnp.dot(
                wcat[i * channels : (i + 1) * channels, :],
                cot3[:, pl.ds(start, 2 * width)],
                preferred_element_type=f32,
            )
            block = term if block is None else block + term
        for h in range(2):
            dpre = block[:, h * width : (h + 1) * width] * dact_s[2 * n + h]
            gact[2 * n + h] = dpre
            shift_sum = shift_sum + dpre
            gain_sum = gain_sum + dpre * normed_s[2 * n + h]
        return shift_sum, gain_sum

    shift_sum, gain_sum = lax.fori_loop(
        0, height // 2, back_step, (zero_block, zero_block)
    )
    mean_grad = group_mean(shift_sum * gain)
    mean_cross = group_mean(gain_sum * gain)

    bias_row = as_row(jnp.sum(bias_total, axis=1, keepdims=True))
    gain_row = as_row(jnp.sum(gain_sum, axis=1, keepdims=True))
    shift_row = as_row(jnp.sum(shift_sum, axis=1, keepdims=True))
    tail_shard = used // shard_rows
    tail_place, tail_spot = tail_shard // line, tail_shard % line
    tail_z, tail_core = tail_spot // 2, tail_spot % 2
    tail_row = used - tail_shard * shard_rows
    owns_tail = core == tail_core
    tails[0] = jnp.zeros(tails.shape[1:], f32)
    tails[0, 0:1, :] = bias_row[:, 0:128]
    tails[0, 1:2, :] = bias_row[:, 128:256]
    tails[0, 2:3, 0:64] = bias_row[:, 256:320]
    tails[0, 2:3, 64:128] = gain_row[:, 0:64]
    tails[0, 3:4, :] = gain_row[:, 64:192]
    tails[0, 4:5, :] = gain_row[:, 192:320]
    tails[0, 5:6, :] = shift_row[:, 0:128]
    tails[0, 6:7, :] = shift_row[:, 128:256]
    tails[0, 7:8, 0:64] = shift_row[:, 256:320]

    tail_pair = copy(tails.at[0], tails.at[plane + 1], st.at[0], rt.at[0], partner)

    @pl.when(core != tail_core)
    def _():
        tail_pair.start()

    def tail_across(t):
        return copy(
            tails.at[plane], tails.at[t], st.at[1], rt.at[t], device(tail_place, spot)
        )

    tail_t = (tail_place + plane - p) % plane

    def far_take(t):
        far_along(t).wait_recv()
        zacc[...] += recvz[t].astype(f32)

    loop(1, depth, far_take)
    loop(0, far, lambda t: far_across(t).start())

    @pl.when(owns_tail)
    def _():
        tail_pair.wait_recv()
        tails[plane] = tails[0] + tails[plane + 1]

        @pl.when(p != tail_place)
        def _():
            tail_across(tail_t).start()

    pair(own_t).wait_recv()
    for k in range(depth):
        acc[k] = pair_sum(p, k)

    def across_take(t):
        across(t).wait_recv()
        acc[...] += recv2[t].astype(f32)

    loop(far, own_t, across_take)

    def along(t):
        return copy(acc.at[(z + t) % depth], recv3.at[t], s3.at[t], r3.at[t], in_depth(t))

    loop(1, depth, lambda t: along(t).start())
    def input_step(r, carry):
        slope = gact[r] * gain
        gin_ref[r] = (rstd * (slope - mean_grad - normed_s[r] * mean_cross)).astype(bf16)
        return carry

    lax.fori_loop(0, height, input_step, 0)

    loop(1, depth, lambda t: along(t).wait_recv())
    summed = acc[z]
    for t in range(1, depth):
        summed = summed + recv3[t]
    loop(0, far, lambda t: far_across(t).wait_recv())
    for t in range(far):
        summed = summed + recvf[t]
    live = lax.broadcasted_iota(jnp.int32, summed.shape, 0) < shard_rows
    summed = jnp.where(live, summed, 0.0)

    squares = summed * summed
    squares = jnp.sum(squares, axis=0, keepdims=True)
    squares = squares + swap_halves(squares)
    row8 = lax.broadcasted_iota(jnp.int32, (8, LANES), 0)
    spare = jnp.logical_and(row8 == 7, jnp.logical_not(lower_half((8, LANES))))
    tails[plane + 1] = jnp.where(spare, squares, 0.0)

    @pl.when(jnp.logical_and(owns_tail, p == tail_place))
    def _():
        def tail_take(t):
            tail_across(t).wait_recv()
            tails[plane] += tails[t]

        loop(1, plane, tail_take)
        tails[plane + 1] += tails[plane]

    norm_line[spot] = tails[plane + 1]
    gsum[z] = summed

    def line_copy(t):
        mine = norm_line.at[spot]
        return copy(mine, mine, sl.at[t], rl.at[t], in_line(t))

    def line_got(t):
        theirs = norm_line.at[(spot + line - t) % line]
        return copy(theirs, theirs, sl.at[t], rl.at[t], in_line(t))

    def spread_sum(t):
        return copy(gsum.at[z], gsum.at[z], sg.at[t], rg.at[t], in_depth(t))

    def sum_got(t):
        theirs = gsum.at[(z + depth - t) % depth]
        return copy(theirs, theirs, sg.at[t], rg.at[t], in_depth(t))

    def state_got(t):
        theirs = state.at[(z + depth - t) % depth]
        return copy(theirs, theirs, ss.at[t], rs.at[t], in_depth(t))

    loop(1, line, lambda t: line_copy(t).start())
    loop(1, depth, lambda t: spread_sum(t).start())
    loop(1, line, lambda t: line_got(t).wait_recv())
    line_sums = norm_line[0]
    for n in range(1, line):
        line_sums = line_sums + norm_line[n]
    entries_sum = jnp.where(spare, 0.0, line_sums)
    sumsq = jnp.where(spare, line_sums, entries_sum * entries_sum)
    norm_plane[p] = sumsq

    def plane_copy(t):
        mine = norm_plane.at[p]
        return copy(mine, mine, sp.at[t], rp.at[t], in_plane(t))

    def plane_got(t):
        theirs = norm_plane.at[(p + plane - t) % plane]
        return copy(theirs, theirs, sp.at[t], rp.at[t], in_plane(t))

    loop(1, plane, lambda t: plane_copy(t).start())
    loop(1, depth, lambda t: state_got(t).wait_recv())
    loop(1, depth, lambda t: sum_got(t).wait_recv())
    loop(1, depth, lambda t: spread_sum(t).wait_send())

    @pl.when(owns_tail)
    def _():
        gsum[tail_z, pl.ds(tail_row, 8)] += entries_sum

    loop(1, plane, lambda t: plane_got(t).wait_recv())
    sumsq = norm_plane[0]
    for n in range(1, plane):
        sumsq = sumsq + norm_plane[n]
    norm_total = jnp.sum(jnp.sum(sumsq, axis=1, keepdims=True), axis=0, keepdims=True)
    clip = jnp.minimum(1.0, clip_limit / (jnp.sqrt(norm_total) + 1e-06))

    def adam(total, master, first, second):
        clipped = clip * total
        new_first = beta_first * first + (1.0 - beta_first) * clipped
        new_second = beta_second * second + (1.0 - beta_second) * clipped * clipped
        step_dir = new_first / correct_first / (
            jnp.sqrt(new_second / correct_second) + adam_epsilon
        )
        return master - learn_rate * (step_dir + weight_decay * master), new_first, new_second

    for k in range(depth):
        updated, _, _ = adam(gsum[k], state[k, 0], state[k, 1], state[k, 2])
        gath[core, xi, wi, k] = updated.astype(bf16)

    half_depth = depth // 2

    def back_x(t):
        return (xi + x_size - t) % x_size

    def back_w(t):
        return (wi + w_size - t) % w_size

    def part(c, h, tx, tw):
        return gath.at[c, back_x(tx), back_w(tw), pl.ds(h * half_depth, half_depth)]

    def slots_x(h, t, tw):
        spots = (h, t, 0) if h == 0 else (h, tw, t)
        return sb.at[spots], rb.at[spots]

    def slots_w(h, t, tx):
        spots = (h, t, 0) if h == 1 else (h, tx, t)
        return sb.at[spots], rb.at[spots]

    def along_x(h, t, tw):
        block = part(core, h, 0, tw)
        target = device(((xi + t) % x_size) * w_size + wi, spot)
        return copy(block, block, *slots_x(h, t, tw), target)

    def along_w(h, t, tx):
        block = part(core, h, tx, 0)
        target = device(xi * w_size + (wi + t) % w_size, spot)
        return copy(block, block, *slots_w(h, t, tx), target)

    def got_x(h, t, tw):
        block = part(core, h, t, tw)
        target = device(((xi + t) % x_size) * w_size + wi, spot)
        return copy(block, block, *slots_x(h, t, tw), target)

    def got_w(h, t, tx):
        block = part(core, h, tx, t)
        target = device(xi * w_size + (wi + t) % w_size, spot)
        return copy(block, block, *slots_w(h, t, tx), target)

    def gather_core(h, tx, tw):
        block = part(core, h, tx, tw)
        return copy(block, block, sc.at[h, tx, tw], rc.at[h, tx, tw], partner)

    def got_core(h, tx, tw):
        block = part(1 - core, h, tx, tw)
        return copy(block, block, sc.at[h, tx, tw], rc.at[h, tx, tw], partner)

    def to_flat(c, h, tx, tw):
        sx, sw = back_x(tx), back_w(tw)
        for k in range(half_depth):
            spot_k = (h * half_depth + k) * 2 + c
            row = ((sx * w_size + sw) * line + spot_k) * shard_rows
            block = gath[c, sx, sw, h * half_depth + k].astype(f32)
            flat[pl.ds(row, shard_rows), :] = block[0:shard_rows]

    loop(1, x_size, lambda t: along_x(0, t, 0).start())
    loop(1, w_size, lambda t: along_w(1, t, 0).start())
    loop(1, w_size, lambda t: along_w(0, t, 0).start())
    loop(1, x_size, lambda t: along_x(1, t, 0).start())
    gather_core(0, 0, 0).start()
    gather_core(1, 0, 0).start()
    to_flat(core, 0, 0, 0)
    to_flat(core, 1, 0, 0)
    results = adam(gsum[z], state[z, 0], state[z, 1], state[z, 2])
    for ref, value in zip((new_master_ref, new_first_ref, new_second_ref), results):
        ref[...] = value[0:shard_rows]

    def first_x(t):
        got_x(0, t, 0).wait_recv()
        loop(1, w_size, lambda s: along_w(0, s, t).start())
        gather_core(0, t, 0).start()

    def first_w(t):
        got_w(1, t, 0).wait_recv()
        loop(1, x_size, lambda s: along_x(1, s, t).start())
        gather_core(1, 0, t).start()

    def first(t):
        first_x(t)
        first_w(t)

    loop(1, x_size, first)

    def first_flat(t):
        to_flat(core, 0, t, 0)
        to_flat(core, 1, 0, t)

    loop(1, x_size, first_flat)

    def second(n):
        a, b = n // (w_size - 1), n % (w_size - 1) + 1
        got_w(0, b, a).wait_recv()
        gather_core(0, a, b).start()
        got_x(1, b, a).wait_recv()
        gather_core(1, b, a).start()
        to_flat(core, 0, a, b)
        to_flat(core, 1, b, a)

    loop(0, x_size * (w_size - 1), second)

    def third(n):
        a, b = n // w_size, n % w_size
        got_core(0, a, b).wait_recv()
        to_flat(1 - core, 0, a, b)
        got_core(1, b, a).wait_recv()
        to_flat(1 - core, 1, b, a)

    loop(0, x_size * w_size, third)

    five = channels * channels // LANES

    def rows_step(n):
        piece = [flat[pl.ds(n * five + b, half, stride=5), :] for b in range(5)]
        turned = [swap_halves(piece[b]) for b in range(2, 5)]
        even = [piece[0], piece[1], piece[2]]
        odd = [
            jnp.where(low, turned[0], turned[1]),
            jnp.where(low, turned[1], turned[2]),
            turned[2],
        ]
        for b in range(3):
            rows[b, pl.ds(0, half, stride=2), :] = even[b]
            rows[b, pl.ds(1, half, stride=2), :] = odd[b]
        place = pl.ds(pl.multiple_of(n * channels, channels), channels)
        wout[place, 0:128] = rows[0].astype(bf16)
        wout[place, 128:256] = rows[1].astype(bf16)
        wout[place, 256:channels] = rows[2, :, 0 : channels - 256].astype(bf16)

    loop(0, 9, rows_step)
    tail_ref[...] = flat[used : used + 8, :]

    loop(0, plane, lambda t: pair(t).wait_send())
    loop(far, own_t, lambda t: across(t).wait_send())
    loop(1, depth, lambda t: along(t).wait_send())
    loop(1, line, lambda t: line_copy(t).wait_send())
    loop(1, plane, lambda t: plane_copy(t).wait_send())
    loop(1, depth, lambda t: spread_state(t).wait_send())
    loop(1, depth, lambda t: far_along(t).wait_send())
    loop(0, far, lambda t: far_across(t).wait_send())

    @pl.when(core != tail_core)
    def _():
        tail_pair.wait_send()

    @pl.when(jnp.logical_and(owns_tail, p != tail_place))
    def _():
        tail_across(tail_t).wait_send()

    def all_sent(n):
        a, b = n // w_size, n % w_size
        gather_core(0, a, b).wait_send()
        gather_core(1, a, b).wait_send()

        @pl.when(b > 0)
        def _():
            along_w(0, b, a).wait_send()
            along_x(1, b, a).wait_send()

    loop(0, x_size * w_size, all_sent)
    loop(1, x_size, lambda t: along_x(0, t, 0).wait_send())
    loop(1, w_size, lambda t: along_w(1, t, 0).wait_send())


def run_layer(x, cot, weight, gain, shift, master, first, second, plane, depth, split_rows):
    f32, bf16 = jnp.float32, jnp.bfloat16
    height, channels, width = x.shape
    line = 2 * depth
    wide = -(-3 * channels // 256) * 256
    flat_rows = plane * line * master.shape[0] + PAD_ROWS
    shard = pltpu.VMEM(master.shape, f32)
    weight = weight.reshape(9, channels, channels)
    far = 4
    ring_w = 2 * split_rows
    ring_x = plane // ring_w
    gathered = (2, ring_x, ring_w, depth, PAD_ROWS, LANES)
    part = (plane, depth, PAD_ROWS, LANES)
    dma = lambda *n: pltpu.SemaphoreType.DMA(n)
    vmem, hbm = pl.BlockSpec(memory_space=pltpu.VMEM), pl.BlockSpec(memory_space=pltpu.HBM)
    operands = (x, cot, weight, gain, shift, master, first, second)
    operands = [pltpu.with_memory_space_constraint(a, pltpu.HBM) for a in operands]
    return pl.pallas_call(
        functools.partial(layer_kernel, split_rows, plane, depth),
        out_shape=(
            pltpu.VMEM(x.shape, bf16),
            pltpu.VMEM((9 * channels, channels), bf16),
            pltpu.VMEM((8, LANES), f32),
            shard,
            shard,
            shard,
        ),
        in_specs=[hbm] * 8,
        out_specs=[vmem] * 6,
        scratch_shapes=[
            pltpu.VMEM(x.shape, bf16),
            pltpu.VMEM(x.shape, bf16),
            pltpu.VMEM(weight.shape, bf16),
            pltpu.VMEM(gain.shape, f32),
            pltpu.VMEM(shift.shape, f32),
            pltpu.VMEM(gathered, bf16),
            pltpu.VMEM((3, channels, LANES), f32),
            pltpu.VMEM((3 * channels, height * width), bf16),
            pltpu.VMEM((wide, (height + 2) * width), bf16),
            pltpu.VMEM((3 * channels, wide), bf16),
            pltpu.VMEM((wide // LANES, 3 * channels, LANES), f32),
            pltpu.VMEM((flat_rows, LANES), f32),
            pltpu.VMEM((height, channels, width), f32),
            pltpu.VMEM((height, channels, width), f32),
            pltpu.VMEM((height, channels, width), f32),
            pltpu.VMEM(part, bf16),
            pltpu.VMEM(part, bf16),
            pltpu.VMEM(part, bf16),
            pltpu.VMEM(part, bf16),
            pltpu.VMEM((depth, PAD_ROWS, LANES), f32),
            pltpu.VMEM((depth, PAD_ROWS, LANES), f32),
            pltpu.VMEM((depth, 3, PAD_ROWS, LANES), f32),
            pltpu.VMEM((depth, PAD_ROWS, LANES), f32),
            pltpu.VMEM((line, 8, LANES), f32),
            pltpu.VMEM((plane, 8, LANES), f32),
            pltpu.VMEM((plane + 2, 8, LANES), f32),
            pltpu.VMEM((depth, far, PAD_ROWS, LANES), bf16),
            pltpu.VMEM((depth, far, PAD_ROWS, LANES), bf16),
            pltpu.VMEM((far, PAD_ROWS, LANES), f32),
            pltpu.VMEM((far, PAD_ROWS, LANES), f32),
            dma(8),
        ]
        + [dma(n) for n in (plane, plane, plane, plane, depth, depth, line, line)]
        + [dma(n) for n in (plane, plane, depth, depth, depth, depth)]
        + [dma(2, ring_x, ring_w)] * 4
        + [dma(2), dma(plane), dma(depth), dma(depth), dma(far), dma(far)],
        compiler_params=pltpu.CompilerParams(
            collective_id=0, has_side_effects=True, vmem_limit_bytes=VMEM_LIMIT
        ),
    )(*operands)


def finish_kernel(tail_ref, *refs):
    count = 5
    sources, targets = refs[:count], refs[count : 2 * count]
    rows_out, sems = refs[2 * count : 2 * count + 3], refs[-1]
    copies = [
        pltpu.make_async_copy(sources[n], targets[n], sems.at[n]) for n in range(count)
    ]
    for each in copies:
        each.start()
    tail = [tail_ref[b : b + 1, :] for b in range(8)]
    rows = (
        [tail[0], tail[1], tail[2][:, 0:64]],
        [tail[2][:, 64:128], tail[3], tail[4]],
        [tail[5], tail[6], tail[7][:, 0:64]],
    )
    for ref, row in zip(rows_out, rows):
        ref[...] = jnp.concatenate(row, axis=1).astype(ref.dtype).reshape(ref.shape)
    for each in copies:
        each.wait()


def finish(tail, results, channels):
    row = jax.ShapeDtypeStruct((channels,), jnp.bfloat16)
    vmem, anywhere = pl.BlockSpec(memory_space=pltpu.VMEM), pl.BlockSpec(memory_space=pl.ANY)
    pinned = [pltpu.with_memory_space_constraint(r, pltpu.VMEM) for r in (tail, *results)]
    return pl.pallas_call(
        finish_kernel,
        out_shape=tuple(jax.ShapeDtypeStruct(r.shape, r.dtype) for r in results) + (row,) * 3,
        in_specs=[vmem] * 6,
        out_specs=[anywhere] * 5 + [vmem] * 3,
        scratch_shapes=[pltpu.SemaphoreType.DMA((5,))],
        compiler_params=pltpu.CompilerParams(vmem_limit_bytes=4 * 1024 * 1024),
    )(*pinned)


def on_device(latents, cotangent, weight, gain, shift, master, first_moment, second_moment):
    groups, owners = lax.axis_size("grp"), lax.axis_size("dp")
    channels = weight.shape[2]
    split_rows = 2
    depth = owners // (2 * split_rows)
    plane = groups * split_rows
    shard_rows = master.shape[0] // LANES
    x = jnp.transpose(latents[0], (0, 2, 1))
    cot = jnp.transpose(cotangent[0], (0, 2, 1))
    shaped = [a.reshape(shard_rows, LANES) for a in (master, first_moment, second_moment)]
    grad_in, new_weight, tail, *state = run_layer(
        x, cot, weight, gain, shift, *shaped, plane, depth, split_rows
    )
    results = finish(tail, (grad_in, new_weight, *state), channels)
    grad_in, new_weight, new_master, new_first, new_second = results[:5]
    new_bias, new_gain, new_shift = results[5:]
    return (
        jnp.transpose(grad_in, (0, 2, 1))[None],
        new_weight.reshape(weight.shape),
        new_bias,
        new_gain,
        new_shift,
        new_master.reshape(-1),
        new_first.reshape(-1),
        new_second.reshape(-1),
    )


def solution(mesh):
    split = ("grp", "dp")
    whole = P(split, None, None, None)
    in_specs = (whole, whole, P(), P(), P(), P(split), P(split), P(split))
    out_specs = (whole, P(), P(), P(), P(), P(split), P(split), P(split))
    return jax.shard_map(
        on_device, mesh=mesh, in_specs=in_specs, out_specs=out_specs, check_vma=False
    )
```

```python
import functools

import jax
import jax.numpy as jnp
from jax import lax
from jax.experimental import pallas as pl
from jax.experimental.pallas import tpu as pltpu
from jax.sharding import PartitionSpec as P

GROUPS = 32
LANES = 128
PAD_ROWS = 32

norm_epsilon = 1e-05
beta_first = 0.9
beta_second = 0.999
adam_epsilon = 1e-08
learn_rate = 0.001
weight_decay = 0.01
clip_limit = 1.0
correct_first = 1.0
correct_second = 0.6323045752290363

MESH = pl.DeviceIdType.MESH
VMEM_LIMIT = 48 * 1024 * 1024


def swap_halves(block):
    return pltpu.roll(block, LANES // 2, axis=1)


def lower_half(shape):
    return lax.broadcasted_iota(jnp.int32, shape, 1) < LANES // 2


def layer_kernel(
    split_rows,
    plane,
    depth,
    x_hbm,
    cot_hbm,
    w_hbm,
    gain_hbm,
    shift_hbm,
    master_hbm,
    first_hbm,
    second_hbm,
    gin_ref,
    wout,
    tail_ref,
    new_master_ref,
    new_first_ref,
    new_second_ref,
    x_ref,
    cot_ref,
    w_ref,
    gain_ref,
    shift_ref,
    gath,
    rows,
    act3,
    cot3,
    wcat,
    kgrad,
    flat,
    normed_s,
    dact_s,
    gact,
    send1,
    recv1,
    send2,
    recv2,
    acc,
    accb,
    recv3,
    state,
    gsum,
    norm_line,
    norm_plane,
    tails,
    sendz,
    recvz,
    zacc,
    recvf,
    in_sem,
    s1,
    r1,
    s2,
    r2,
    s3,
    r3,
    sl,
    rl,
    sp,
    rp,
    ss,
    rs,
    sg,
    rg,
    sb,
    rb,
    sc,
    rc,
    st,
    rt,
    sz,
    rz,
    sf,
    rf,
):
    f32, bf16 = jnp.float32, jnp.bfloat16
    line = 2 * depth
    grp, dp = lax.axis_index("grp"), lax.axis_index("dp")
    p = grp * split_rows + dp // line
    spot = dp % line
    z, core = spot // 2, spot % 2
    shard_rows = master_hbm.shape[0]

    def device(p_, spot_):
        return (p_ // split_rows, (p_ % split_rows) * line + spot_)

    def in_plane(t):
        return device((p + t) % plane, spot)

    def in_line(t):
        return device(p, (spot + t) % line)

    def in_depth(t):
        return device(p, ((z + t) % depth) * 2 + core)

    partner = device(p, z * 2 + 1 - core)

    def copy(src, dst, send, recv, target):
        return pltpu.make_async_remote_copy(
            src_ref=src,
            dst_ref=dst,
            send_sem=send,
            recv_sem=recv,
            device_id=target,
            device_id_type=MESH,
        )

    def loop(lo, hi, body):
        def step(t, carry):
            body(t)
            return carry

        lax.fori_loop(lo, hi, step, 0)

    state[z] = jnp.zeros(state.shape[1:], f32)
    pairs = [(x_hbm, x_ref), (gain_hbm, gain_ref), (shift_hbm, shift_ref)]
    pairs += [(cot_hbm, cot_ref), (w_hbm, w_ref)]
    for n, ref in enumerate((master_hbm, first_hbm, second_hbm)):
        pairs.append((ref, state.at[z, n, pl.ds(0, shard_rows)]))
    loads = [
        pltpu.make_async_copy(source, target, in_sem.at[n])
        for n, (source, target) in enumerate(pairs)
    ]
    for load in loads:
        load.start()

    barrier = pltpu.get_barrier_semaphore()

    def greet(target):
        pl.semaphore_signal(barrier, inc=1, device_id=target, device_id_type=MESH)

    loop(1, plane, lambda t: greet(in_plane(t)))
    loop(1, line, lambda t: greet(in_line(t)))

    height, channels, width = x_ref.shape
    count = height * width * (channels // GROUPS)

    row_id = lax.broadcasted_iota(jnp.int32, (channels, channels), 0)
    col_id = lax.broadcasted_iota(jnp.int32, (channels, channels), 1)
    eye = (row_id == col_id).astype(f32)
    per = 1.0 / (channels // GROUPS)
    row_group = jnp.floor((row_id.astype(f32) + 0.5) * per)
    col_group = jnp.floor((col_id.astype(f32) + 0.5) * per)
    same_group = (row_group == col_group).astype(f32)

    def group_mean(block):
        mixed = jnp.dot(
            same_group, block, precision=lax.Precision.HIGHEST, preferred_element_type=f32
        )
        return jnp.sum(mixed, axis=1, keepdims=True) * (1.0 / count)

    def as_column(row):
        return jnp.sum(eye * row, axis=1, keepdims=True)

    def as_row(column):
        return jnp.sum(eye * column, axis=0, keepdims=True)

    for load in loads[:3]:
        load.wait()
    gain = as_column(gain_ref[...].reshape(1, channels))
    shift = as_column(shift_ref[...].reshape(1, channels))

    zero_block = jnp.zeros((channels, width), f32)
    total = lax.fori_loop(
        0, height, lambda r, s: s + x_ref[r].astype(f32), zero_block
    )
    centre = group_mean(total)

    def spread_step(r, s):
        centred = x_ref[r].astype(f32) - centre
        return s + centred * centred

    spread = group_mean(lax.fori_loop(0, height, spread_step, zero_block))
    rstd = lax.rsqrt(spread + norm_epsilon)

    pl.semaphore_wait(barrier, plane + line - 2)

    for load in loads[5:]:
        load.wait()

    def spread_state(t):
        return copy(state.at[z], state.at[z], ss.at[t], rs.at[t], in_depth(t))

    loop(1, depth, lambda t: spread_state(t).start())

    lane = lax.broadcasted_iota(jnp.int32, (channels, width), 1)
    zero_bf = jnp.zeros((channels, width), bf16)
    act3[0:channels, 0:width] = zero_bf
    act3[2 * channels : 3 * channels, (height - 1) * width : height * width] = zero_bf
    cot3[:, 0:width] = jnp.zeros((cot3.shape[0], width), bf16)
    cot3[:, (height + 1) * width :] = jnp.zeros((cot3.shape[0], width), bf16)
    cot3[3 * channels :, :] = jnp.zeros((cot3.shape[0] - 3 * channels, cot3.shape[1]), bf16)

    loads[3].wait()
    bias_total = zero_block
    for r in range(height):
        normed = (x_ref[r].astype(f32) - centre) * rstd
        pre = normed * gain + shift
        sig = 1.0 / (1.0 + jnp.exp(-pre))
        act = (pre * sig).astype(bf16)
        normed_s[r] = normed
        dact_s[r] = sig * (1.0 + pre * (1.0 - sig))
        for i in range(3):
            dest = r - i + 1
            if 0 <= dest < height:
                act3[i * channels : (i + 1) * channels, dest * width : (dest + 1) * width] = act
        cot = cot_ref[r].astype(f32)
        bias_total = bias_total + cot
        place = slice((r + 1) * width, (r + 2) * width)
        ahead = jnp.where(lane < width - 1, pltpu.roll(cot, width - 1, axis=1), 0.0)
        behind = jnp.where(lane > 0, pltpu.roll(cot, 1, axis=1), 0.0)
        cot3[0:channels, place] = ahead.astype(bf16)
        cot3[channels : 2 * channels, place] = cot_ref[r]
        cot3[2 * channels : 3 * channels, place] = behind.astype(bf16)

    for n in range(cot3.shape[0] // 256):
        block = lax.dot_general(
            act3[...],
            cot3[n * 256 : (n + 1) * 256, width : (height + 1) * width],
            (((1,), (1,)), ((), ())),
            preferred_element_type=f32,
        )
        kgrad[2 * n] = block[:, :LANES]
        kgrad[2 * n + 1] = block[:, LANES:]

    half = channels // 2
    low = lower_half((half, LANES))
    flat_rows = flat.shape[0]
    for i in range(3):
        for j in range(3):
            first = (j * channels) // LANES
            even = [kgrad[first + b, pl.ds(i * channels, half, stride=2), :] for b in range(3)]
            odd = [kgrad[first + b, pl.ds(i * channels + 1, half, stride=2), :] for b in range(3)]
            if j == 1:
                even_r = [swap_halves(e) for e in even]
                pieces = [
                    jnp.where(low, even_r[0], even_r[1]),
                    jnp.where(low, even_r[1], even_r[2]),
                    jnp.where(low, even_r[2], odd[0]),
                    odd[1],
                    odd[2],
                ]
            else:
                odd_r = [swap_halves(o) for o in odd]
                pieces = [
                    even[0],
                    even[1],
                    jnp.where(low, even[2], odd_r[0]),
                    jnp.where(low, odd_r[0], odd_r[1]),
                    jnp.where(low, odd_r[1], odd_r[2]),
                ]
            base = (3 * i + j) * (channels * channels // LANES)
            for b in range(5):
                flat[pl.ds(base + b, half, stride=5), :] = pieces[b]

    used = 9 * channels * channels // LANES
    flat[used:flat_rows, :] = jnp.zeros((flat_rows - used, LANES), f32)


    def far_first(n):
        return jnp.where(n == 0, 2, jnp.where(n == 1, 1, jnp.where(n == 2, 3, 0)))

    x_size, w_size = gath.shape[1], gath.shape[2]
    xi, wi = p // w_size, p % w_size
    yi = (wi % 2) * 2 + wi // 2
    own_t = plane - 1

    def chunk(t):
        t = jnp.where(t == 3, 4, jnp.where(t == 4, 3, t))
        x_to = (xi + far_first(t // 4)) % x_size
        y_to = (yi + far_first(t % 4)) % w_size
        return x_to * w_size + (y_to % 2) * 2 + y_to // 2

    def pair(t):
        q = chunk(t)
        return copy(send1.at[q], recv1.at[q], s1.at[t], r1.at[t], partner)

    def pair_start(t):
        q = chunk(t)
        for k in range(depth):
            row = ((q * depth + k) * 2 + 1 - core) * shard_rows
            send1[q, k] = flat[pl.ds(row, PAD_ROWS), :].astype(bf16)
        pair(t).start()

    def across(t):
        return copy(send2.at[t], recv2.at[t], s2.at[t], r2.at[t], device(chunk(t), spot))

    def pair_sum(q, k):
        row = ((q * depth + k) * 2 + core) * shard_rows
        return flat[pl.ds(row, PAD_ROWS), :] + recv1[q, k].astype(f32)

    def across_start(t):
        pair(t).wait_recv()
        q = chunk(t)
        for k in range(depth):
            send2[t, k] = pair_sum(q, k).astype(bf16)
        across(t).start()

    far, lead = zacc.shape[0], 4

    def far_step(t):
        pair_start(t + lead)
        pair(t).wait_recv()
        q = chunk(t)
        for k in range(depth):
            sendz[k, t] = pair_sum(q, k).astype(bf16)
        zacc[t] = pair_sum(q, z)

    def far_along(t):
        return copy(
            sendz.at[(z + t) % depth], recvz.at[t], sz.at[t], rz.at[t], in_depth(t)
        )

    def far_across(t):
        return copy(zacc.at[t], recvf.at[t], sf.at[t], rf.at[t], device(chunk(t), spot))

    def both(t):
        pair_start(t + lead)
        across_start(t)

    loop(0, lead, pair_start)
    loop(0, far, far_step)
    loop(1, depth, lambda t: far_along(t).start())
    loop(far, plane - lead, both)
    loop(plane - lead, own_t, across_start)

    loads[4].wait()
    wcat[...] = jnp.zeros_like(wcat)
    for i in range(3):
        for j in range(3):
            wcat[i * channels : (i + 1) * channels, j * channels : (j + 1) * channels] = w_ref[
                3 * i + j
            ]

    def back_step(n, carry):
        shift_sum, gain_sum = carry
        block = None
        for i in range(3):
            start = pl.multiple_of((2 * n + 2 - i) * width, width)
            term = jnp.dot(
                wcat[i * channels : (i + 1) * channels, :],
                cot3[:, pl.ds(start, 2 * width)],
                preferred_element_type=f32,
            )
            block = term if block is None else block + term
        for h in range(2):
            dpre = block[:, h * width : (h + 1) * width] * dact_s[2 * n + h]
            gact[2 * n + h] = dpre
            shift_sum = shift_sum + dpre
            gain_sum = gain_sum + dpre * normed_s[2 * n + h]
        return shift_sum, gain_sum

    shift_sum, gain_sum = lax.fori_loop(
        0, height // 2, back_step, (zero_block, zero_block)
    )
    mean_grad = group_mean(shift_sum * gain)
    mean_cross = group_mean(gain_sum * gain)

    bias_row = as_row(jnp.sum(bias_total, axis=1, keepdims=True))
    gain_row = as_row(jnp.sum(gain_sum, axis=1, keepdims=True))
    shift_row = as_row(jnp.sum(shift_sum, axis=1, keepdims=True))
    tail_shard = used // shard_rows
    tail_place, tail_spot = tail_shard // line, tail_shard % line
    tail_z, tail_core = tail_spot // 2, tail_spot % 2
    tail_row = used - tail_shard * shard_rows
    owns_tail = core == tail_core
    tails[0] = jnp.zeros(tails.shape[1:], f32)
    tails[0, 0:1, :] = bias_row[:, 0:128]
    tails[0, 1:2, :] = bias_row[:, 128:256]
    tails[0, 2:3, 0:64] = bias_row[:, 256:320]
    tails[0, 2:3, 64:128] = gain_row[:, 0:64]
    tails[0, 3:4, :] = gain_row[:, 64:192]
    tails[0, 4:5, :] = gain_row[:, 192:320]
    tails[0, 5:6, :] = shift_row[:, 0:128]
    tails[0, 6:7, :] = shift_row[:, 128:256]
    tails[0, 7:8, 0:64] = shift_row[:, 256:320]

    tail_pair = copy(tails.at[0], tails.at[plane + 1], st.at[0], rt.at[0], partner)

    @pl.when(core != tail_core)
    def _():
        tail_pair.start()

    def tail_across(t):
        return copy(
            tails.at[plane], tails.at[t], st.at[1], rt.at[t], device(tail_place, spot)
        )

    tail_t = (tail_place + plane - p) % plane

    def far_take(t):
        far_along(t).wait_recv()
        zacc[...] += recvz[t].astype(f32)

    loop(1, depth, far_take)
    loop(0, far, lambda t: far_across(t).start())

    @pl.when(owns_tail)
    def _():
        tail_pair.wait_recv()
        tails[plane] = tails[0] + tails[plane + 1]

        @pl.when(p != tail_place)
        def _():
            tail_across(tail_t).start()

    pair(own_t).wait_recv()
    for k in range(depth):
        acc[k] = pair_sum(p, k)

    def across_take(t):
        across(t).wait_recv()
        acc[...] += recv2[t].astype(f32)

    loop(far, own_t, across_take)

    def along(t):
        return copy(accb.at[(z + t) % depth], recv3.at[t], s3.at[t], r3.at[t], in_depth(t))

    accb[...] = acc[...].astype(bf16)
    loop(1, depth, lambda t: along(t).start())
    def input_step(r, carry):
        slope = gact[r] * gain
        gin_ref[r] = (rstd * (slope - mean_grad - normed_s[r] * mean_cross)).astype(bf16)
        return carry

    lax.fori_loop(0, height, input_step, 0)

    loop(1, depth, lambda t: along(t).wait_recv())
    summed = acc[z]
    for t in range(1, depth):
        summed = summed + recv3[t].astype(f32)
    loop(0, far, lambda t: far_across(t).wait_recv())
    for t in range(far):
        summed = summed + recvf[t]
    live = lax.broadcasted_iota(jnp.int32, summed.shape, 0) < shard_rows
    summed = jnp.where(live, summed, 0.0)

    squares = summed * summed
    squares = jnp.sum(squares, axis=0, keepdims=True)
    squares = squares + swap_halves(squares)
    row8 = lax.broadcasted_iota(jnp.int32, (8, LANES), 0)
    spare = jnp.logical_and(row8 == 7, jnp.logical_not(lower_half((8, LANES))))
    tails[plane + 1] = jnp.where(spare, squares, 0.0)

    @pl.when(jnp.logical_and(owns_tail, p == tail_place))
    def _():
        def tail_take(t):
            tail_across(t).wait_recv()
            tails[plane] += tails[t]

        loop(1, plane, tail_take)
        tails[plane + 1] += tails[plane]

    norm_line[spot] = tails[plane + 1]
    gsum[z] = summed

    def line_copy(t):
        mine = norm_line.at[spot]
        return copy(mine, mine, sl.at[t], rl.at[t], in_line(t))

    def line_got(t):
        theirs = norm_line.at[(spot + line - t) % line]
        return copy(theirs, theirs, sl.at[t], rl.at[t], in_line(t))

    def spread_sum(t):
        return copy(gsum.at[z], gsum.at[z], sg.at[t], rg.at[t], in_depth(t))

    def sum_got(t):
        theirs = gsum.at[(z + depth - t) % depth]
        return copy(theirs, theirs, sg.at[t], rg.at[t], in_depth(t))

    def state_got(t):
        theirs = state.at[(z + depth - t) % depth]
        return copy(theirs, theirs, ss.at[t], rs.at[t], in_depth(t))

    loop(1, line, lambda t: line_copy(t).start())
    loop(1, depth, lambda t: spread_sum(t).start())
    loop(1, line, lambda t: line_got(t).wait_recv())
    line_sums = norm_line[0]
    for n in range(1, line):
        line_sums = line_sums + norm_line[n]
    entries_sum = jnp.where(spare, 0.0, line_sums)
    sumsq = jnp.where(spare, line_sums, entries_sum * entries_sum)
    norm_plane[p] = sumsq

    def plane_copy(t):
        mine = norm_plane.at[p]
        return copy(mine, mine, sp.at[t], rp.at[t], in_plane(t))

    def plane_got(t):
        theirs = norm_plane.at[(p + plane - t) % plane]
        return copy(theirs, theirs, sp.at[t], rp.at[t], in_plane(t))

    loop(1, plane, lambda t: plane_copy(t).start())
    loop(1, depth, lambda t: state_got(t).wait_recv())
    loop(1, depth, lambda t: sum_got(t).wait_recv())
    loop(1, depth, lambda t: spread_sum(t).wait_send())

    @pl.when(owns_tail)
    def _():
        gsum[tail_z, pl.ds(tail_row, 8)] += entries_sum

    loop(1, plane, lambda t: plane_got(t).wait_recv())
    sumsq = norm_plane[0]
    for n in range(1, plane):
        sumsq = sumsq + norm_plane[n]
    norm_total = jnp.sum(jnp.sum(sumsq, axis=1, keepdims=True), axis=0, keepdims=True)
    clip = jnp.minimum(1.0, clip_limit / (jnp.sqrt(norm_total) + 1e-06))

    def adam(total, master, first, second):
        clipped = clip * total
        new_first = beta_first * first + (1.0 - beta_first) * clipped
        new_second = beta_second * second + (1.0 - beta_second) * clipped * clipped
        step_dir = new_first / correct_first / (
            jnp.sqrt(new_second / correct_second) + adam_epsilon
        )
        return master - learn_rate * (step_dir + weight_decay * master), new_first, new_second

    for k in range(depth):
        updated, _, _ = adam(gsum[k], state[k, 0], state[k, 1], state[k, 2])
        gath[core, xi, wi, k] = updated.astype(bf16)

    half_depth = depth // 2

    def back_x(t):
        return (xi + x_size - t) % x_size

    def back_w(t):
        return (wi + w_size - t) % w_size

    def part(c, h, tx, tw):
        return gath.at[c, back_x(tx), back_w(tw), pl.ds(h * half_depth, half_depth)]

    def slots_x(h, t, tw):
        spots = (h, t, 0) if h == 0 else (h, tw, t)
        return sb.at[spots], rb.at[spots]

    def slots_w(h, t, tx):
        spots = (h, t, 0) if h == 1 else (h, tx, t)
        return sb.at[spots], rb.at[spots]

    def along_x(h, t, tw):
        block = part(core, h, 0, tw)
        target = device(((xi + t) % x_size) * w_size + wi, spot)
        return copy(block, block, *slots_x(h, t, tw), target)

    def along_w(h, t, tx):
        block = part(core, h, tx, 0)
        target = device(xi * w_size + (wi + t) % w_size, spot)
        return copy(block, block, *slots_w(h, t, tx), target)

    def got_x(h, t, tw):
        block = part(core, h, t, tw)
        target = device(((xi + t) % x_size) * w_size + wi, spot)
        return copy(block, block, *slots_x(h, t, tw), target)

    def got_w(h, t, tx):
        block = part(core, h, tx, t)
        target = device(xi * w_size + (wi + t) % w_size, spot)
        return copy(block, block, *slots_w(h, t, tx), target)

    def gather_core(h, tx, tw):
        block = part(core, h, tx, tw)
        return copy(block, block, sc.at[h, tx, tw], rc.at[h, tx, tw], partner)

    def got_core(h, tx, tw):
        block = part(1 - core, h, tx, tw)
        return copy(block, block, sc.at[h, tx, tw], rc.at[h, tx, tw], partner)

    def to_flat(c, h, tx, tw):
        sx, sw = back_x(tx), back_w(tw)
        for k in range(half_depth):
            spot_k = (h * half_depth + k) * 2 + c
            row = ((sx * w_size + sw) * line + spot_k) * shard_rows
            block = gath[c, sx, sw, h * half_depth + k].astype(f32)
            flat[pl.ds(row, shard_rows), :] = block[0:shard_rows]

    loop(1, x_size, lambda t: along_x(0, t, 0).start())
    loop(1, w_size, lambda t: along_w(1, t, 0).start())
    loop(1, w_size, lambda t: along_w(0, t, 0).start())
    loop(1, x_size, lambda t: along_x(1, t, 0).start())
    gather_core(0, 0, 0).start()
    gather_core(1, 0, 0).start()
    to_flat(core, 0, 0, 0)
    to_flat(core, 1, 0, 0)
    results = adam(gsum[z], state[z, 0], state[z, 1], state[z, 2])
    for ref, value in zip((new_master_ref, new_first_ref, new_second_ref), results):
        ref[...] = value[0:shard_rows]

    def first_x(t):
        got_x(0, t, 0).wait_recv()
        loop(1, w_size, lambda s: along_w(0, s, t).start())
        gather_core(0, t, 0).start()

    def first_w(t):
        got_w(1, t, 0).wait_recv()
        loop(1, x_size, lambda s: along_x(1, s, t).start())
        gather_core(1, 0, t).start()

    def first(t):
        first_x(t)
        first_w(t)

    loop(1, x_size, first)

    def first_flat(t):
        to_flat(core, 0, t, 0)
        to_flat(core, 1, 0, t)

    loop(1, x_size, first_flat)

    def second(n):
        a, b = n // (w_size - 1), n % (w_size - 1) + 1
        got_w(0, b, a).wait_recv()
        gather_core(0, a, b).start()
        got_x(1, b, a).wait_recv()
        gather_core(1, b, a).start()
        to_flat(core, 0, a, b)
        to_flat(core, 1, b, a)

    loop(0, x_size * (w_size - 1), second)

    def third(n):
        a, b = n // w_size, n % w_size
        got_core(0, a, b).wait_recv()
        to_flat(1 - core, 0, a, b)
        got_core(1, b, a).wait_recv()
        to_flat(1 - core, 1, b, a)

    loop(0, x_size * w_size, third)

    five = channels * channels // LANES

    def rows_step(n):
        piece = [flat[pl.ds(n * five + b, half, stride=5), :] for b in range(5)]
        turned = [swap_halves(piece[b]) for b in range(2, 5)]
        even = [piece[0], piece[1], piece[2]]
        odd = [
            jnp.where(low, turned[0], turned[1]),
            jnp.where(low, turned[1], turned[2]),
            turned[2],
        ]
        for b in range(3):
            rows[b, pl.ds(0, half, stride=2), :] = even[b]
            rows[b, pl.ds(1, half, stride=2), :] = odd[b]
        place = pl.ds(pl.multiple_of(n * channels, channels), channels)
        wout[place, 0:128] = rows[0].astype(bf16)
        wout[place, 128:256] = rows[1].astype(bf16)
        wout[place, 256:channels] = rows[2, :, 0 : channels - 256].astype(bf16)

    loop(0, 9, rows_step)
    tail_ref[...] = flat[used : used + 8, :]

    loop(0, plane, lambda t: pair(t).wait_send())
    loop(far, own_t, lambda t: across(t).wait_send())
    loop(1, depth, lambda t: along(t).wait_send())
    loop(1, line, lambda t: line_copy(t).wait_send())
    loop(1, plane, lambda t: plane_copy(t).wait_send())
    loop(1, depth, lambda t: spread_state(t).wait_send())
    loop(1, depth, lambda t: far_along(t).wait_send())
    loop(0, far, lambda t: far_across(t).wait_send())

    @pl.when(core != tail_core)
    def _():
        tail_pair.wait_send()

    @pl.when(jnp.logical_and(owns_tail, p != tail_place))
    def _():
        tail_across(tail_t).wait_send()

    def all_sent(n):
        a, b = n // w_size, n % w_size
        gather_core(0, a, b).wait_send()
        gather_core(1, a, b).wait_send()

        @pl.when(b > 0)
        def _():
            along_w(0, b, a).wait_send()
            along_x(1, b, a).wait_send()

    loop(0, x_size * w_size, all_sent)
    loop(1, x_size, lambda t: along_x(0, t, 0).wait_send())
    loop(1, w_size, lambda t: along_w(1, t, 0).wait_send())


def run_layer(x, cot, weight, gain, shift, master, first, second, plane, depth, split_rows):
    f32, bf16 = jnp.float32, jnp.bfloat16
    height, channels, width = x.shape
    line = 2 * depth
    wide = -(-3 * channels // 256) * 256
    flat_rows = plane * line * master.shape[0] + PAD_ROWS
    shard = pltpu.VMEM(master.shape, f32)
    weight = weight.reshape(9, channels, channels)
    far = 4
    ring_w = 2 * split_rows
    ring_x = plane // ring_w
    gathered = (2, ring_x, ring_w, depth, PAD_ROWS, LANES)
    part = (plane, depth, PAD_ROWS, LANES)
    dma = lambda *n: pltpu.SemaphoreType.DMA(n)
    vmem, hbm = pl.BlockSpec(memory_space=pltpu.VMEM), pl.BlockSpec(memory_space=pltpu.HBM)
    operands = (x, cot, weight, gain, shift, master, first, second)
    operands = [pltpu.with_memory_space_constraint(a, pltpu.HBM) for a in operands]
    return pl.pallas_call(
        functools.partial(layer_kernel, split_rows, plane, depth),
        out_shape=(
            pltpu.VMEM(x.shape, bf16),
            pltpu.VMEM((9 * channels, channels), bf16),
            pltpu.VMEM((8, LANES), f32),
            shard,
            shard,
            shard,
        ),
        in_specs=[hbm] * 8,
        out_specs=[vmem] * 6,
        scratch_shapes=[
            pltpu.VMEM(x.shape, bf16),
            pltpu.VMEM(x.shape, bf16),
            pltpu.VMEM(weight.shape, bf16),
            pltpu.VMEM(gain.shape, f32),
            pltpu.VMEM(shift.shape, f32),
            pltpu.VMEM(gathered, bf16),
            pltpu.VMEM((3, channels, LANES), f32),
            pltpu.VMEM((3 * channels, height * width), bf16),
            pltpu.VMEM((wide, (height + 2) * width), bf16),
            pltpu.VMEM((3 * channels, wide), bf16),
            pltpu.VMEM((wide // LANES, 3 * channels, LANES), f32),
            pltpu.VMEM((flat_rows, LANES), f32),
            pltpu.VMEM((height, channels, width), f32),
            pltpu.VMEM((height, channels, width), f32),
            pltpu.VMEM((height, channels, width), f32),
            pltpu.VMEM(part, bf16),
            pltpu.VMEM(part, bf16),
            pltpu.VMEM(part, bf16),
            pltpu.VMEM(part, bf16),
            pltpu.VMEM((depth, PAD_ROWS, LANES), f32),
            pltpu.VMEM((depth, PAD_ROWS, LANES), bf16),
            pltpu.VMEM((depth, PAD_ROWS, LANES), bf16),
            pltpu.VMEM((depth, 3, PAD_ROWS, LANES), f32),
            pltpu.VMEM((depth, PAD_ROWS, LANES), f32),
            pltpu.VMEM((line, 8, LANES), f32),
            pltpu.VMEM((plane, 8, LANES), f32),
            pltpu.VMEM((plane + 2, 8, LANES), f32),
            pltpu.VMEM((depth, far, PAD_ROWS, LANES), bf16),
            pltpu.VMEM((depth, far, PAD_ROWS, LANES), bf16),
            pltpu.VMEM((far, PAD_ROWS, LANES), f32),
            pltpu.VMEM((far, PAD_ROWS, LANES), f32),
            dma(8),
        ]
        + [dma(n) for n in (plane, plane, plane, plane, depth, depth, line, line)]
        + [dma(n) for n in (plane, plane, depth, depth, depth, depth)]
        + [dma(2, ring_x, ring_w)] * 4
        + [dma(2), dma(plane), dma(depth), dma(depth), dma(far), dma(far)],
        compiler_params=pltpu.CompilerParams(
            collective_id=0, has_side_effects=True, vmem_limit_bytes=VMEM_LIMIT
        ),
    )(*operands)


def finish_kernel(tail_ref, *refs):
    count = 5
    sources, targets = refs[:count], refs[count : 2 * count]
    rows_out, sems = refs[2 * count : 2 * count + 3], refs[-1]
    copies = [
        pltpu.make_async_copy(sources[n], targets[n], sems.at[n]) for n in range(count)
    ]
    for each in copies:
        each.start()
    tail = [tail_ref[b : b + 1, :] for b in range(8)]
    rows = (
        [tail[0], tail[1], tail[2][:, 0:64]],
        [tail[2][:, 64:128], tail[3], tail[4]],
        [tail[5], tail[6], tail[7][:, 0:64]],
    )
    for ref, row in zip(rows_out, rows):
        ref[...] = jnp.concatenate(row, axis=1).astype(ref.dtype).reshape(ref.shape)
    for each in copies:
        each.wait()


def finish(tail, results, channels):
    row = jax.ShapeDtypeStruct((channels,), jnp.bfloat16)
    vmem, anywhere = pl.BlockSpec(memory_space=pltpu.VMEM), pl.BlockSpec(memory_space=pl.ANY)
    pinned = [pltpu.with_memory_space_constraint(r, pltpu.VMEM) for r in (tail, *results)]
    return pl.pallas_call(
        finish_kernel,
        out_shape=tuple(jax.ShapeDtypeStruct(r.shape, r.dtype) for r in results) + (row,) * 3,
        in_specs=[vmem] * 6,
        out_specs=[anywhere] * 5 + [vmem] * 3,
        scratch_shapes=[pltpu.SemaphoreType.DMA((5,))],
        compiler_params=pltpu.CompilerParams(vmem_limit_bytes=4 * 1024 * 1024),
    )(*pinned)


def on_device(latents, cotangent, weight, gain, shift, master, first_moment, second_moment):
    groups, owners = lax.axis_size("grp"), lax.axis_size("dp")
    channels = weight.shape[2]
    split_rows = 2
    depth = owners // (2 * split_rows)
    plane = groups * split_rows
    shard_rows = master.shape[0] // LANES
    x = jnp.transpose(latents[0], (0, 2, 1))
    cot = jnp.transpose(cotangent[0], (0, 2, 1))
    shaped = [a.reshape(shard_rows, LANES) for a in (master, first_moment, second_moment)]
    grad_in, new_weight, tail, *state = run_layer(
        x, cot, weight, gain, shift, *shaped, plane, depth, split_rows
    )
    results = finish(tail, (grad_in, new_weight, *state), channels)
    grad_in, new_weight, new_master, new_first, new_second = results[:5]
    new_bias, new_gain, new_shift = results[5:]
    return (
        jnp.transpose(grad_in, (0, 2, 1))[None],
        new_weight.reshape(weight.shape),
        new_bias,
        new_gain,
        new_shift,
        new_master.reshape(-1),
        new_first.reshape(-1),
        new_second.reshape(-1),
    )


def solution(mesh):
    split = ("grp", "dp")
    whole = P(split, None, None, None)
    in_specs = (whole, whole, P(), P(), P(), P(split), P(split), P(split))
    out_specs = (whole, P(), P(), P(), P(), P(split), P(split), P(split))
    return jax.shard_map(
        on_device, mesh=mesh, in_specs=in_specs, out_specs=out_specs, check_vma=False
    )
```
